128 devices in a mesh: gz: 32 (over z, x_lo, y), gx: 4 (over x_hi, core).
Axes of the slice: x: 4 (x_hi: 2, x_lo: 2; x = x_hi * 2 + x_lo), y: 4, z: 4, core: 2. Of those that a mesh axis runs over, the one named last changes fastest.
Arguments:
- right_side: float32 [2, 3, 2, 128, 128, 128], P(None, None, None, 'gz', 'gx'), may hold values from -10 to 10
- conductance: float32 [128, 128, 128], P('gz', 'gx'), may hold values from 0.05 to 5
- owned_cells: int32 [128, 4, 32], P(('gz', 'gx')), may hold values from 0 to 4095, as said below
- spectra: float32 [512, 4], replicated, may hold values from -8 to 8
- scenario_tile: int32 [512], replicated, may hold values from 0 to 3
Outputs:
- solution_field: float32 [2, 3, 2, 128, 128, 128], P(None, None, None, 'gz', 'gx')
- hazard: float32 [16384, 512], P(('gz', 'gx'))
The draws below stay inside these ranges and needn't reach their ends.
Inputs may be any that keep to these rules, and one draw needn't show every extreme that they name: For each tile j, owned_cells[:, j, :] holds each of the 4096 cell numbers of tile j exactly once.
All inputs are finite; a program needn't handle non-finite values.
Results may differ from the reference program's by a relative error of at most 0.0015.
Values sent between devices are 32-bit elements; how exact they have to be, the bound alone decides.
No kernel may reach another device: no remote copies, remote signals or barrier semaphores. Data moves between devices by JAX's collectives and lax.ppermute only.
A program may use at most 64 MiB of HBM per device.

```python
import math
import jax
import jax.numpy as jnp
from jax import lax

CX = 32
NY = 128
SCEN = 512
ITERS = 3
NZ = 128
NX = 128
TILE_CELLS = 4096
TILE_SLOTS = 32
N_GZ = 32
N_GX = 4


def draw_right_side(key, part):
    key = jax.random.fold_in(key, 3)
    shape = (2, 3, 2, NZ, NX, NY)
    depth = (jnp.arange(NZ, dtype=jnp.float32) / max(NZ - 1, 1))[:, None, None]
    base = jax.random.truncated_normal(key, -5.0, 5.0, shape, jnp.float32)
    return base * (0.5 + 1.5 * depth)


def draw_owned_cells(key, part):
    key = jax.random.fold_in(key, 7)
    lists = []
    for tile in range(N_GX):
        order = jax.random.permutation(jax.random.fold_in(key, tile), TILE_CELLS)
        lists.append(order.reshape(N_GZ * N_GX, TILE_SLOTS))
    return jnp.stack(lists, axis=1).astype(jnp.int32)


def with_ends(entries, own_key, smallest, high):
    index_at = [jax.random.randint(jax.random.fold_in(own_key, axis), (), 0, length) for axis, length in enumerate(entries.shape)]
    widest = entries.shape.index(max(entries.shape))
    next_to = index_at[:widest] + [(index_at[widest] + 1) % entries.shape[widest]] + index_at[widest + 1:]
    return entries.at[tuple(index_at)].set(smallest).at[tuple(next_to)].set(high)


def block_scale(rng, shape, cuts, smallest, high):
    factor_of, own = 1.0, jax.random.fold_in(rng, 6)
    for dim, shards_of in cuts:
        draws = jnp.exp(jax.random.uniform(jax.random.fold_in(own, dim), (shards_of,), jnp.float32, smallest / len(cuts), high / len(cuts)))
        factor_of = factor_of * jnp.repeat(draws, shape[dim] // shards_of).reshape([-1 if axis == dim else 1 for axis in range(len(shape))])
    return factor_of


def scatter_about(stream_key, extent, scale, reach, held_as=jnp.bfloat16):
    return jnp.clip(scale * jax.random.normal(stream_key, extent, jnp.float32), -reach, reach).astype(held_as)


def setup_inputs(seed: int = 0) -> dict:
    arg_keys = jax.random.split(jax.random.key(seed), 6)
    return {
        "right_side": draw_right_side(jax.random.fold_in(arg_keys[5], 71), 0),
        "conductance": jnp.clip(jnp.exp(math.log(5.0) - 4.6051702 * jax.random.uniform(arg_keys[1], (NZ, NX, NY), jnp.float32) ** block_scale(arg_keys[1], (NZ, NX, NY), ((0, 32), (1, 4)), -0.2, 0.2)), 0.05, 5.0),
        "owned_cells": draw_owned_cells(jax.random.fold_in(arg_keys[5], 71), 0),
        "spectra": scatter_about(arg_keys[3], (SCEN, 4), 2.0, 8.0, jnp.float32),
        "scenario_tile": with_ends(jax.random.randint(arg_keys[4], (SCEN,), 0, N_GX), jax.random.fold_in(arg_keys[4], 1), 0, N_GX - 1).astype(jnp.int32),
    }


def shift_next(field, axis):
    size = field.shape[axis]
    rest = lax.slice_in_dim(field, 1, size, axis=axis)
    return jnp.concatenate([rest, jnp.zeros_like(lax.slice_in_dim(field, 0, 1, axis=axis))], axis=axis)


def shift_prev(field, axis):
    size = field.shape[axis]
    rest = lax.slice_in_dim(field, 0, size - 1, axis=axis)
    return jnp.concatenate([jnp.zeros_like(lax.slice_in_dim(field, 0, 1, axis=axis)), rest], axis=axis)


def forward(field, axis):
    return shift_next(field, axis) - field


def backward(field, axis):
    return field - shift_prev(field, axis)


def curl_curl(padded):
    ex_part = padded[:, 0]
    ey_part = padded[:, 1]
    ez_part = padded[:, 2]
    hx_part = forward(ez_part, 4) - forward(ey_part, 2)
    hy_part = forward(ex_part, 2) - forward(ez_part, 3)
    hz_part = forward(ey_part, 3) - forward(ex_part, 4)
    cx_part = backward(hz_part, 4) - backward(hy_part, 2)
    cy_part = backward(hx_part, 2) - backward(hz_part, 3)
    cz_part = backward(hy_part, 3) - backward(hx_part, 4)
    whole = jnp.stack([cx_part, cy_part, cz_part], axis=1)
    return whole[:, :, :, 1:-1, 1:-1, 1:-1]


def apply_operator(field, padded, conductance):
    curled = curl_curl(padded)
    real_part = curled[:, :, 0] - conductance * field[:, :, 1]
    imag_part = curled[:, :, 1] + conductance * field[:, :, 0]
    return jnp.stack([real_part, imag_part], axis=2)


def precondition(field, conductance):
    denom = 16.0 + conductance * conductance
    m_real = 4.0 / denom
    m_imag = -conductance / denom
    real_part = m_real * field[:, :, 0] - m_imag * field[:, :, 1]
    imag_part = m_real * field[:, :, 1] + m_imag * field[:, :, 0]
    return jnp.stack([real_part, imag_part], axis=2)


def inner(left, right):
    real_part = jnp.sum(left[:, :, 0] * right[:, :, 0] + left[:, :, 1] * right[:, :, 1], axis=(1, 2, 3, 4))
    imag_part = jnp.sum(left[:, :, 0] * right[:, :, 1] - left[:, :, 1] * right[:, :, 0], axis=(1, 2, 3, 4))
    return real_part, imag_part


def squares(field):
    return jnp.sum(field * field, axis=(1, 2, 3, 4, 5))


def cdiv(numer, denom, floor):
    size = jnp.maximum(denom[0] * denom[0] + denom[1] * denom[1], floor)
    return ((numer[0] * denom[0] + numer[1] * denom[1]) / size, (numer[1] * denom[0] - numer[0] * denom[1]) / size)


def cmul(left, right):
    return (left[0] * right[0] - left[1] * right[1], left[0] * right[1] + left[1] * right[0])


def cscale(scalar, field):
    s_real = scalar[0][:, None, None, None, None]
    s_imag = scalar[1][:, None, None, None, None]
    real_part = s_real * field[:, :, 0] - s_imag * field[:, :, 1]
    imag_part = s_real * field[:, :, 1] + s_imag * field[:, :, 0]
    return jnp.stack([real_part, imag_part], axis=2)


def impedance(top, below):
    ones = jnp.ones_like(top[0, 0, 0])
    zeros = jnp.zeros_like(top[0, 0, 0])
    ex_pol = []
    ey_pol = []
    hx_pol = []
    hy_pol = []
    for pol in range(2):
        ex_pol.append((top[pol, 0, 0], top[pol, 0, 1]))
        ey_pol.append((top[pol, 1, 0], top[pol, 1, 1]))
        base_x = ones if pol == 0 else zeros
        base_y = ones if pol == 1 else zeros
        hx_pol.append((base_x - 2.0 * (below[pol, 1, 0] - top[pol, 1, 0]), -2.0 * (below[pol, 1, 1] - top[pol, 1, 1])))
        hy_pol.append((base_y + 2.0 * (below[pol, 0, 0] - top[pol, 0, 0]), 2.0 * (below[pol, 0, 1] - top[pol, 0, 1])))

    def csub(left, right):
        return (left[0] - right[0], left[1] - right[1])

    det = csub(cmul(hx_pol[0], hy_pol[1]), cmul(hx_pol[1], hy_pol[0]))
    zxx = cdiv(csub(cmul(ex_pol[0], hy_pol[1]), cmul(ex_pol[1], hy_pol[0])), det, 0.25)
    zxy = cdiv(csub(cmul(ex_pol[1], hx_pol[0]), cmul(ex_pol[0], hx_pol[1])), det, 0.25)
    zyx = cdiv(csub(cmul(ey_pol[0], hy_pol[1]), cmul(ey_pol[1], hy_pol[0])), det, 0.25)
    zyy = cdiv(csub(cmul(ey_pol[1], hx_pol[0]), cmul(ey_pol[0], hx_pol[1])), det, 0.25)
    return jnp.stack([zxx[0], zxx[1], zxy[0], zxy[1], zyx[0], zyx[1], zyy[0], zyy[1]], axis=0)


def hazard_rows(chosen, spectra, scenario_tile, slots, tiles):
    bx_real = spectra[:, 0][None, :]
    bx_imag = spectra[:, 1][None, :]
    by_real = spectra[:, 2][None, :]
    by_imag = spectra[:, 3][None, :]
    zxx_r, zxx_i, zxy_r, zxy_i, zyx_r, zyx_i, zyy_r, zyy_i = [chosen[index][:, None] for index in range(8)]
    gx_real = zxx_r * bx_real - zxx_i * bx_imag + zxy_r * by_real - zxy_i * by_imag
    gx_imag = zxx_r * bx_imag + zxx_i * bx_real + zxy_r * by_imag + zxy_i * by_real
    gy_real = zyx_r * bx_real - zyx_i * bx_imag + zyy_r * by_real - zyy_i * by_imag
    gy_imag = zyx_r * bx_imag + zyx_i * bx_real + zyy_r * by_imag + zyy_i * by_real
    rows = chosen.shape[1]
    tile_row = (jnp.arange(rows, dtype=jnp.int32) // slots) % tiles
    weight = jnp.where(tile_row[:, None] == scenario_tile[None, :], 1.0, 0.25).astype(spectra.dtype)
    return weight * (gx_real * gx_real + gx_imag * gx_imag + gy_real * gy_real + gy_imag * gy_imag)


def reference(right_side, conductance, owned_cells, spectra, scenario_tile):
    pads = ((0, 0), (0, 0), (0, 0), (1, 1), (1, 1), (1, 1))

    def operate(field):
        return apply_operator(field, jnp.pad(field, pads), conductance)

    solution = jnp.zeros_like(right_side)
    residual = right_side
    shadow = right_side
    direction = right_side
    image = right_side
    rho_prev = None
    alpha = None
    omega = None
    floor = None
    for step in range(ITERS):
        rho = inner(shadow, residual)
        if step == 0:
            floor = 1e-6 * rho[0] * rho[0]
            direction = residual
        else:
            beta = cmul(cdiv(rho, rho_prev, floor), cdiv(alpha, omega, 1e-4))
            direction = residual + cscale(beta, direction - cscale(omega, image))
        search = precondition(direction, conductance)
        image = operate(search)
        alpha = cdiv(rho, inner(shadow, image), floor)
        middle = residual - cscale(alpha, image)
        smooth = precondition(middle, conductance)
        bent = operate(smooth)
        bent_middle = inner(bent, middle)
        bent_norm = squares(bent) + 1e-6
        omega = (bent_middle[0] / bent_norm, bent_middle[1] / bent_norm)
        solution = solution + cscale(alpha, search) + cscale(omega, smooth)
        residual = middle - cscale(omega, bent)
        rho_prev = rho
    surface = impedance(solution[:, :, :, 0], solution[:, :, :, 1])
    tiles = surface.reshape(8, N_GX, CX * NY)
    picks = []
    for tile in range(N_GX):
        picks.append(jnp.take(tiles[:, tile], owned_cells[:, tile, :], axis=1))
    chosen = jnp.stack(picks, axis=2).reshape(8, -1)
    hazard = hazard_rows(chosen, spectra, scenario_tile, TILE_SLOTS, N_GX)
    return solution, hazard
```

```python
import jax
import jax.numpy as jnp
from jax import lax
from jax.experimental import pallas as pl
from jax.experimental.pallas import tpu as pltpu
from jax.sharding import PartitionSpec as P

SHIFTS = (1.8, 0.6, 1.8, 0.6, 1.8, 0.6)
SCALE = 1.0
ITERS = 3
REACH = 3
SIDE = 2 * REACH
NF = 12
CX, NZL, NY = 32, 4, 128
WX = 48
EZ = NZL + 2 * REACH
BACK = 40
f32 = jnp.float32
VM = pl.BlockSpec(memory_space=pltpu.VMEM)
LIMIT = 48 * 1024 * 1024


def call(body, outs, scratch=(), n_in=1, flops=0, moved=0):
    return pl.pallas_call(
        body,
        out_shape=[jax.ShapeDtypeStruct(s, d) for s, d in outs],
        in_specs=[VM] * n_in,
        out_specs=[VM] * len(outs),
        scratch_shapes=list(scratch),
        compiler_params=pltpu.CompilerParams(vmem_limit_bytes=LIMIT),
        cost_estimate=pl.CostEstimate(flops=flops, bytes_accessed=moved, transcendentals=0),
    )


def pack_x(r, k, up, down):
    for f in range(NF + 1):
        for z in range(NZL):
            row = (f * NZL + z) * SIDE
            src = k.at[z] if f == NF else r.at[f, z]
            up[row : row + SIDE, :] = src[CX - SIDE : CX, :]
            down[row : row + SIDE, :] = src[0:SIDE, :]


def pack_z(r, k, left, right, up, down):
    width = CX + 2 * SIDE
    for f in range(NF + 1):
        for z in range(NZL):
            near = (f * NZL + z) * SIDE
            src = k.at[z] if f == NF else r.at[f, z]
            for out, first in ((up, NZL - REACH), (down, 0)):
                if first <= z < first + REACH:
                    row = (f * REACH + z - first) * width
                    out[row : row + SIDE, :] = left[near : near + SIDE, :]
                    out[row + SIDE : row + SIDE + CX, :] = src[:, :]
                    out[row + SIDE + CX : row + width, :] = right[near : near + SIDE, :]


def lanes():
    lane = lax.broadcasted_iota(jnp.int32, (WX, NY), 1)
    return lane == 0, lane == NY - 1


def next_y(a, last):
    return jnp.where(last, 0.0, pltpu.roll(a, NY - 1, 1))


def next_x(a):
    return pltpu.roll(a, WX - 1, 0)


def prev_x(a):
    return pltpu.roll(a, 1, 0)


def h_flat(y, base, z, last):
    ex, ey, ez = y[base, z], y[base + 2, z], y[base + 4, z]
    hx = next_y(ez, last) - ez - (y[base + 2, z + 1] - ey)
    hy = y[base, z + 1] - ex - (next_x(ez) - ez)
    return hx, hy


def smooth(b, y, m, base, z):
    mr, mi = m[0, z], m[1, z]
    for c in range(3):
        re, im = b[base + 2 * c, z], b[base + 2 * c + 1, z]
        y[base + 2 * c, z] = mr * re - mi * im
        y[base + 2 * c + 1, z] = mr * im + mi * re


def apply_k(b, y, bn, yn, m, lo, hi, shift, want_y):
    first, last = lanes()
    own = (1.0 - shift) / SCALE
    inv = 1.0 / SCALE

    def pol(p, _):
        base = p * 6

        def layer(z, prev):
            out = []
            for q in range(2):
                e = base + q
                hxp, hyp = prev[q]
                ex, ey, ez = y[e, z], y[e + 2, z], y[e + 4, z]
                hx, hy = h_flat(y, e, z, last)
                hz = next_x(ey) - ey - (next_y(ex, last) - ex)
                cx = hz - jnp.where(first, -ex, pltpu.roll(hz, 1, 1)) - (hy - hyp)
                cy = hx - hxp - (hz - prev_x(hz))
                cz = hy - prev_x(hy) - (hx - jnp.where(first, ez, pltpu.roll(hx, 1, 1)))
                for c, (cur, old) in enumerate(((cx, ex), (cy, ey), (cz, ez))):
                    new = cur - 4.0 * old
                    if inv != 1.0:
                        new = new * inv
                    bn[e + 2 * c, z] = new + own * b[e + 2 * c, z]
                out.append((hx, hy))
            if want_y:
                smooth(bn, yn, m, base, z)
            return tuple(out)

        start = tuple(h_flat(y, base + q, lo - 1, last) for q in range(2))
        lax.fori_loop(lo, hi, layer, start)
        return 0

    lax.fori_loop(0, 2, pol, 0)


def all_smooth(b, y, m):
    def pol(p, _):
        def layer(z, _):
            smooth(b, y, m, p * 6, z)
            return 0

        return lax.fori_loop(0, EZ, layer, 0)

    lax.fori_loop(0, 2, pol, 0)


def first_half(r, k, left, right, below, above, b1, b2, b3w, m, up, down, ba, bb, ya, yb, kx):
    width = CX + 2 * SIDE
    x0 = 8 - SIDE
    for f in range(NF + 1):
        dst = kx if f == NF else ba.at[f]
        src = k if f == NF else r.at[f]
        zero = jnp.zeros((EZ, 8, NY), f32)
        dst[:, 0:8, :] = zero
        dst[:, WX - 8 : WX, :] = zero
        for z in range(NZL):
            near = (f * NZL + z) * SIDE
            dst[REACH + z, x0:8, :] = left[near : near + SIDE, :]
            dst[REACH + z, 8 : 8 + CX, :] = src[z]
            dst[REACH + z, 8 + CX : 8 + CX + SIDE, :] = right[near : near + SIDE, :]
        for z in range(REACH):
            row = (f * REACH + z) * width
            dst[z, x0 : x0 + width, :] = below[row : row + width, :]
            dst[REACH + NZL + z, x0 : x0 + width, :] = above[row : row + width, :]

    def weights(z, _):
        kz = kx[z]
        inv = jnp.where(kz > 0.0, 1.0, 0.0) / (16.0 + kz * kz)
        m[0, z] = 4.0 * inv
        m[1, z] = -kz * inv
        return 0

    lax.fori_loop(0, EZ, weights, 0)
    all_smooth(ba, ya, m)

    def keep(src, out):
        def field(f, _):
            out[f] = src[f, REACH : REACH + NZL, 8 : 8 + CX, :]
            return 0

        lax.fori_loop(0, NF, field, 0)

    apply_k(ba, ya, bb, yb, m, 1, EZ - 1, SHIFTS[0], True)
    keep(bb, b1)
    apply_k(bb, yb, ba, ya, m, 2, EZ - 2, SHIFTS[1], True)
    keep(ba, b2)
    apply_k(ba, ya, bb, yb, m, 3, EZ - 3, SHIFTS[2], False)
    cut = (WX - BACK) // 2

    def field(f, _):
        b3w[f] = bb[f, REACH : REACH + NZL]
        up[f] = bb[f, NZL : REACH + NZL, cut : cut + BACK, :]
        down[f] = bb[f, REACH : 2 * REACH, cut : cut + BACK, :]
        return 0

    lax.fori_loop(0, NF, field, 0)


PAIRS = [(i, j) for i in range(7) for j in range(i, 7)]
LOW = [pair for pair in PAIRS if pair[1] <= REACH]
HIGH = [pair for pair in PAIRS if pair[1] > REACH]
SLOT = {}
for _pair in LOW + HIGH:
    SLOT[_pair] = sum(1 if a == b else 2 for a, b in SLOT)


def gram(read, pairs, out):
    used = sorted({i for pair in pairs for i in pair})
    count = sum(1 if i == j else 2 for i, j in pairs)

    def pol(p, _):
        def block(step, acc):
            c, z = step // NZL, step % NZL
            acc = list(acc)
            for xb in range(CX // 8):
                vec = {}
                for i in used:
                    vec[i] = (read(i, p * 6 + 2 * c, z, xb), read(i, p * 6 + 2 * c + 1, z, xb))
                at = 0
                for i, j in pairs:
                    (ar, ai), (br, bi) = vec[i], vec[j]
                    acc[at] = acc[at] + (ar * br + ai * bi)
                    at += 1
                    if i != j:
                        acc[at] = acc[at] + (ar * bi - ai * br)
                        at += 1
            return tuple(acc)

        acc = lax.fori_loop(0, 3 * NZL, block, (jnp.zeros((8, NY), f32),) * count)
        at = 0
        for i, j in pairs:
            for part in range(1 if i == j else 2):
                out[pl.ds(p * 64 + SLOT[i, j] + part, 1), :] = jnp.sum(acc[at], axis=0, keepdims=True)
                at += 1
        return 0

    lax.fori_loop(0, 2, pol, 0)


def reader(refs, wide):
    def read(i, f, z, xb):
        off = 8 if i in wide else 0
        return refs[i][f, z, pl.ds(off + 8 * xb, 8), :]

    return read


def low_gram(b0, b1, b2, b3w, part):
    part[...] = jnp.zeros((NY, NY), f32)
    gram(reader([b0, b1, b2, b3w], (3,)), LOW, part)


def second_half(b0, b1, b2, b3w, m, below, above, part, owned, b4, b5, send, ba, bb, ya, yb, bc, total):
    cut = (WX - BACK) // 2

    def field(f, _):
        zero = jnp.zeros((REACH, 8, NY), f32)
        for first, halo in ((0, below), (REACH + NZL, above)):
            ba[f, first : first + REACH, 0:8, :] = zero
            ba[f, first : first + REACH, WX - 8 : WX, :] = zero
            ba[f, first : first + REACH, cut : cut + BACK, :] = halo[f]
        ba[f, REACH : REACH + NZL] = b3w[f]
        return 0

    lax.fori_loop(0, NF, field, 0)
    all_smooth(ba, ya, m)

    def keep(src, out):
        def field(f, _):
            out[f] = src[f, REACH : REACH + NZL, 8 : 8 + CX, :]
            return 0

        lax.fori_loop(0, NF, field, 0)

    apply_k(ba, ya, bb, yb, m, 1, EZ - 1, SHIFTS[3], True)
    keep(bb, b4)
    apply_k(bb, yb, ba, ya, m, 2, EZ - 2, SHIFTS[4], True)
    keep(ba, b5)
    apply_k(ba, ya, bc, yb, m, 3, EZ - 3, SHIFTS[5], False)
    total[...] = part[...]
    low = reader([b0, b1, b2, b3w, b4, b5], (3,))

    def read(i, f, z, xb):
        if i == 6:
            return bc[f, REACH + z, pl.ds(8 + 8 * xb, 8), :]
        return low(i, f, z, xb)

    gram(read, HIGH, total)
    sums = jnp.sum(jnp.transpose(total[...]), axis=0, keepdims=True)
    cells = jnp.concatenate([owned[j : j + 1, :] for j in range(4)], axis=1).astype(f32)
    send[...] = jnp.broadcast_to(jnp.concatenate([sums, cells], axis=1), (128, 2 * NY))


def cadd(a, b):
    return (a[0] + b[0], a[1] + b[1])


def csub(a, b):
    return (a[0] - b[0], a[1] - b[1])


def cmul(a, b):
    return (a[0] * b[0] - a[1] * b[1], a[0] * b[1] + a[1] * b[0])


def cconj_mul(a, b):
    return (a[0] * b[0] + a[1] * b[1], a[0] * b[1] - a[1] * b[0])


def cdiv(numer, denom, floor):
    size = jnp.maximum(denom[0] * denom[0] + denom[1] * denom[1], floor)
    return (
        (numer[0] * denom[0] + numer[1] * denom[1]) / size,
        (numer[1] * denom[0] - numer[0] * denom[1]) / size,
    )


def tree(terms):
    terms = list(terms)
    while len(terms) > 1:
        terms = [cadd(*terms[i : i + 2]) if i + 1 < len(terms) else terms[i] for i in range(0, len(terms), 2)]
    return terms[0]


def combine(a, scale, b):
    out = []
    for i in range(max(len(a), len(b))):
        if i >= len(b):
            out.append(a[i])
        elif i >= len(a):
            out.append(cmul(scale, b[i]))
        else:
            out.append(cadd(a[i], cmul(scale, b[i])))
    return out


def times_k(a):
    zero = (jnp.zeros_like(a[0][0]),) * 2
    out = [(SHIFTS[i] * v[0], SHIFTS[i] * v[1]) for i, v in enumerate(a)] + [zero]
    return [
        cadd(out[i], (SCALE * a[i - 1][0], SCALE * a[i - 1][1])) if i > 0 else out[i]
        for i in range(len(out))
    ]


def coefficients(entry):
    def g(i, j):
        if i > j:
            re, im = g(j, i)
            return (re, -im)
        if i == j:
            return (entry(SLOT[i, j]), 0.0)
        return (entry(SLOT[i, j]), entry(SLOT[i, j] + 1))

    def times_g(b, rows):
        return [tree([cmul(g(i, j), b[j]) for j in range(len(b))]) for i in range(rows)]

    def dot(a, gb):
        return tree([cconj_mul(a[i], gb[i]) for i in range(len(a))])

    def shadow(b):
        return tree([cmul(g(0, j), b[j]) for j in range(len(b))])

    one = jnp.ones_like(entry(0))
    residual = [(one, jnp.zeros_like(one))]
    direction = residual
    solution = []
    for step in range(ITERS):
        rho = shadow(residual)
        if step == 0:
            floor = 1e-06 * rho[0] * rho[0]
        else:
            beta = cmul(cdiv(rho, rho_prev, floor), cdiv(alpha, omega, 0.0001))
            minus = (-omega[0], -omega[1])
            direction = combine(residual, beta, combine(direction, minus, image))
        image = times_k(direction)
        alpha = cdiv(rho, shadow(image), floor)
        middle = combine(residual, (-alpha[0], -alpha[1]), image)
        bent = times_k(middle)
        seen = times_g(bent, len(bent))
        norm = dot(bent, seen)[0] + 1e-06
        against = dot(middle, seen)
        omega = (against[0] / norm, -against[1] / norm)
        solution = combine(combine(solution, alpha, direction), omega, middle)
        residual = combine(middle, (-omega[0], -omega[1]), bent)
        rho_prev = rho
    return solution


def impedance(x, z0, rows):
    def e(p, c, z):
        f = p * 6 + 2 * c
        return (x[f, z, rows, :], x[f + 1, z, rows, :])

    ex, ey, hx, hy = [], [], [], []
    for p in range(2):
        ex0, ey0 = e(p, 0, z0), e(p, 1, z0)
        ex1, ey1 = e(p, 0, z0 + 1), e(p, 1, z0 + 1)
        ex.append(ex0)
        ey.append(ey0)
        one_x, one_y = (1.0, 0.0) if p == 0 else (0.0, 1.0)
        hx.append((one_x - 2.0 * (ey1[0] - ey0[0]), -2.0 * (ey1[1] - ey0[1])))
        hy.append((one_y + 2.0 * (ex1[0] - ex0[0]), 2.0 * (ex1[1] - ex0[1])))
    det = csub(cmul(hx[0], hy[1]), cmul(hx[1], hy[0]))
    zxx = cdiv(csub(cmul(ex[0], hy[1]), cmul(ex[1], hy[0])), det, 0.25)
    zxy = cdiv(csub(cmul(ex[1], hx[0]), cmul(ex[0], hx[1])), det, 0.25)
    zyx = cdiv(csub(cmul(ey[0], hy[1]), cmul(ey[1], hy[0])), det, 0.25)
    zyy = cdiv(csub(cmul(ey[1], hx[0]), cmul(ey[0], hx[1])), det, 0.25)
    return [*zxx, *zxy, *zyx, *zyy]


def finish(tile, got, b0, b1, b2, b3w, b4, b5, m, x, send, surface, picked):
    sub = lax.broadcasted_iota(jnp.int32, (8, NY), 0)
    row = jnp.broadcast_to(jnp.sum(got[:, 0:NY], axis=0, keepdims=True), (8, NY))
    table = jnp.where(sub == 0, row, pltpu.roll(row, 64, 1))
    cache = {}

    def entry(slot):
        if slot not in cache:
            cache[slot] = jnp.broadcast_to(table[:, slot : slot + 1], (8, NY))
        return cache[slot]

    coefs = coefficients(entry)
    refs = [b0, b1, b2, b3w, b4, b5]
    read = reader(refs, (3,))
    for p in range(2):
        scal = [tuple(jnp.broadcast_to(part[p : p + 1, :], (8, NY)) for part in c) for c in coefs]

        def block(step, _):
            c, z = step // NZL, step % NZL
            f = p * 6 + 2 * c
            for xb in range(CX // 8):
                terms = [cmul(scal[i], (read(i, f, z, xb), read(i, f + 1, z, xb))) for i in range(2 * ITERS)]
                total = tree(terms)
                cols = pl.ds(8 + 8 * xb, 8)
                y = cmul((m[0, REACH + z, cols, :], m[1, REACH + z, cols, :]), total)
                rows = pl.ds(8 * xb, 8)
                x[f, z, rows, :] = y[0]
                x[f + 1, z, rows, :] = y[1]
            return 0

        lax.fori_loop(0, 3 * NZL, block, 0)

    for xb in range(CX // 8):
        rows = pl.ds(8 * xb, 8)
        for v, value in enumerate(impedance(x, 0, rows)):
            surface[v * CX + 8 * xb : v * CX + 8 * xb + 8, :] = value
    mine = pltpu.roll(got[:, NY : 2 * NY], lax.rem(NY - 32 * tile[0], NY), 1).astype(jnp.int32)
    group = lax.broadcasted_iota(jnp.int32, (32, NY), 1) // 32
    cells = mine[0:32, :]
    for e in range(1, 4):
        cells = jnp.where(group == e, pltpu.roll(mine[32 * e : 32 * e + 32, :], 32 * e, 1), cells)
    col = cells % NY
    line = cells // NY
    cols = [col[8 * i : 8 * i + 8, :] for i in range(4)]
    lines = [line[8 * i : 8 * i + 8, :] for i in range(4)]

    def value(v, _):
        acc = [jnp.zeros((8, NY), f32)] * 4
        for r in range(CX):
            src = jnp.broadcast_to(surface[pl.ds(v * CX + r, 1), :], (8, NY))
            for i in range(4):
                hit = jnp.take_along_axis(src, cols[i], axis=1, mode="promise_in_bounds")
                acc[i] = jnp.where(lines[i] == r, hit, acc[i])
        for i in range(4):
            picked[pl.ds(pl.multiple_of(v * 32, 32) + 8 * i, 8), :] = acc[i]
        return 0

    lax.fori_loop(0, 8, value, 0)
    for e in range(4):
        for h in range(2):
            out = None
            for w in range(4):
                v = 4 * h + w
                part = picked[v * 32 : v * 32 + 32, :]
                if w != e:
                    part = pltpu.roll(part, (32 * (w - e)) % NY, 1)
                out = part if out is None else jnp.where(group == w, part, out)
            send[32 * e : 32 * e + 32, NY * h : NY * h + NY] = out


def hazard_rows(got, spectra, scenario, out):
    scen = scenario.shape[1]
    turned = []
    for h in range(2):
        block = got[0:8, NY * h : NY * h + NY]
        turned.append(jnp.transpose(jnp.concatenate([block, jnp.zeros((NY - 8, NY), f32)], axis=0)))
    b = [spectra[i : i + 1, :] for i in range(4)]
    bx, by = (b[0], b[1]), (b[2], b[3])
    for j in range(4):
        weight = jnp.where(scenario[...] == j, 1.0, 0.25)
        for qb in range(4):
            z = []
            for v in range(8):
                first = (v % 4) * 32 + 8 * qb
                z.append(jnp.broadcast_to(turned[v // 4][first : first + 8, j : j + 1], (8, scen)))
            gx = cadd(cmul((z[0], z[1]), bx), cmul((z[2], z[3]), by))
            gy = cadd(cmul((z[4], z[5]), bx), cmul((z[6], z[7]), by))
            power = gx[0] * gx[0] + gx[1] * gx[1] + gy[0] * gy[0] + gy[1] * gy[1]
            row = 32 * j + 8 * qb
            out[row : row + 8, :] = weight * power


def neighbours(count):
    up = [(i, i + 1) for i in range(count - 1)]
    return up, [(j, i) for i, j in up]


def per_device(right_side, conductance, owned_cells, spectra, scenario_tile):
    up_z, down_z = neighbours(lax.axis_size("gz"))
    up_x, down_x = neighbours(lax.axis_size("gx"))
    block = (NF, NZL, CX, NY)
    slab = (NF, EZ, WX, NY)
    r = right_side.reshape(block)
    k = conductance
    side = ((NF + 1) * NZL * SIDE, NY)
    to_up, to_down = call(pack_x, [(side, f32)] * 2, n_in=2, moved=1 << 21)(r, k)
    left = lax.ppermute(to_up, "gx", up_x)
    right = lax.ppermute(to_down, "gx", down_x)
    deep = ((NF + 1) * REACH * (CX + 2 * SIDE), NY)
    to_up, to_down = call(pack_z, [(deep, f32)] * 2, n_in=4, moved=1 << 22)(r, k, left, right)
    below = lax.ppermute(to_up, "gz", up_z)
    above = lax.ppermute(to_down, "gz", down_z)
    wide = (NF, NZL, WX, NY)
    back = (NF, REACH, BACK, NY)
    space = pltpu.VMEM(slab, f32)
    b1, b2, b3w, m, to_up, to_down = call(
        first_half,
        [(block, f32), (block, f32), (wide, f32), ((2, EZ, WX, NY), f32), (back, f32), (back, f32)],
        [space] * 4 + [pltpu.VMEM((EZ, WX, NY), f32)],
        n_in=6,
        flops=1 << 25,
        moved=1 << 23,
    )(r, k, left, right, below, above)
    below = lax.ppermute(to_up, "gz", up_z)
    above = lax.ppermute(to_down, "gz", down_z)
    (part,) = call(low_gram, [((NY, NY), f32)], n_in=4, flops=1 << 24, moved=1 << 22)(r, b1, b2, b3w)
    b4, b5, send = call(
        second_half,
        [(block, f32), (block, f32), ((128, 2 * NY), f32)],
        [space] * 5 + [pltpu.VMEM((NY, NY), f32)],
        n_in=9,
        flops=1 << 25,
        moved=1 << 23,
    )(r, b1, b2, b3w, m, below, above, part, owned_cells[0])
    got = lax.all_to_all(send, ("gz", "gx"), 0, 0, tiled=True)
    tile = lax.axis_index("gx").astype(jnp.int32).reshape(1)
    x, send = pl.pallas_call(
        finish,
        out_shape=[jax.ShapeDtypeStruct(block, f32), jax.ShapeDtypeStruct((128, 2 * NY), f32)],
        in_specs=[pl.BlockSpec(memory_space=pltpu.SMEM)] + [VM] * 8,
        out_specs=[VM] * 2,
        scratch_shapes=[pltpu.VMEM((8 * CX, NY), f32)] * 2,
        compiler_params=pltpu.CompilerParams(vmem_limit_bytes=LIMIT),
    )(tile, got, r, b1, b2, b3w, b4, b5, m)
    got = lax.all_to_all(send, ("gz", "gx"), 0, 0, tiled=True)
    scen = spectra.shape[0]
    (hazard,) = call(hazard_rows, [((128, scen), f32)], n_in=3)(got, spectra.T, scenario_tile.reshape(1, scen))
    return x.reshape(right_side.shape), hazard


def solution(mesh):
    return jax.shard_map(
        per_device,
        mesh=mesh,
        in_specs=(
            P(None, None, None, "gz", "gx", None),
            P("gz", "gx", None),
            P(("gz", "gx"), None, None),
            P(),
            P(),
        ),
        out_specs=(P(None, None, None, "gz", "gx", None), P(("gz", "gx"), None)),
        check_vma=False,
    )
```

```python
import jax
import jax.numpy as jnp
from jax import lax
from jax.experimental import pallas as pl
from jax.experimental.pallas import tpu as pltpu
from jax.sharding import PartitionSpec as P

SHIFTS = (1.8, 0.6, 1.8, 0.6, 1.8, 0.6)
SCALE = 1.0
ITERS = 3
REACH = 3
SIDE = 2 * REACH
NF = 6
CX, NZL, NY = 32, 4, 128
WX = 48
EZ = NZL + 2 * REACH
BACK = CX + 2 * REACH
f32 = jnp.float32
VM = pl.BlockSpec(memory_space=pltpu.VMEM)
LIMIT = 14 * 1024 * 1024


HBM = pl.BlockSpec(memory_space=pltpu.HBM)


def call(body, ins, outs, scratch=(), flops=0, moved=0):
    return pl.pallas_call(
        body,
        out_shape=[jax.ShapeDtypeStruct(shape, f32) for shape, _ in outs],
        in_specs=ins,
        out_specs=[spec for _, spec in outs],
        scratch_shapes=list(scratch),
        compiler_params=pltpu.CompilerParams(vmem_limit_bytes=LIMIT),
        cost_estimate=pl.CostEstimate(flops=flops, bytes_accessed=moved, transcendentals=0),
    )


def odd(axis):
    return lax.rem(lax.axis_index(axis), 2) == 1


def either(flag, body, first, second):
    @pl.when(jnp.logical_not(flag))
    def _():
        body(first, second)

    @pl.when(flag)
    def _():
        body(second, first)


def start_all(pairs, sem, first=0):
    copies = [pltpu.make_async_copy(src, dst, sem.at[first + i]) for i, (src, dst) in enumerate(pairs)]
    for copy in copies:
        copy.start()
    return copies


def wait_all(copies):
    for copy in copies:
        copy.wait()


def pack_x(r, k, to_a, to_b, rim, rim_k, sem):
    pairs = []
    for i in range(2):
        src = pl.ds(i * (CX - 8), 8)
        pairs.append((r.at[:, :, src, :], rim.at[:, :, pl.ds(8 * i, 8), :]))
        pairs.append((k.at[:, src, :], rim_k.at[:, pl.ds(8 * i, 8), :]))
    wait_all(start_all(pairs, sem))

    def fill(up, down):
        for f in range(2 * NF + 1):
            for z in range(NZL):
                row = (f * NZL + z) * SIDE
                src = rim_k.at[z] if f == 2 * NF else rim.at[f, z]
                up[row : row + SIDE, :] = src[16 - SIDE : 16, :]
                down[row : row + SIDE, :] = src[0:SIDE, :]

    either(odd("gx"), fill, to_a, to_b)


def sides(from_a, from_b, near):
    a, b = from_a[near : near + SIDE, :], from_b[near : near + SIDE, :]
    flag = odd("gx")
    return jnp.where(flag, a, b), jnp.where(flag, b, a)


def pack_z(r, k, xa, xb, a_0, b_0, a_1, b_1):
    width = CX + 2 * SIDE

    def fill(first, second):
        outs = [((first[p], NZL - REACH), (second[p], 0)) for p in range(2)]
        for p in range(2):
            fields = [p * NF + i for i in range(NF)] + ([2 * NF] if p == 0 else [])
            for at, f in enumerate(fields):
                for z in range(NZL):
                    left, right = sides(xa, xb, (f * NZL + z) * SIDE)
                    src = k.at[z] if f == 2 * NF else r.at[f, z]
                    for out, low in outs[p]:
                        if low <= z < low + REACH:
                            row = (at * REACH + z - low) * width
                            out[row : row + SIDE, :] = left
                            out[row + SIDE : row + SIDE + CX, :] = src[:, :]
                            out[row + SIDE + CX : row + width, :] = right

    either(odd("gz"), fill, (a_0, a_1), (b_0, b_1))


def lanes():
    lane = lax.broadcasted_iota(jnp.int32, (WX, NY), 1)
    return lane == 0, lane == NY - 1


def next_y(a, last):
    return jnp.where(last, 0.0, pltpu.roll(a, NY - 1, 1))


def next_x(a):
    return pltpu.roll(a, WX - 1, 0)


def prev_x(a):
    return pltpu.roll(a, 1, 0)


def h_flat(y, base, z, last):
    ex, ey, ez = y[base, z], y[base + 2, z], y[base + 4, z]
    hx = next_y(ez, last) - ez - (y[base + 2, z + 1] - ey)
    hy = y[base, z + 1] - ex - (next_x(ez) - ez)
    return hx, hy


def smooth(b, y, m, base, z):
    mr, mi = m[0, z], m[1, z]
    for c in range(3):
        re, im = b[base + 2 * c, z], b[base + 2 * c + 1, z]
        y[base + 2 * c, z] = mr * re - mi * im
        y[base + 2 * c + 1, z] = mr * im + mi * re


def apply_k(b, y, bn, yn, m, lo, hi, shift, want_y):
    first, last = lanes()
    own = (1.0 - shift) / SCALE
    inv = 1.0 / SCALE

    def layer(z, prev):
        out = []
        for e in range(2):
            hxp, hyp = prev[e]
            ex, ey, ez = y[e, z], y[e + 2, z], y[e + 4, z]
            hx, hy = h_flat(y, e, z, last)
            hz = next_x(ey) - ey - (next_y(ex, last) - ex)
            cx = hz - jnp.where(first, -ex, pltpu.roll(hz, 1, 1)) - (hy - hyp)
            cy = hx - hxp - (hz - prev_x(hz))
            cz = hy - prev_x(hy) - (hx - jnp.where(first, ez, pltpu.roll(hx, 1, 1)))
            for c, (cur, old) in enumerate(((cx, ex), (cy, ey), (cz, ez))):
                new = cur - 4.0 * old
                if inv != 1.0:
                    new = new * inv
                bn[e + 2 * c, z] = new + own * b[e + 2 * c, z]
            out.append((hx, hy))
        if want_y:
            smooth(bn, yn, m, 0, z)
        return tuple(out)

    lax.fori_loop(lo, hi, layer, tuple(h_flat(y, e, lo - 1, last) for e in range(2)))


def all_smooth(b, y, m):
    def layer(z, _):
        smooth(b, y, m, 0, z)
        return 0

    lax.fori_loop(0, EZ, layer, 0)


def weights(k, xa, xb, za, zb, m, kx):
    extend([kx], [k], xa, xb, za, zb, 2 * NF, NF)

    def layer(z, _):
        kz = kx[z]
        inv = jnp.where(kz > 0.0, 1.0, 0.0) / (16.0 + kz * kz)
        m[0, z] = 4.0 * inv
        m[1, z] = -kz * inv
        return 0

    lax.fori_loop(0, EZ, layer, 0)


def extend(outs, srcs, xa, xb, za, zb, near, far):
    width = CX + 2 * SIDE
    x0 = 8 - SIDE
    zero = jnp.zeros((EZ, 8, NY), f32)
    for i, (dst, src) in enumerate(zip(outs, srcs)):
        dst[:, 0:8, :] = zero
        dst[:, WX - 8 : WX, :] = zero
        for z in range(NZL):
            left, right = sides(xa, xb, ((near + i) * NZL + z) * SIDE)
            dst[REACH + z, x0:8, :] = left
            dst[REACH + z, 8 : 8 + CX, :] = src[z]
            dst[REACH + z, 8 + CX : 8 + CX + SIDE, :] = right

    def fill(above, below):
        for i, dst in enumerate(outs):
            for z in range(REACH):
                row = ((far + i) * REACH + z) * width
                dst[z, x0 : x0 + width, :] = below[row : row + width, :]
                dst[REACH + NZL + z, x0 : x0 + width, :] = above[row : row + width, :]

    either(odd("gz"), fill, za, zb)


def keep(src, out):
    def field(f, _):
        out[f] = src[f, REACH : REACH + NZL, 8 : 8 + CX, :]
        return 0

    lax.fori_loop(0, NF, field, 0)


def first_steps(p, r, xa, xb, za, zb, b1, b2, b3w, to_a, to_b, b1_far, b2_far, m, ba, bb, ya, yb, sem):
    fields = range(NF)
    extend([ba.at[f] for f in fields], [r.at[p * NF + f] for f in fields], xa, xb, za, zb, p * NF, 0)
    all_smooth(ba, ya, m)
    apply_k(ba, ya, bb, yb, m, 1, EZ - 1, SHIFTS[0], True)
    keep(bb, b1)
    copies = start_all([(b1, b1_far)], sem)
    apply_k(bb, yb, ba, ya, m, 2, EZ - 2, SHIFTS[1], True)
    keep(ba, b2)
    copies += start_all([(b2, b2_far)], sem, 1)
    apply_k(ba, ya, bb, yb, m, 3, EZ - 3, SHIFTS[2], False)
    cut = (WX - BACK) // 2
    for f in fields:
        b3w[f] = bb[f, REACH : REACH + NZL]

    def fill(up, down):
        for f in fields:
            for z in range(REACH):
                row = (f * REACH + z) * BACK
                up[row : row + BACK, :] = bb[f, NZL + z, cut : cut + BACK, :]
                down[row : row + BACK, :] = bb[f, REACH + z, cut : cut + BACK, :]

    either(odd("gz"), fill, to_a, to_b)
    wait_all(copies)


def first_half_0(r, k, xa, xb, za, zb, b1, b2, b3w, to_a, to_b, b1_far, b2_far, m, ba, bb, ya, yb, sem, kx):
    weights(k, xa, xb, za, zb, m, kx)
    first_steps(0, r, xa, xb, za, zb, b1, b2, b3w, to_a, to_b, b1_far, b2_far, m, ba, bb, ya, yb, sem)


def first_half_1(r, m, xa, xb, za, zb, b1, b2, b3w, to_a, to_b, b1_far, b2_far, ba, bb, ya, yb, sem):
    first_steps(1, r, xa, xb, za, zb, b1, b2, b3w, to_a, to_b, b1_far, b2_far, m, ba, bb, ya, yb, sem)


PAIRS = [(i, j) for i in range(7) for j in range(i, 7)]
LOW = [pair for pair in PAIRS if pair[1] <= REACH]
HIGH = [pair for pair in PAIRS if pair[1] > REACH]
SLOT = {}
for _pair in LOW + HIGH:
    SLOT[_pair] = sum(1 if a == b else 2 for a, b in SLOT)


def gram(read, pairs, out):
    used = sorted({i for pair in pairs for i in pair})
    count = sum(1 if i == j else 2 for i, j in pairs)

    def block(step, acc):
        c, z = step // NZL, step % NZL
        acc = list(acc)
        for xb in range(CX // 8):
            vec = {i: (read(i, 2 * c, z, xb), read(i, 2 * c + 1, z, xb)) for i in used}
            at = 0
            for i, j in pairs:
                (ar, ai), (br, bi) = vec[i], vec[j]
                acc[at] = acc[at] + (ar * br + ai * bi)
                at += 1
                if i != j:
                    acc[at] = acc[at] + (ar * bi - ai * br)
                    at += 1
        return tuple(acc)

    acc = lax.fori_loop(0, 3 * NZL, block, (jnp.zeros((8, NY), f32),) * count)
    at = 0
    for i, j in pairs:
        for part in range(1 if i == j else 2):
            row = SLOT[i, j] + part
            out[row : row + 1, :] = jnp.sum(acc[at], axis=0, keepdims=True)
            at += 1


def low_gram(b0, b1_0, b2_0, b3w_0, b1_1, b2_1, b3w_1, part_0, part_1):
    for p, (b1, b2, b3w, part) in enumerate(((b1_0, b2_0, b3w_0, part_0), (b1_1, b2_1, b3w_1, part_1))):
        part[...] = jnp.zeros((64, NY), f32)
        gram(reader(p, b0, b1, b2, b3w), LOW, part)


def reader(p, b0, b1, b2, b3w, *slabs):
    def read(i, f, z, xb):
        if i == 0:
            return b0[p * NF + f, z, pl.ds(8 * xb, 8), :]
        if i < 3:
            return (b1, b2)[i - 1][f, z, pl.ds(8 * xb, 8), :]
        if i == 3:
            return b3w[f, z, pl.ds(8 + 8 * xb, 8), :]
        return slabs[i - 4][f, REACH + z, pl.ds(8 + 8 * xb, 8), :]

    return read


def second_steps(p, b0, b1, b2, b3w, m, za, zb, part, b3_far, b4_far, b5_far, total, ba, bb, bc, bd, ya, yb, sem):
    cut = (WX - BACK) // 2
    own = pl.ds(REACH, NZL)
    mid = pl.ds(8, CX)
    copies = start_all([(b3w.at[:, :, mid, :], b3_far)], sem)
    zero = jnp.zeros((REACH, 8, NY), f32)
    for f in range(NF):
        for first in (0, REACH + NZL):
            ba[f, first : first + REACH, 0:8, :] = zero
            ba[f, first : first + REACH, WX - 8 : WX, :] = zero
        ba[f, REACH : REACH + NZL] = b3w[f]

    def fill(above, below):
        for f in range(NF):
            for z in range(REACH):
                row = (f * REACH + z) * BACK
                ba[f, z, cut : cut + BACK, :] = below[row : row + BACK, :]
                ba[f, REACH + NZL + z, cut : cut + BACK, :] = above[row : row + BACK, :]

    either(odd("gz"), fill, za, zb)
    all_smooth(ba, ya, m)
    apply_k(ba, ya, bb, yb, m, 1, EZ - 1, SHIFTS[3], True)
    copies += start_all([(bb.at[:, own, mid, :], b4_far)], sem, 1)
    apply_k(bb, yb, bc, ya, m, 2, EZ - 2, SHIFTS[4], True)
    copies += start_all([(bc.at[:, own, mid, :], b5_far)], sem, 2)
    apply_k(bc, ya, bd, yb, m, 3, EZ - 3, SHIFTS[5], False)
    total[...] = part[...]
    gram(reader(p, b0, b1, b2, b3w, bb, bc, bd), HIGH, total)
    wait_all(copies)


def second_half_0(b0, b1, b2, b3w, m, za, zb, part, b3_far, b4_far, b5_far, total, *space):
    second_steps(0, b0, b1, b2, b3w, m, za, zb, part, b3_far, b4_far, b5_far, total, *space)


def second_half_1(b0, b1, b2, b3w, m, za, zb, part, other, owned, b3_far, b4_far, b5_far, send, total, *space):
    second_steps(1, b0, b1, b2, b3w, m, za, zb, part, b3_far, b4_far, b5_far, total, *space)
    both = jnp.concatenate([other[...], total[...]], axis=0)
    sums = jnp.sum(jnp.transpose(both), axis=0, keepdims=True)
    cells = jnp.concatenate([owned[j : j + 1, :] for j in range(4)], axis=1).astype(f32)
    send[...] = jnp.broadcast_to(jnp.concatenate([sums, cells], axis=1), (128, 2 * NY))


def cadd(a, b):
    return (a[0] + b[0], a[1] + b[1])


def csub(a, b):
    return (a[0] - b[0], a[1] - b[1])


def cmul(a, b):
    return (a[0] * b[0] - a[1] * b[1], a[0] * b[1] + a[1] * b[0])


def cconj_mul(a, b):
    return (a[0] * b[0] + a[1] * b[1], a[0] * b[1] - a[1] * b[0])


def cdiv(numer, denom, floor):
    size = jnp.maximum(denom[0] * denom[0] + denom[1] * denom[1], floor)
    return (
        (numer[0] * denom[0] + numer[1] * denom[1]) / size,
        (numer[1] * denom[0] - numer[0] * denom[1]) / size,
    )


def tree(terms):
    terms = list(terms)
    while len(terms) > 1:
        terms = [cadd(*terms[i : i + 2]) if i + 1 < len(terms) else terms[i] for i in range(0, len(terms), 2)]
    return terms[0]


def combine(a, scale, b):
    out = []
    for i in range(max(len(a), len(b))):
        if i >= len(b):
            out.append(a[i])
        elif i >= len(a):
            out.append(cmul(scale, b[i]))
        else:
            out.append(cadd(a[i], cmul(scale, b[i])))
    return out


def times_k(a):
    zero = (jnp.zeros_like(a[0][0]),) * 2
    out = [(SHIFTS[i] * v[0], SHIFTS[i] * v[1]) for i, v in enumerate(a)] + [zero]
    return [
        cadd(out[i], (SCALE * a[i - 1][0], SCALE * a[i - 1][1])) if i > 0 else out[i]
        for i in range(len(out))
    ]


def coefficients(entry):
    def g(i, j):
        if i > j:
            re, im = g(j, i)
            return (re, -im)
        if i == j:
            return (entry(SLOT[i, j]), 0.0)
        return (entry(SLOT[i, j]), entry(SLOT[i, j] + 1))

    def times_g(b, rows):
        return [tree([cmul(g(i, j), b[j]) for j in range(len(b))]) for i in range(rows)]

    def dot(a, gb):
        return tree([cconj_mul(a[i], gb[i]) for i in range(len(a))])

    def shadow(b):
        return tree([cmul(g(0, j), b[j]) for j in range(len(b))])

    one = jnp.ones_like(entry(0))
    residual = [(one, jnp.zeros_like(one))]
    direction = residual
    solution = []
    for step in range(ITERS):
        rho = shadow(residual)
        if step == 0:
            floor = 1e-06 * rho[0] * rho[0]
        else:
            beta = cmul(cdiv(rho, rho_prev, floor), cdiv(alpha, omega, 0.0001))
            minus = (-omega[0], -omega[1])
            direction = combine(residual, beta, combine(direction, minus, image))
        image = times_k(direction)
        alpha = cdiv(rho, shadow(image), floor)
        middle = combine(residual, (-alpha[0], -alpha[1]), image)
        bent = times_k(middle)
        seen = times_g(bent, len(bent))
        norm = dot(bent, seen)[0] + 1e-06
        against = dot(middle, seen)
        omega = (against[0] / norm, -against[1] / norm)
        solution = combine(combine(solution, alpha, direction), omega, middle)
        residual = combine(middle, (-omega[0], -omega[1]), bent)
        rho_prev = rho
    return solution


def impedance(x, z0, rows):
    def e(p, c, z):
        f = p * 6 + 2 * c
        return (x[f, z, rows, :], x[f + 1, z, rows, :])

    ex, ey, hx, hy = [], [], [], []
    for p in range(2):
        ex0, ey0 = e(p, 0, z0), e(p, 1, z0)
        ex1, ey1 = e(p, 0, z0 + 1), e(p, 1, z0 + 1)
        ex.append(ex0)
        ey.append(ey0)
        one_x, one_y = (1.0, 0.0) if p == 0 else (0.0, 1.0)
        hx.append((one_x - 2.0 * (ey1[0] - ey0[0]), -2.0 * (ey1[1] - ey0[1])))
        hy.append((one_y + 2.0 * (ex1[0] - ex0[0]), 2.0 * (ex1[1] - ex0[1])))
    det = csub(cmul(hx[0], hy[1]), cmul(hx[1], hy[0]))
    zxx = cdiv(csub(cmul(ex[0], hy[1]), cmul(ex[1], hy[0])), det, 0.25)
    zxy = cdiv(csub(cmul(ex[1], hx[0]), cmul(ex[0], hx[1])), det, 0.25)
    zyx = cdiv(csub(cmul(ey[0], hy[1]), cmul(ey[1], hy[0])), det, 0.25)
    zyy = cdiv(csub(cmul(ey[1], hx[0]), cmul(ey[0], hx[1])), det, 0.25)
    return [*zxx, *zxy, *zyx, *zyy]


def finish(got, k, *rest):
    fars, (x_far, send, basis, x, kv, surface, picked, sem) = rest[:11], rest[11:]
    pairs = [(k, kv), (fars[0], basis.at[0])]
    for p in range(2):
        pairs += [(fars[1 + 5 * p + i], basis.at[1 + i, pl.ds(p * NF, NF)]) for i in range(5)]
    copies = start_all(pairs, sem)
    sub = lax.broadcasted_iota(jnp.int32, (8, NY), 0)
    row = jnp.broadcast_to(jnp.sum(got[:, 0:NY], axis=0, keepdims=True), (8, NY))
    table = jnp.where(sub == 0, row, pltpu.roll(row, 64, 1))
    cache = {}

    def entry(slot):
        if slot not in cache:
            cache[slot] = jnp.broadcast_to(table[:, slot : slot + 1], (8, NY))
        return cache[slot]

    coefs = coefficients(entry)
    wait_all(copies)
    outs = []
    for p in range(2):
        scal = [tuple(jnp.broadcast_to(part[p : p + 1, :], (8, NY)) for part in c) for c in coefs]

        def block(z, _):
            for xb in range(CX // 8):
                rows = pl.ds(8 * xb, 8)
                kz = kv[z, rows, :]
                inv = 1.0 / (16.0 + kz * kz)
                weight = (4.0 * inv, -kz * inv)
                for f in range(p * NF, p * NF + NF, 2):
                    terms = [cmul(scal[i], (basis[i, f, z, rows, :], basis[i, f + 1, z, rows, :])) for i in range(6)]
                    y = cmul(weight, tree(terms))
                    x[f, z, rows, :] = y[0]
                    x[f + 1, z, rows, :] = y[1]
            return 0

        lax.fori_loop(0, NZL, block, 0)
        part = pl.ds(p * NF, NF)
        outs += start_all([(x.at[part], x_far.at[part])], sem, 12 + p)

    for xb in range(CX // 8):
        rows = pl.ds(8 * xb, 8)
        for v, value in enumerate(impedance(x, 0, rows)):
            surface[v * CX + 8 * xb : v * CX + 8 * xb + 8, :] = value
    mine = pltpu.roll(got[:, NY : 2 * NY], lax.rem(NY - 32 * lax.axis_index("gx"), NY), 1).astype(jnp.int32)
    group = lax.broadcasted_iota(jnp.int32, (32, NY), 1) // 32
    cells = mine[0:32, :]
    for e in range(1, 4):
        cells = jnp.where(group == e, pltpu.roll(mine[32 * e : 32 * e + 32, :], 32 * e, 1), cells)
    col = cells % NY
    line = cells // NY
    cols = [col[8 * i : 8 * i + 8, :] for i in range(4)]
    lines = [line[8 * i : 8 * i + 8, :] for i in range(4)]

    def value(v, _):
        acc = [jnp.zeros((8, NY), f32)] * 4
        for r in range(CX):
            src = jnp.broadcast_to(surface[pl.ds(v * CX + r, 1), :], (8, NY))
            for i in range(4):
                hit = jnp.take_along_axis(src, cols[i], axis=1, mode="promise_in_bounds")
                acc[i] = jnp.where(lines[i] == r, hit, acc[i])
        for i in range(4):
            picked[pl.ds(pl.multiple_of(v * 32, 32) + 8 * i, 8), :] = acc[i]
        return 0

    lax.fori_loop(0, 8, value, 0)
    for e in range(4):
        for h in range(2):
            out = None
            for w in range(4):
                v = 4 * h + w
                part = picked[v * 32 : v * 32 + 32, :]
                if w != e:
                    part = pltpu.roll(part, (32 * (w - e)) % NY, 1)
                out = part if out is None else jnp.where(group == w, part, out)
            send[32 * e : 32 * e + 32, NY * h : NY * h + NY] = out
    wait_all(outs)


def hazard_rows(got, spectra, scenario, out):
    scen = scenario.shape[1]
    turned = []
    for h in range(2):
        block = got[0:8, NY * h : NY * h + NY]
        turned.append(jnp.transpose(jnp.concatenate([block, jnp.zeros((NY - 8, NY), f32)], axis=0)))
    b = [spectra[i : i + 1, :] for i in range(4)]
    bx, by = (b[0], b[1]), (b[2], b[3])
    for j in range(4):
        weight = jnp.where(scenario[...] == j, 1.0, 0.25)
        for qb in range(4):
            z = []
            for v in range(8):
                first = (v % 4) * 32 + 8 * qb
                z.append(jnp.broadcast_to(turned[v // 4][first : first + 8, j : j + 1], (8, scen)))
            gx = cadd(cmul((z[0], z[1]), bx), cmul((z[2], z[3]), by))
            gy = cadd(cmul((z[4], z[5]), bx), cmul((z[6], z[7]), by))
            power = gx[0] * gx[0] + gx[1] * gx[1] + gy[0] * gy[0] + gy[1] * gy[1]
            row = 32 * j + 8 * qb
            out[row : row + 8, :] = weight * power


def partners(count):
    first = [(i, i ^ 1) for i in range(count)]
    second = [(i, ((i + 1) ^ 1) - 1) for i in range(1, count - 1)]
    return first, second


def exchange(to_a, to_b, axis):
    first, second = partners(lax.axis_size(axis))
    return lax.ppermute(to_a, axis, first), lax.ppermute(to_b, axis, second)


def per_device(right_side, conductance, owned_cells, spectra, scenario_tile):
    block = (NF, NZL, CX, NY)
    wide = (NF, NZL, WX, NY)
    whole = (2 * NF, NZL, CX, NY)
    dma = pltpu.SemaphoreType.DMA
    space = pltpu.VMEM((NF, EZ, WX, NY), f32)
    r = right_side.reshape(whole)
    k = conductance
    side = ((2 * NF + 1) * NZL * SIDE, NY)
    rims = [pltpu.VMEM((2 * NF, NZL, 16, NY), f32), pltpu.VMEM((NZL, 16, NY), f32), dma((4,))]
    near = exchange(*call(pack_x, [HBM] * 2, [(side, VM)] * 2, rims)(r, k), "gx")
    deep = [((n * REACH * (CX + 2 * SIDE), NY), VM) for n in (NF + 1, NF)]
    packed = call(pack_z, [VM] * 4, [deep[0]] * 2 + [deep[1]] * 2, moved=1 << 22)(r, k, *near)
    halo_0 = exchange(*packed[0:2], "gz")
    halo_1 = exchange(*packed[2:4], "gz")
    back = ((NF * REACH * BACK, NY), VM)
    firsts = [(block, VM), (block, VM), (wide, VM), back, back, (block, HBM), (block, HBM)]
    cost = {"flops": 1 << 24, "moved": 1 << 23}
    *b_0, to_a, to_b, b1_0, b2_0, m = call(
        first_half_0,
        [VM] * 6,
        firsts + [((2, EZ, WX, NY), VM)],
        [space] * 4 + [dma((2,)), pltpu.VMEM((EZ, WX, NY), f32)],
        **cost,
    )(r, k, *near, *halo_0)
    halo_0 = exchange(to_a, to_b, "gz")
    *b_1, to_a, to_b, b1_1, b2_1 = call(
        first_half_1, [VM] * 6, firsts, [space] * 4 + [dma((2,))], **cost
    )(r, m, *near, *halo_1)
    halo_1 = exchange(to_a, to_b, "gz")
    table = ((64, NY), VM)
    part_0, part_1 = call(low_gram, [VM] * 7, [table] * 2, **cost)(r, *b_0, *b_1)
    seconds = [(block, HBM)] * 3
    spaces = [space] * 6 + [dma((3,))]
    *high_0, total = call(
        second_half_0, [VM] * 8, seconds + [table], spaces, **cost
    )(r, *b_0, m, *halo_0, part_0)
    *high_1, send = call(
        second_half_1,
        [VM] * 10,
        seconds + [((128, 2 * NY), VM)],
        [pltpu.VMEM((64, NY), f32)] + spaces,
        **cost,
    )(r, *b_1, m, *halo_1, part_1, total, owned_cells[0])
    held = (send, k, r, b1_0, b2_0, *high_0, b1_1, b2_1, *high_1)
    send, *fars = lax.optimization_barrier(held)
    got = lax.all_to_all(send, ("gz", "gx"), 0, 0, tiled=True)
    x, send = call(
        finish,
        [VM] + [HBM] * 12,
        [(whole, HBM), ((128, 2 * NY), VM)],
        [
            pltpu.VMEM((6, *whole), f32),
            pltpu.VMEM(whole, f32),
            pltpu.VMEM((NZL, CX, NY), f32),
            pltpu.VMEM((8 * CX, NY), f32),
            pltpu.VMEM((8 * CX, NY), f32),
            dma((14,)),
        ],
    )(got, *fars)
    got = lax.all_to_all(send, ("gz", "gx"), 0, 0, tiled=True)
    scen = spectra.shape[0]
    (hazard,) = call(hazard_rows, [VM] * 3, [((128, scen), VM)])(got, spectra.T, scenario_tile.reshape(1, scen))
    return x.reshape(right_side.shape), hazard


def solution(mesh):
    return jax.shard_map(
        per_device,
        mesh=mesh,
        in_specs=(
            P(None, None, None, "gz", "gx", None),
            P("gz", "gx", None),
            P(("gz", "gx"), None, None),
            P(),
            P(),
        ),
        out_specs=(P(None, None, None, "gz", "gx", None), P(("gz", "gx"), None)),
        check_vma=False,
    )
```

```python
import jax
import jax.numpy as jnp
from jax import lax
from jax.experimental import pallas as pl
from jax.experimental.pallas import tpu as pltpu
from jax.sharding import PartitionSpec as P

SHIFTS = (1.8, 0.6, 1.8, 0.6, 1.8, 0.6)
SCALE = 1.0
ITERS = 3
REACH = 3
SIDE = 2 * REACH
NF = 6
CX, NZL, NY = 32, 4, 128
WX = 48
EZ = NZL + 2 * REACH
BACK = CX + 2 * REACH
f32 = jnp.float32
VM = pl.BlockSpec(memory_space=pltpu.VMEM)
LIMIT = 14 * 1024 * 1024


HBM = pl.BlockSpec(memory_space=pltpu.HBM)


def call(body, ins, outs, scratch=(), flops=0, moved=0):
    return pl.pallas_call(
        body,
        out_shape=[jax.ShapeDtypeStruct(shape, f32) for shape, _ in outs],
        in_specs=ins,
        out_specs=[spec for _, spec in outs],
        scratch_shapes=list(scratch),
        compiler_params=pltpu.CompilerParams(vmem_limit_bytes=LIMIT),
        cost_estimate=pl.CostEstimate(flops=flops, bytes_accessed=moved, transcendentals=0),
    )


def odd(axis):
    return lax.rem(lax.axis_index(axis), 2) == 1


def either(flag, body, first, second):
    @pl.when(jnp.logical_not(flag))
    def _():
        body(first, second)

    @pl.when(flag)
    def _():
        body(second, first)


def start_all(pairs, sem, first=0):
    copies = [pltpu.make_async_copy(src, dst, sem.at[first + i]) for i, (src, dst) in enumerate(pairs)]
    for copy in copies:
        copy.start()
    return copies


def wait_all(copies):
    for copy in copies:
        copy.wait()


def pack_x(r_far, k_far, to_a, to_b, r, k, sem):
    wait_all(start_all([(r_far, r), (k_far, k)], sem))

    def fill(up, down):
        for f in range(2 * NF + 1):
            for z in range(NZL):
                row = (f * NZL + z) * SIDE
                src = k.at[z] if f == 2 * NF else r.at[f, z]
                up[row : row + SIDE, :] = src[CX - SIDE : CX, :]
                down[row : row + SIDE, :] = src[0:SIDE, :]

    either(odd("gx"), fill, to_a, to_b)


def sides(from_a, from_b, near):
    a, b = from_a[near : near + SIDE, :], from_b[near : near + SIDE, :]
    flag = odd("gx")
    return jnp.where(flag, a, b), jnp.where(flag, b, a)


def pack_z(r, k, xa, xb, a_0, b_0, a_1, b_1):
    width = CX + 2 * SIDE

    def fill(first, second):
        outs = [((first[p], NZL - REACH), (second[p], 0)) for p in range(2)]
        for p in range(2):
            fields = [p * NF + i for i in range(NF)] + ([2 * NF] if p == 0 else [])
            for at, f in enumerate(fields):
                for z in range(NZL):
                    left, right = sides(xa, xb, (f * NZL + z) * SIDE)
                    src = k.at[z] if f == 2 * NF else r.at[f, z]
                    for out, low in outs[p]:
                        if low <= z < low + REACH:
                            row = (at * REACH + z - low) * width
                            out[row : row + SIDE, :] = left
                            out[row + SIDE : row + SIDE + CX, :] = src[:, :]
                            out[row + SIDE + CX : row + width, :] = right

    either(odd("gz"), fill, (a_0, a_1), (b_0, b_1))


def lanes():
    lane = lax.broadcasted_iota(jnp.int32, (WX, NY), 1)
    return lane == 0, lane == NY - 1


def next_y(a, last):
    return jnp.where(last, 0.0, pltpu.roll(a, NY - 1, 1))


def next_x(a):
    return pltpu.roll(a, WX - 1, 0)


def prev_x(a):
    return pltpu.roll(a, 1, 0)


def smooth(b, y, m, base, z):
    mr, mi = m[0, z], m[1, z]
    for c in range(3):
        re, im = b[base + 2 * c, z], b[base + 2 * c + 1, z]
        y[base + 2 * c, z] = mr * re - mi * im
        y[base + 2 * c + 1, z] = mr * im + mi * re


def apply_k(b, y, bn, yn, hs, m, lo, hi, shift, want_y):
    first, last = lanes()
    own = (1.0 - shift) / SCALE
    inv = 1.0 / SCALE
    for z in range(lo - 1, hi):
        for e in range(2):
            ex, ey, ez = y[e, z], y[e + 2, z], y[e + 4, z]
            hs[e, z] = next_y(ez, last) - ez - (y[e + 2, z + 1] - ey)
            hs[e + 2, z] = y[e, z + 1] - ex - (next_x(ez) - ez)
            hs[e + 4, z] = next_x(ey) - ey - (next_y(ex, last) - ex)
    for z in range(lo, hi):
        for e in range(2):
            hx, hy, hz = hs[e, z], hs[e + 2, z], hs[e + 4, z]
            ex, ey, ez = y[e, z], y[e + 2, z], y[e + 4, z]
            cx = hz - jnp.where(first, -ex, pltpu.roll(hz, 1, 1)) - (hy - hs[e + 2, z - 1])
            cy = hx - hs[e, z - 1] - (hz - prev_x(hz))
            cz = hy - prev_x(hy) - (hx - jnp.where(first, ez, pltpu.roll(hx, 1, 1)))
            for c, (cur, old) in enumerate(((cx, ex), (cy, ey), (cz, ez))):
                new = cur - 4.0 * old
                if inv != 1.0:
                    new = new * inv
                bn[e + 2 * c, z] = new + own * b[e + 2 * c, z]
        if want_y:
            smooth(bn, yn, m, 0, z)


def all_smooth(b, y, m):
    def layer(z, _):
        smooth(b, y, m, 0, z)
        return 0

    lax.fori_loop(0, EZ, layer, 0)


def weights(k, xa, xb, za, zb, m, kx):
    extend([kx], [k], xa, xb, za, zb, 2 * NF, NF)

    def layer(z, _):
        kz = kx[z]
        inv = jnp.where(kz > 0.0, 1.0, 0.0) / (16.0 + kz * kz)
        m[0, z] = 4.0 * inv
        m[1, z] = -kz * inv
        return 0

    lax.fori_loop(0, EZ, layer, 0)


def extend(outs, srcs, xa, xb, za, zb, near, far):
    width = CX + 2 * SIDE
    x0 = 8 - SIDE
    zero = jnp.zeros((EZ, 8, NY), f32)
    for i, (dst, src) in enumerate(zip(outs, srcs)):
        dst[:, 0:8, :] = zero
        dst[:, WX - 8 : WX, :] = zero
        for z in range(NZL):
            left, right = sides(xa, xb, ((near + i) * NZL + z) * SIDE)
            dst[REACH + z, x0:8, :] = left
            dst[REACH + z, 8 : 8 + CX, :] = src[z]
            dst[REACH + z, 8 + CX : 8 + CX + SIDE, :] = right

    def fill(above, below):
        for i, dst in enumerate(outs):
            for z in range(REACH):
                row = ((far + i) * REACH + z) * width
                dst[z, x0 : x0 + width, :] = below[row : row + width, :]
                dst[REACH + NZL + z, x0 : x0 + width, :] = above[row : row + width, :]

    either(odd("gz"), fill, za, zb)


def keep(src, out):
    def field(f, _):
        out[f] = src[f, REACH : REACH + NZL, 8 : 8 + CX, :]
        return 0

    lax.fori_loop(0, NF, field, 0)


def first_steps(p, r, xa, xb, za, zb, b1, b2, b3w, to_a, to_b, b1_far, b2_far, m, ba, bb, ya, yb, hs, sem):
    fields = range(NF)
    extend([ba.at[f] for f in fields], [r.at[p * NF + f] for f in fields], xa, xb, za, zb, p * NF, 0)
    all_smooth(ba, ya, m)
    apply_k(ba, ya, bb, yb, hs, m, 1, EZ - 1, SHIFTS[0], True)
    keep(bb, b1)
    copies = start_all([(b1, b1_far)], sem)
    apply_k(bb, yb, ba, ya, hs, m, 2, EZ - 2, SHIFTS[1], True)
    keep(ba, b2)
    copies += start_all([(b2, b2_far)], sem, 1)
    apply_k(ba, ya, bb, yb, hs, m, 3, EZ - 3, SHIFTS[2], False)
    cut = (WX - BACK) // 2
    for f in fields:
        b3w[f] = bb[f, REACH : REACH + NZL]

    def fill(up, down):
        for f in fields:
            for z in range(REACH):
                row = (f * REACH + z) * BACK
                up[row : row + BACK, :] = bb[f, NZL + z, cut : cut + BACK, :]
                down[row : row + BACK, :] = bb[f, REACH + z, cut : cut + BACK, :]

    either(odd("gz"), fill, to_a, to_b)
    wait_all(copies)


def first_half_0(r, k, xa, xb, za, zb, b1, b2, b3w, to_a, to_b, b1_far, b2_far, m, ba, bb, ya, yb, hs, sem, kx):
    weights(k, xa, xb, za, zb, m, kx)
    first_steps(0, r, xa, xb, za, zb, b1, b2, b3w, to_a, to_b, b1_far, b2_far, m, ba, bb, ya, yb, hs, sem)


def first_half_1(r, m, xa, xb, za, zb, b1, b2, b3w, to_a, to_b, b1_far, b2_far, ba, bb, ya, yb, hs, sem):
    first_steps(1, r, xa, xb, za, zb, b1, b2, b3w, to_a, to_b, b1_far, b2_far, m, ba, bb, ya, yb, hs, sem)


PAIRS = [(i, j) for i in range(7) for j in range(i, 7)]
LOW = [pair for pair in PAIRS if pair[1] <= REACH]
HIGH = [pair for pair in PAIRS if pair[1] > REACH]
SLOT = {}
for _pair in LOW + HIGH:
    SLOT[_pair] = sum(1 if a == b else 2 for a, b in SLOT)


def gram(read, pairs, out):
    used = sorted({i for pair in pairs for i in pair})
    count = sum(1 if i == j else 2 for i, j in pairs)

    def block(step, acc):
        c, z = step // NZL, step % NZL
        acc = list(acc)
        for xb in range(CX // 8):
            vec = {i: (read(i, 2 * c, z, xb), read(i, 2 * c + 1, z, xb)) for i in used}
            at = 0
            for i, j in pairs:
                (ar, ai), (br, bi) = vec[i], vec[j]
                acc[at] = acc[at] + (ar * br + ai * bi)
                at += 1
                if i != j:
                    acc[at] = acc[at] + (ar * bi - ai * br)
                    at += 1
        return tuple(acc)

    acc = lax.fori_loop(0, 3 * NZL, block, (jnp.zeros((8, NY), f32),) * count)
    at = 0
    for i, j in pairs:
        for part in range(1 if i == j else 2):
            row = SLOT[i, j] + part
            out[row : row + 1, :] = jnp.sum(acc[at], axis=0, keepdims=True)
            at += 1


def low_gram(b0, b1_0, b2_0, b3w_0, b1_1, b2_1, b3w_1, part_0, part_1):
    for p, (b1, b2, b3w, part) in enumerate(((b1_0, b2_0, b3w_0, part_0), (b1_1, b2_1, b3w_1, part_1))):
        part[...] = jnp.zeros((64, NY), f32)
        gram(reader(p, b0, b1, b2, b3w), LOW, part)


def reader(p, b0, b1, b2, b3w, *slabs):
    def read(i, f, z, xb):
        if i == 0:
            return b0[p * NF + f, z, pl.ds(8 * xb, 8), :]
        if i < 3:
            return (b1, b2)[i - 1][f, z, pl.ds(8 * xb, 8), :]
        if i == 3:
            return b3w[f, z, pl.ds(8 + 8 * xb, 8), :]
        return slabs[i - 4][f, REACH + z, pl.ds(8 + 8 * xb, 8), :]

    return read


def second_steps(p, b0, b1, b2, b3w, m, za, zb, part, b3_far, b4_far, b5_far, total, ba, bb, bc, bd, ya, yb, hs, sem):
    cut = (WX - BACK) // 2
    own = pl.ds(REACH, NZL)
    mid = pl.ds(8, CX)
    copies = start_all([(b3w.at[:, :, mid, :], b3_far)], sem)
    zero = jnp.zeros((REACH, 8, NY), f32)
    for f in range(NF):
        for first in (0, REACH + NZL):
            ba[f, first : first + REACH, 0:8, :] = zero
            ba[f, first : first + REACH, WX - 8 : WX, :] = zero
        ba[f, REACH : REACH + NZL] = b3w[f]

    def fill(above, below):
        for f in range(NF):
            for z in range(REACH):
                row = (f * REACH + z) * BACK
                ba[f, z, cut : cut + BACK, :] = below[row : row + BACK, :]
                ba[f, REACH + NZL + z, cut : cut + BACK, :] = above[row : row + BACK, :]

    either(odd("gz"), fill, za, zb)
    all_smooth(ba, ya, m)
    apply_k(ba, ya, bb, yb, hs, m, 1, EZ - 1, SHIFTS[3], True)
    copies += start_all([(bb.at[:, own, mid, :], b4_far)], sem, 1)
    apply_k(bb, yb, bc, ya, hs, m, 2, EZ - 2, SHIFTS[4], True)
    copies += start_all([(bc.at[:, own, mid, :], b5_far)], sem, 2)
    apply_k(bc, ya, bd, yb, hs, m, 3, EZ - 3, SHIFTS[5], False)
    total[...] = part[...]
    gram(reader(p, b0, b1, b2, b3w, bb, bc, bd), HIGH, total)
    wait_all(copies)


def second_half_0(b0, b1, b2, b3w, m, za, zb, part, b3_far, b4_far, b5_far, total, *space):
    second_steps(0, b0, b1, b2, b3w, m, za, zb, part, b3_far, b4_far, b5_far, total, *space)


def second_half_1(b0, b1, b2, b3w, m, za, zb, part, other, owned, b3_far, b4_far, b5_far, send, total, *space):
    second_steps(1, b0, b1, b2, b3w, m, za, zb, part, b3_far, b4_far, b5_far, total, *space)
    both = jnp.concatenate([other[...], total[...]], axis=0)
    sums = jnp.sum(jnp.transpose(both), axis=0, keepdims=True)
    cells = jnp.concatenate([owned[j : j + 1, :] for j in range(4)], axis=1).astype(f32)
    send[...] = jnp.broadcast_to(jnp.concatenate([sums, cells], axis=1), (128, 2 * NY))


def cadd(a, b):
    return (a[0] + b[0], a[1] + b[1])


def csub(a, b):
    return (a[0] - b[0], a[1] - b[1])


def cmul(a, b):
    return (a[0] * b[0] - a[1] * b[1], a[0] * b[1] + a[1] * b[0])


def cconj_mul(a, b):
    return (a[0] * b[0] + a[1] * b[1], a[0] * b[1] - a[1] * b[0])


def cdiv(numer, denom, floor):
    size = jnp.maximum(denom[0] * denom[0] + denom[1] * denom[1], floor)
    return (
        (numer[0] * denom[0] + numer[1] * denom[1]) / size,
        (numer[1] * denom[0] - numer[0] * denom[1]) / size,
    )


def tree(terms):
    terms = list(terms)
    while len(terms) > 1:
        terms = [cadd(*terms[i : i + 2]) if i + 1 < len(terms) else terms[i] for i in range(0, len(terms), 2)]
    return terms[0]


def combine(a, scale, b):
    out = []
    for i in range(max(len(a), len(b))):
        if i >= len(b):
            out.append(a[i])
        elif i >= len(a):
            out.append(cmul(scale, b[i]))
        else:
            out.append(cadd(a[i], cmul(scale, b[i])))
    return out


def times_k(a):
    zero = (jnp.zeros_like(a[0][0]),) * 2
    out = [(SHIFTS[i] * v[0], SHIFTS[i] * v[1]) for i, v in enumerate(a)] + [zero]
    return [
        cadd(out[i], (SCALE * a[i - 1][0], SCALE * a[i - 1][1])) if i > 0 else out[i]
        for i in range(len(out))
    ]


def coefficients(entry):
    def g(i, j):
        if i > j:
            re, im = g(j, i)
            return (re, -im)
        if i == j:
            return (entry(SLOT[i, j]), 0.0)
        return (entry(SLOT[i, j]), entry(SLOT[i, j] + 1))

    def times_g(b, rows):
        return [tree([cmul(g(i, j), b[j]) for j in range(len(b))]) for i in range(rows)]

    def dot(a, gb):
        return tree([cconj_mul(a[i], gb[i]) for i in range(len(a))])

    def shadow(b):
        return tree([cmul(g(0, j), b[j]) for j in range(len(b))])

    one = jnp.ones_like(entry(0))
    residual = [(one, jnp.zeros_like(one))]
    direction = residual
    solution = []
    for step in range(ITERS):
        rho = shadow(residual)
        if step == 0:
            floor = 1e-06 * rho[0] * rho[0]
        else:
            beta = cmul(cdiv(rho, rho_prev, floor), cdiv(alpha, omega, 0.0001))
            minus = (-omega[0], -omega[1])
            direction = combine(residual, beta, combine(direction, minus, image))
        image = times_k(direction)
        alpha = cdiv(rho, shadow(image), floor)
        middle = combine(residual, (-alpha[0], -alpha[1]), image)
        bent = times_k(middle)
        seen = times_g(bent, len(bent))
        norm = dot(bent, seen)[0] + 1e-06
        against = dot(middle, seen)
        omega = (against[0] / norm, -against[1] / norm)
        solution = combine(combine(solution, alpha, direction), omega, middle)
        residual = combine(middle, (-omega[0], -omega[1]), bent)
        rho_prev = rho
    return solution


def surface_power(x, rows):
    def e(p, c, z):
        f = p * NF + 2 * c
        return (x[f, z, rows, :], x[f + 1, z, rows, :])

    ex, ey, hx, hy = [], [], [], []
    for p in range(2):
        ex0, ey0 = e(p, 0, 0), e(p, 1, 0)
        ex1, ey1 = e(p, 0, 1), e(p, 1, 1)
        ex.append(ex0)
        ey.append(ey0)
        one_x, one_y = (1.0, 0.0) if p == 0 else (0.0, 1.0)
        hx.append((one_x - 2.0 * (ey1[0] - ey0[0]), -2.0 * (ey1[1] - ey0[1])))
        hy.append((one_y + 2.0 * (ex1[0] - ex0[0]), 2.0 * (ex1[1] - ex0[1])))
    det = csub(cmul(hx[0], hy[1]), cmul(hx[1], hy[0]))
    zxx = csub(cmul(ex[0], hy[1]), cmul(ex[1], hy[0]))
    zxy = csub(cmul(ex[1], hx[0]), cmul(ex[0], hx[1]))
    zyx = csub(cmul(ey[0], hy[1]), cmul(ey[1], hy[0]))
    zyy = csub(cmul(ey[1], hx[0]), cmul(ey[0], hx[1]))
    size = det[0] * det[0] + det[1] * det[1]
    inv = 1.0 / jnp.maximum(size, 0.25)
    scale = size * inv * inv
    cross = cadd(cconj_mul(zxx, zxy), cconj_mul(zyx, zyy))
    first = zxx[0] * zxx[0] + zxx[1] * zxx[1] + (zyx[0] * zyx[0] + zyx[1] * zyx[1])
    second = zxy[0] * zxy[0] + zxy[1] * zxy[1] + (zyy[0] * zyy[0] + zyy[1] * zyy[1])
    return [scale * first, scale * second, scale * cross[0], scale * cross[1]]


def finish(got, k, *rest):
    fars, (x_far, send, basis, x, kv, surface, picked, sem) = rest[:11], rest[11:]
    pairs = []
    for z in (0, 2):
        part = pl.ds(z, 2)
        pairs.append((k.at[part], kv.at[part]))
        pairs.append((fars[0].at[:, part], basis.at[0, :, part]))
        for p in range(2):
            for i in range(5):
                pairs.append((fars[1 + 5 * p + i].at[:, part], basis.at[1 + i, pl.ds(p * NF, NF), part]))
    copies = start_all(pairs, sem)
    sub = lax.broadcasted_iota(jnp.int32, (8, NY), 0)
    row = jnp.broadcast_to(jnp.sum(got[:, 0:NY], axis=0, keepdims=True), (8, NY))
    table = jnp.where(sub == 0, row, pltpu.roll(row, 64, 1))
    cache = {}

    def entry(slot):
        if slot not in cache:
            cache[slot] = jnp.broadcast_to(table[:, slot : slot + 1], (8, NY))
        return cache[slot]

    coefs = coefficients(entry)
    scal = [[tuple(jnp.broadcast_to(half[p : p + 1, :], (8, NY)) for half in c) for c in coefs] for p in range(2)]

    mine = pltpu.roll(got[:, NY : 2 * NY], lax.rem(NY - 32 * lax.axis_index("gx"), NY), 1).astype(jnp.int32)
    group = lax.broadcasted_iota(jnp.int32, (32, NY), 1) // 32
    cells = mine[0:32, :]
    for e in range(1, 4):
        cells = jnp.where(group == e, pltpu.roll(mine[32 * e : 32 * e + 32, :], 32 * e, 1), cells)
    col = cells % NY
    line = cells // NY
    cols = [col[8 * i : 8 * i + 8, :] for i in range(4)]
    lines = [line[8 * i : 8 * i + 8, :] for i in range(4)]

    def layer(p, z):
        for xb in range(CX // 8):
            rows = pl.ds(8 * xb, 8)
            kz = kv[z, rows, :]
            inv = 1.0 / (16.0 + kz * kz)
            weight = (4.0 * inv, -kz * inv)
            for f in range(p * NF, p * NF + NF, 2):
                terms = [cmul(scal[p][i], (basis[i, f, z, rows, :], basis[i, f + 1, z, rows, :])) for i in range(6)]
                y = cmul(weight, tree(terms))
                x[f, z, rows, :] = y[0]
                x[f + 1, z, rows, :] = y[1]

    outs = []

    def leave(p, z, count):
        part = pl.ds(p * NF, NF), pl.ds(z, count)
        outs.extend(start_all([(x.at[part], x_far.at[part])], sem, len(pairs) + len(outs)))

    half = len(pairs) // 2
    wait_all(copies[:half])
    for p in range(2):
        for z in range(2):
            layer(p, z)
        leave(p, 0, 2)
    for xb in range(CX // 8):
        for v, value in enumerate(surface_power(x, pl.ds(8 * xb, 8))):
            surface[v * CX + 8 * xb : v * CX + 8 * xb + 8, :] = value
    wait_all(copies[half:])
    for v in range(4):
        acc = [jnp.zeros((8, NY), f32)] * 4
        for r in range(CX):
            src = jnp.broadcast_to(surface[v * CX + r : v * CX + r + 1, :], (8, NY))
            for i in range(4):
                hit = jnp.take_along_axis(src, cols[i], axis=1, mode="promise_in_bounds")
                acc[i] = jnp.where(lines[i] == r, hit, acc[i])
        for i in range(4):
            picked[v * 32 + 8 * i : v * 32 + 8 * i + 8, :] = acc[i]
        p, z = v // 2, 2 + v % 2
        layer(p, z)
        leave(p, z, 1)
    for e in range(4):
        out = None
        for v in range(4):
            part = picked[v * 32 : v * 32 + 32, :]
            if v != e:
                part = pltpu.roll(part, (32 * (v - e)) % NY, 1)
            out = part if out is None else jnp.where(group == v, part, out)
        send[32 * e : 32 * e + 32, :] = out
    wait_all(outs)


def hazard_rows(got, spectra, scenario, out):
    scen = scenario.shape[1]
    block = jnp.concatenate([got[0:8, :], jnp.zeros((NY - 8, NY), f32)], axis=0)
    turned = jnp.transpose(block)
    xr, xi, yr, yi = [spectra[i : i + 1, :] for i in range(4)]
    base = [
        xr * xr + xi * xi,
        yr * yr + yi * yi,
        2.0 * (xr * yr + xi * yi),
        2.0 * (xi * yr - xr * yi),
    ]
    for j in range(4):
        weight = jnp.where(scenario[...] == j, 1.0, 0.25)
        power = [weight * value for value in base]
        for qb in range(4):
            total = None
            for v in range(4):
                first = v * 32 + 8 * qb
                term = jnp.broadcast_to(turned[first : first + 8, j : j + 1], (8, scen)) * power[v]
                total = term if total is None else total + term
            row = 32 * j + 8 * qb
            out[row : row + 8, :] = total


def partners(count):
    first = [(i, i ^ 1) for i in range(count)]
    second = [(i, ((i + 1) ^ 1) - 1) for i in range(1, count - 1)]
    return first, second


def exchange(to_a, to_b, axis):
    first, second = partners(lax.axis_size(axis))
    return lax.ppermute(to_a, axis, first), lax.ppermute(to_b, axis, second)


def per_device(right_side, conductance, owned_cells, spectra, scenario_tile):
    block = (NF, NZL, CX, NY)
    wide = (NF, NZL, WX, NY)
    whole = (2 * NF, NZL, CX, NY)
    dma = pltpu.SemaphoreType.DMA
    space = pltpu.VMEM((NF, EZ, WX, NY), f32)
    r_far = right_side.reshape(whole)
    side = (((2 * NF + 1) * NZL * SIDE, NY), VM)
    loaded = [(whole, VM), ((NZL, CX, NY), VM)]
    to_a, to_b, r, k = call(pack_x, [HBM] * 2, [side] * 2 + loaded, [dma((2,))])(r_far, conductance)
    near = exchange(to_a, to_b, "gx")
    deep = [((n * REACH * (CX + 2 * SIDE), NY), VM) for n in (NF + 1, NF)]
    packed = call(pack_z, [VM] * 4, [deep[0]] * 2 + [deep[1]] * 2, moved=1 << 22)(r, k, *near)
    halo_0 = exchange(*packed[0:2], "gz")
    halo_1 = exchange(*packed[2:4], "gz")
    back = ((NF * REACH * BACK, NY), VM)
    firsts = [(block, VM), (block, VM), (wide, VM), back, back, (block, HBM), (block, HBM)]
    cost = {"flops": 1 << 24, "moved": 1 << 23}
    *b_0, to_a, to_b, b1_0, b2_0, m = call(
        first_half_0,
        [VM] * 6,
        firsts + [((2, EZ, WX, NY), VM)],
        [space] * 5 + [dma((2,)), pltpu.VMEM((EZ, WX, NY), f32)],
        **cost,
    )(r, k, *near, *halo_0)
    halo_0 = exchange(to_a, to_b, "gz")
    *b_1, to_a, to_b, b1_1, b2_1 = call(
        first_half_1, [VM] * 6, firsts, [space] * 5 + [dma((2,))], **cost
    )(r, m, *near, *halo_1)
    halo_1 = exchange(to_a, to_b, "gz")
    table = ((64, NY), VM)
    part_0, part_1 = call(low_gram, [VM] * 7, [table] * 2, **cost)(r, *b_0, *b_1)
    seconds = [(block, HBM)] * 3
    spaces = [space] * 7 + [dma((3,))]
    *high_0, total = call(
        second_half_0, [VM] * 8, seconds + [table], spaces, **cost
    )(r, *b_0, m, *halo_0, part_0)
    *high_1, send = call(
        second_half_1,
        [VM] * 10,
        seconds + [((128, 2 * NY), VM)],
        [pltpu.VMEM((64, NY), f32)] + spaces,
        **cost,
    )(r, *b_1, m, *halo_1, part_1, total, owned_cells[0])
    held = (send, conductance, r_far, b1_0, b2_0, *high_0, b1_1, b2_1, *high_1)
    send, *fars = lax.optimization_barrier(held)
    got = lax.all_to_all(send, ("gz", "gx"), 0, 0, tiled=True)
    x, send = call(
        finish,
        [VM] + [HBM] * 12,
        [(whole, HBM), ((128, NY), VM)],
        [
            pltpu.VMEM((6, *whole), f32),
            pltpu.VMEM(whole, f32),
            pltpu.VMEM((NZL, CX, NY), f32),
            pltpu.VMEM((4 * CX, NY), f32),
            pltpu.VMEM((4 * CX, NY), f32),
            dma((30,)),
        ],
    )(got, *fars)
    got = lax.all_to_all(send, ("gz", "gx"), 0, 0, tiled=True)
    scen = spectra.shape[0]
    (hazard,) = call(hazard_rows, [VM] * 3, [((128, scen), VM)])(got, spectra.T, scenario_tile.reshape(1, scen))
    return x.reshape(right_side.shape), hazard


def solution(mesh):
    return jax.shard_map(
        per_device,
        mesh=mesh,
        in_specs=(
            P(None, None, None, "gz", "gx", None),
            P("gz", "gx", None),
            P(("gz", "gx"), None, None),
            P(),
            P(),
        ),
        out_specs=(P(None, None, None, "gz", "gx", None), P(("gz", "gx"), None)),
        check_vma=False,
    )
```

```python
import jax
import jax.numpy as jnp
from jax import lax
from jax.experimental import pallas as pl
from jax.experimental.pallas import tpu as pltpu
from jax.sharding import PartitionSpec as P

SHIFTS = (1.8, 0.6, 1.8, 0.6, 1.8, 0.6)
SCALE = 1.0
ITERS = 3
REACH = 3
SIDE = 2 * REACH
NF = 6
CX, NZL, NY = 32, 4, 128
WX = 48
EZ = NZL + 2 * REACH
f32 = jnp.float32
VM = pl.BlockSpec(memory_space=pltpu.VMEM)
LIMIT = 14 * 1024 * 1024
FIRST_LIMIT = 60 * 1024 * 1024


HBM = pl.BlockSpec(memory_space=pltpu.HBM)


def call(body, ins, outs, scratch=(), flops=0, moved=0, limit=LIMIT):
    return pl.pallas_call(
        body,
        out_shape=[jax.ShapeDtypeStruct(shape, f32) for shape, _ in outs],
        in_specs=ins,
        out_specs=[spec for _, spec in outs],
        scratch_shapes=list(scratch),
        compiler_params=pltpu.CompilerParams(vmem_limit_bytes=limit),
        cost_estimate=pl.CostEstimate(flops=flops, bytes_accessed=moved, transcendentals=0),
    )


def odd(axis):
    return lax.rem(lax.axis_index(axis), 2) == 1


def either(flag, body, first, second):
    @pl.when(jnp.logical_not(flag))
    def _():
        body(first, second)

    @pl.when(flag)
    def _():
        body(second, first)


def start_all(pairs, sem, first=0):
    copies = [pltpu.make_async_copy(src, dst, sem.at[first + i]) for i, (src, dst) in enumerate(pairs)]
    for copy in copies:
        copy.start()
    return copies


def wait_all(copies):
    for copy in copies:
        copy.wait()


def pack_x(r, k, spectra, scenario, to_a, to_b, power, rim, rim_k, spec, scen, sem):
    pairs = []
    for i in range(2):
        src = pl.ds(i * (CX - 8), 8)
        pairs.append((r.at[:, :, src, :], rim.at[:, :, pl.ds(8 * i, 8), :]))
        pairs.append((k.at[:, src, :], rim_k.at[:, pl.ds(8 * i, 8), :]))
    pairs += [(spectra, spec), (scenario, scen)]
    wait_all(start_all(pairs, sem))

    def fill(up, down):
        for f in range(2 * NF + 1):
            for z in range(NZL):
                row = (f * NZL + z) * SIDE
                src = rim_k.at[z] if f == 2 * NF else rim.at[f, z]
                up[row : row + SIDE, :] = src[16 - SIDE : 16, :]
                down[row : row + SIDE, :] = src[0:SIDE, :]

    either(odd("gx"), fill, to_a, to_b)
    xr, xi, yr, yi = [spec[i : i + 1, :] for i in range(4)]
    base = [
        xr * xr + xi * xi,
        yr * yr + yi * yi,
        2.0 * (xr * yr + xi * yi),
        2.0 * (xi * yr - xr * yi),
    ]
    for j in range(4):
        weight = jnp.where(scen[...] == j, 1.0, 0.25)
        for v in range(4):
            power[4 * j + v : 4 * j + v + 1, :] = weight * base[v]


def sides(from_a, from_b, near):
    a, b = from_a[near : near + SIDE, :], from_b[near : near + SIDE, :]
    flag = odd("gx")
    return jnp.where(flag, a, b), jnp.where(flag, b, a)


def spans(margin):
    low, high = margin + REACH, CX - 1 + margin
    below = ((1 - low, high + 3), (2 - low, high + 3), (3 - low, high + 2))
    above = ((-low, high + 2), (-low, high + 1), (-low, high))
    return below, above


def layout(span, with_k):
    near, row = {}, 0
    for i in range(REACH - 1):
        for f in range(NF):
            near[i, f] = row
            row += span[i][1] - span[i][0] + 1
    far = []
    for _ in range(4):
        far.append(row)
        row += span[-1][1] - span[-1][0] + 1
    k = []
    for i in range(REACH - 1 if with_k else 0):
        k.append(row)
        row += span[i][1] - span[i][0] + 1
    return near, far, k, row


def rows_of(margin, with_k):
    return max(layout(span, with_k)[3] for span in spans(margin))


def cut(span):
    return slice(8 + span[0], 9 + span[1]), span[1] - span[0] + 1


def far_fields(b, first, weight, far):
    _, last = lanes()

    def y(z, c):
        mr, mi = weight(z)
        re, im = b[2 * c, first + z], b[2 * c + 1, first + z]
        return mr * re - mi * im, mr * im + mi * re

    ex, ey, ez = [y(NZL - REACH, c) for c in range(3)]
    for q in range(2):
        far[q] = ex[q] + (next_x(ez[q]) - ez[q])
        far[2 + q] = ey[q] + (next_y(ez[q], last) - ez[q])
    for c in range(2):
        far[4 + 2 * c], far[5 + 2 * c] = y(REACH - 1, c)


def fill_messages(b, first, far, k, margin, up, down):
    for side, (out, span) in enumerate(zip((up, down), spans(margin))):
        near, far_rows, k_rows, _ = layout(span, k is not None)
        for i in range(REACH - 1):
            z = first + (NZL - 1 - i if side == 0 else i)
            cols, n = cut(span[i])
            for f in range(NF):
                out[near[i, f] : near[i, f] + n, :] = b[f, z, cols, :]
            if k is not None:
                out[k_rows[i] : k_rows[i] + n, :] = k[z, cols, :]
        cols, n = cut(span[-1])
        for j, row in enumerate(far_rows):
            out[row : row + n, :] = far[4 * side + j, cols, :]


def take_messages(b, y, k, margin, above, below):
    for side, (src, span) in enumerate(zip((below, above), spans(margin))):
        near, far_rows, k_rows, _ = layout(span, k is not None)
        for i in range(REACH - 1):
            z = REACH - 1 - i if side == 0 else REACH + NZL + i
            cols, n = cut(span[i])
            for f in range(NF):
                b[f, z, cols, :] = src[near[i, f] : near[i, f] + n, :]
            if k is not None:
                k[z, cols, :] = src[k_rows[i] : k_rows[i] + n, :]
        cols, n = cut(span[-1])
        z = 0 if side == 0 else EZ - 1
        for j, row in enumerate(far_rows):
            y[j, z, cols, :] = src[row : row + n, :]


def clear_sides(ref):
    zero = jnp.zeros((EZ, 8, NY), f32)
    ref[:, 0:8, :] = zero
    ref[:, WX - 8 : WX, :] = zero


def clear_far(y):
    for f in range(NF):
        for z in (0, EZ - 1):
            if f < 4:
                y[f, z, 0:8, :] = jnp.zeros((8, NY), f32)
                y[f, z, WX - 8 : WX, :] = jnp.zeros((8, NY), f32)
            else:
                y[f, z] = jnp.zeros((WX, NY), f32)


def own_layers(dst, first, src, xa, xb, near):
    for z in range(NZL):
        left, right = sides(xa, xb, (near * NZL + z) * SIDE)
        dst[first + z, 8 - SIDE : 8, :] = left
        dst[first + z, 8 : 8 + CX, :] = src[z]
        dst[first + z, 8 + CX : 8 + CX + SIDE, :] = right


def weight_of(kz):
    inv = jnp.where(kz > 0.0, 1.0, 0.0) / (16.0 + kz * kz)
    return 4.0 * inv, -kz * inv


def pack_z(r, k, xa, xb, owned, a_0, b_0, a_1, b_1, cells, b, kx, far):
    for f in range(2 * NF + 1):
        dst = kx if f == 2 * NF else b.at[f]
        zero = jnp.zeros((NZL, 8, NY), f32)
        dst[:, 0:8, :] = zero
        dst[:, WX - 8 : WX, :] = zero
        own_layers(dst, 0, k if f == 2 * NF else r.at[f], xa, xb, f)
    weights = {z: weight_of(kx[z]) for z in (NZL - REACH, REACH - 1)}
    for p in range(2):
        far_fields(b.at[pl.ds(p * NF, NF)], 0, lambda z: weights[z], far.at[p])

    def fill(first, second):
        for p in range(2):
            own = b.at[pl.ds(p * NF, NF)]
            fill_messages(own, 0, far.at[p], kx if p == 0 else None, REACH, first[p], second[p])

    either(odd("gz"), fill, (a_0, a_1), (b_0, b_1))
    cells[...] = jnp.concatenate([owned[j : j + 1, :] for j in range(4)], axis=1).astype(f32)


def lanes():
    lane = lax.broadcasted_iota(jnp.int32, (WX, NY), 1)
    return lane == 0, lane == NY - 1


def next_y(a, last):
    return jnp.where(last, 0.0, pltpu.roll(a, NY - 1, 1))


def next_x(a):
    return pltpu.roll(a, WX - 1, 0)


def prev_x(a):
    return pltpu.roll(a, 1, 0)


def smooth(b, y, m, base, z):
    mr, mi = m[0, z], m[1, z]
    for c in range(3):
        re, im = b[base + 2 * c, z], b[base + 2 * c + 1, z]
        y[base + 2 * c, z] = mr * re - mi * im
        y[base + 2 * c + 1, z] = mr * im + mi * re


def apply_k(b, y, bn, yn, hs, m, lo, hi, shift, want_y):
    first, last = lanes()
    own = (1.0 - shift) / SCALE
    inv = 1.0 / SCALE
    for z in range(lo - 1, hi):
        for e in range(2):
            ex, ey, ez = y[e, z], y[e + 2, z], y[e + 4, z]
            hs[e, z] = next_y(ez, last) - ez - (y[e + 2, z + 1] - ey)
            hs[e + 2, z] = y[e, z + 1] - ex - (next_x(ez) - ez)
            hs[e + 4, z] = next_x(ey) - ey - (next_y(ex, last) - ex)
    for z in range(lo, hi):
        for e in range(2):
            hx, hy, hz = hs[e, z], hs[e + 2, z], hs[e + 4, z]
            ex, ey, ez = y[e, z], y[e + 2, z], y[e + 4, z]
            cx = hz - jnp.where(first, -ex, pltpu.roll(hz, 1, 1)) - (hy - hs[e + 2, z - 1])
            cy = hx - hs[e, z - 1] - (hz - prev_x(hz))
            cz = hy - prev_x(hy) - (hx - jnp.where(first, ez, pltpu.roll(hx, 1, 1)))
            for c, (cur, old) in enumerate(((cx, ex), (cy, ey), (cz, ez))):
                new = cur - 4.0 * old
                if inv != 1.0:
                    new = new * inv
                bn[e + 2 * c, z] = new + own * b[e + 2 * c, z]
        if want_y:
            smooth(bn, yn, m, 0, z)


def all_smooth(b, y, m):
    def layer(z, _):
        smooth(b, y, m, 0, z)
        return 0

    lax.fori_loop(1, EZ - 1, layer, 0)


def keep(src, out):
    def field(f, _):
        out[f] = src[f, REACH : REACH + NZL, 8 : 8 + CX, :]
        return 0

    lax.fori_loop(0, NF, field, 0)


def first_steps(p, r, k, kx, xa, xb, za, zb, b1, b2, b3w, to_a, to_b, b1_far, b2_far, m, ba, bb, ya, yb, hs, far, sem):
    for f in range(NF):
        clear_sides(ba.at[f])
        own_layers(ba.at[f], REACH, r.at[p * NF + f], xa, xb, p * NF + f)
    clear_far(ya)
    if p == 0:
        clear_sides(kx)
        own_layers(kx, REACH, k, xa, xb, 2 * NF)

    def take(above, below):
        take_messages(ba, ya, kx if p == 0 else None, REACH, above, below)

    either(odd("gz"), take, za, zb)
    if p == 0:

        def layer(z, _):
            m[0, z], m[1, z] = weight_of(kx[z])
            return 0

        lax.fori_loop(1, EZ - 1, layer, 0)
    all_smooth(ba, ya, m)
    apply_k(ba, ya, bb, yb, hs, m, 1, EZ - 1, SHIFTS[0], True)
    keep(bb, b1)
    copies = start_all([(b1, b1_far)], sem)
    apply_k(bb, yb, ba, ya, hs, m, 2, EZ - 2, SHIFTS[1], True)
    keep(ba, b2)
    copies += start_all([(b2, b2_far)], sem, 1)
    apply_k(ba, ya, bb, yb, hs, m, 3, EZ - 3, SHIFTS[2], False)
    for f in range(NF):
        b3w[f] = bb[f, REACH : REACH + NZL]
    far_fields(bb, REACH, lambda z: (m[0, REACH + z], m[1, REACH + z]), far)
    either(odd("gz"), lambda up, down: fill_messages(bb, REACH, far, None, 0, up, down), to_a, to_b)
    wait_all(copies)


def first_half_0(r, k, xa, xb, za, zb, b1, b2, b3w, to_a, to_b, b1_far, b2_far, m, kx, *space):
    first_steps(0, r, k, kx, xa, xb, za, zb, b1, b2, b3w, to_a, to_b, b1_far, b2_far, m, *space)


def first_half_1(r, m, xa, xb, za, zb, b1, b2, b3w, to_a, to_b, b1_far, b2_far, *space):
    first_steps(1, r, None, None, xa, xb, za, zb, b1, b2, b3w, to_a, to_b, b1_far, b2_far, m, *space)


PAIRS = [(i, j) for i in range(7) for j in range(i, 7)]
LOW = [pair for pair in PAIRS if pair[1] <= REACH]
HIGH = [pair for pair in PAIRS if pair[1] > REACH]
SLOT = {}
for _pair in LOW + HIGH:
    SLOT[_pair] = sum(1 if a == b else 2 for a, b in SLOT)


def gram(read, pairs, out):
    used = sorted({i for pair in pairs for i in pair})
    count = sum(1 if i == j else 2 for i, j in pairs)

    def block(step, acc):
        c, z = step // NZL, step % NZL
        acc = list(acc)
        for xb in range(CX // 8):
            vec = {i: (read(i, 2 * c, z, xb), read(i, 2 * c + 1, z, xb)) for i in used}
            at = 0
            for i, j in pairs:
                (ar, ai), (br, bi) = vec[i], vec[j]
                acc[at] = acc[at] + (ar * br + ai * bi)
                at += 1
                if i != j:
                    acc[at] = acc[at] + (ar * bi - ai * br)
                    at += 1
        return tuple(acc)

    acc = lax.fori_loop(0, 3 * NZL, block, (jnp.zeros((8, NY), f32),) * count)
    at = 0
    for i, j in pairs:
        for part in range(1 if i == j else 2):
            row = SLOT[i, j] + part
            out[row : row + 1, :] = jnp.sum(acc[at], axis=0, keepdims=True)
            at += 1


def low_gram(b0, b1_0, b2_0, b3w_0, b1_1, b2_1, b3w_1, part_0, part_1):
    for p, (b1, b2, b3w, part) in enumerate(((b1_0, b2_0, b3w_0, part_0), (b1_1, b2_1, b3w_1, part_1))):
        part[...] = jnp.zeros((64, NY), f32)
        gram(reader(p, b0, b1, b2, b3w), LOW, part)


def reader(p, b0, b1, b2, b3w, *slabs):
    def read(i, f, z, xb):
        if i == 0:
            return b0[p * NF + f, z, pl.ds(8 * xb, 8), :]
        if i < 3:
            return (b1, b2)[i - 1][f, z, pl.ds(8 * xb, 8), :]
        if i == 3:
            return b3w[f, z, pl.ds(8 + 8 * xb, 8), :]
        return slabs[i - 4][f, REACH + z, pl.ds(8 + 8 * xb, 8), :]

    return read


def second_steps(p, b0, b1, b2, b3w, m, za, zb, part, b3_far, b4_far, b5_far, total, ba, bb, bc, bd, ya, yb, hs, sem):
    own = pl.ds(REACH, NZL)
    mid = pl.ds(8, CX)
    copies = start_all([(b3w.at[:, :, mid, :], b3_far)], sem)
    for f in range(NF):
        clear_sides(ba.at[f])
        ba[f, REACH : REACH + NZL] = b3w[f]
    clear_far(ya)
    either(odd("gz"), lambda above, below: take_messages(ba, ya, None, 0, above, below), za, zb)
    all_smooth(ba, ya, m)
    apply_k(ba, ya, bb, yb, hs, m, 1, EZ - 1, SHIFTS[3], True)
    copies += start_all([(bb.at[:, own, mid, :], b4_far)], sem, 1)
    apply_k(bb, yb, bc, ya, hs, m, 2, EZ - 2, SHIFTS[4], True)
    copies += start_all([(bc.at[:, own, mid, :], b5_far)], sem, 2)
    apply_k(bc, ya, bd, yb, hs, m, 3, EZ - 3, SHIFTS[5], False)
    total[...] = part[...]
    gram(reader(p, b0, b1, b2, b3w, bb, bc, bd), HIGH, total)
    wait_all(copies)


def second_half_0(b0, b1, b2, b3w, m, za, zb, part, b3_far, b4_far, b5_far, total, *space):
    second_steps(0, b0, b1, b2, b3w, m, za, zb, part, b3_far, b4_far, b5_far, total, *space)


def second_half_1(b0, b1, b2, b3w, m, za, zb, part, other, cells, b3_far, b4_far, b5_far, send, total, *space):
    second_steps(1, b0, b1, b2, b3w, m, za, zb, part, b3_far, b4_far, b5_far, total, *space)
    both = jnp.concatenate([other[...], total[...]], axis=0)
    sums = jnp.sum(jnp.transpose(both), axis=0, keepdims=True)
    send[...] = jnp.broadcast_to(jnp.concatenate([sums, cells[...]], axis=1), (128, 2 * NY))


def cadd(a, b):
    return (a[0] + b[0], a[1] + b[1])


def csub(a, b):
    return (a[0] - b[0], a[1] - b[1])


def cmul(a, b):
    return (a[0] * b[0] - a[1] * b[1], a[0] * b[1] + a[1] * b[0])


def cconj_mul(a, b):
    return (a[0] * b[0] + a[1] * b[1], a[0] * b[1] - a[1] * b[0])


def cdiv(numer, denom, floor):
    size = jnp.maximum(denom[0] * denom[0] + denom[1] * denom[1], floor)
    return (
        (numer[0] * denom[0] + numer[1] * denom[1]) / size,
        (numer[1] * denom[0] - numer[0] * denom[1]) / size,
    )


def tree(terms):
    terms = list(terms)
    while len(terms) > 1:
        terms = [cadd(*terms[i : i + 2]) if i + 1 < len(terms) else terms[i] for i in range(0, len(terms), 2)]
    return terms[0]


def combine(a, scale, b):
    out = []
    for i in range(max(len(a), len(b))):
        if i >= len(b):
            out.append(a[i])
        elif i >= len(a):
            out.append(cmul(scale, b[i]))
        else:
            out.append(cadd(a[i], cmul(scale, b[i])))
    return out


def times_k(a):
    zero = (jnp.zeros_like(a[0][0]),) * 2
    out = [(SHIFTS[i] * v[0], SHIFTS[i] * v[1]) for i, v in enumerate(a)] + [zero]
    return [
        cadd(out[i], (SCALE * a[i - 1][0], SCALE * a[i - 1][1])) if i > 0 else out[i]
        for i in range(len(out))
    ]


def coefficients(entry):
    def g(i, j):
        if i > j:
            re, im = g(j, i)
            return (re, -im)
        if i == j:
            return (entry(SLOT[i, j]), 0.0)
        return (entry(SLOT[i, j]), entry(SLOT[i, j] + 1))

    def times_g(b, rows):
        return [tree([cmul(g(i, j), b[j]) for j in range(len(b))]) for i in range(rows)]

    def dot(a, gb):
        return tree([cconj_mul(a[i], gb[i]) for i in range(len(a))])

    def shadow(b):
        return tree([cmul(g(0, j), b[j]) for j in range(len(b))])

    one = jnp.ones_like(entry(0))
    residual = [(one, jnp.zeros_like(one))]
    direction = residual
    solution = []
    for step in range(ITERS):
        rho = shadow(residual)
        if step == 0:
            floor = 1e-06 * rho[0] * rho[0]
        else:
            beta = cmul(cdiv(rho, rho_prev, floor), cdiv(alpha, omega, 0.0001))
            minus = (-omega[0], -omega[1])
            direction = combine(residual, beta, combine(direction, minus, image))
        image = times_k(direction)
        alpha = cdiv(rho, shadow(image), floor)
        middle = combine(residual, (-alpha[0], -alpha[1]), image)
        bent = times_k(middle)
        seen = times_g(bent, len(bent))
        norm = dot(bent, seen)[0] + 1e-06
        against = dot(middle, seen)
        omega = (against[0] / norm, -against[1] / norm)
        solution = combine(combine(solution, alpha, direction), omega, middle)
        residual = combine(middle, (-omega[0], -omega[1]), bent)
        rho_prev = rho
    return solution


def surface_power(x, rows):
    def e(p, c, z):
        f = p * NF + 2 * c
        return (x[f, z, rows, :], x[f + 1, z, rows, :])

    ex, ey, hx, hy = [], [], [], []
    for p in range(2):
        ex0, ey0 = e(p, 0, 0), e(p, 1, 0)
        ex1, ey1 = e(p, 0, 1), e(p, 1, 1)
        ex.append(ex0)
        ey.append(ey0)
        one_x, one_y = (1.0, 0.0) if p == 0 else (0.0, 1.0)
        hx.append((one_x - 2.0 * (ey1[0] - ey0[0]), -2.0 * (ey1[1] - ey0[1])))
        hy.append((one_y + 2.0 * (ex1[0] - ex0[0]), 2.0 * (ex1[1] - ex0[1])))
    det = csub(cmul(hx[0], hy[1]), cmul(hx[1], hy[0]))
    zxx = csub(cmul(ex[0], hy[1]), cmul(ex[1], hy[0]))
    zxy = csub(cmul(ex[1], hx[0]), cmul(ex[0], hx[1]))
    zyx = csub(cmul(ey[0], hy[1]), cmul(ey[1], hy[0]))
    zyy = csub(cmul(ey[1], hx[0]), cmul(ey[0], hx[1]))
    size = det[0] * det[0] + det[1] * det[1]
    inv = 1.0 / jnp.maximum(size, 0.25)
    scale = size * inv * inv
    cross = cadd(cconj_mul(zxx, zxy), cconj_mul(zyx, zyy))
    first = zxx[0] * zxx[0] + zxx[1] * zxx[1] + (zyx[0] * zyx[0] + zyx[1] * zyx[1])
    second = zxy[0] * zxy[0] + zxy[1] * zxy[1] + (zyy[0] * zyy[0] + zyy[1] * zyy[1])
    return [scale * first, scale * second, scale * cross[0], scale * cross[1]]


def finish(got, k, *rest):
    fars, (x_far, send, x, surface, picked, sem) = rest[:11], rest[11:]
    sub = lax.broadcasted_iota(jnp.int32, (8, NY), 0)
    row = jnp.broadcast_to(jnp.sum(got[:, 0:NY], axis=0, keepdims=True), (8, NY))
    table = jnp.where(sub == 0, row, pltpu.roll(row, 64, 1))
    cache = {}

    def entry(slot):
        if slot not in cache:
            cache[slot] = jnp.broadcast_to(table[:, slot : slot + 1], (8, NY))
        return cache[slot]

    coefs = coefficients(entry)
    scal = [[tuple(jnp.broadcast_to(half[p : p + 1, :], (8, NY)) for half in c) for c in coefs] for p in range(2)]

    mine = pltpu.roll(got[:, NY : 2 * NY], lax.rem(NY - 32 * lax.axis_index("gx"), NY), 1).astype(jnp.int32)
    group = lax.broadcasted_iota(jnp.int32, (32, NY), 1) // 32
    cells = mine[0:32, :]
    for e in range(1, 4):
        cells = jnp.where(group == e, pltpu.roll(mine[32 * e : 32 * e + 32, :], 32 * e, 1), cells)
    col = cells % NY
    line = cells // NY
    cols = [col[8 * i : 8 * i + 8, :] for i in range(4)]
    lines = [line[8 * i : 8 * i + 8, :] for i in range(4)]

    def layer(p, z):
        for xb in range(CX // 8):
            rows = pl.ds(8 * xb, 8)
            kz = k[z, rows, :]
            inv = 1.0 / (16.0 + kz * kz)
            weight = (4.0 * inv, -kz * inv)
            for f in range(p * NF, p * NF + NF, 2):
                terms = [cmul(scal[p][i], (basis(i, f, z, rows), basis(i, f + 1, z, rows))) for i in range(6)]
                y = cmul(weight, tree(terms))
                x[f, z, rows, :] = y[0]
                x[f + 1, z, rows, :] = y[1]

    def basis(i, f, z, rows):
        if i == 0:
            return fars[0][f, z, rows, :]
        return fars[5 * (f // NF) + i][f % NF, z, rows, :]

    outs = []

    def leave(p, z, count):
        part = pl.ds(p * NF, NF), pl.ds(z, count)
        outs.extend(start_all([(x.at[part], x_far.at[part])], sem, len(outs)))

    for p in range(2):
        for z in range(2):
            layer(p, z)
        leave(p, 0, 2)
    for xb in range(CX // 8):
        for v, value in enumerate(surface_power(x, pl.ds(8 * xb, 8))):
            surface[v * CX + 8 * xb : v * CX + 8 * xb + 8, :] = value
    for i in range(4):
        acc = [jnp.zeros((8, NY), f32)] * 4
        for r in range(CX):
            for v in range(4):
                src = jnp.broadcast_to(surface[v * CX + r : v * CX + r + 1, :], (8, NY))
                hit = jnp.take_along_axis(src, cols[i], axis=1, mode="promise_in_bounds")
                acc[v] = jnp.where(lines[i] == r, hit, acc[v])
        for v in range(4):
            picked[v * 32 + 8 * i : v * 32 + 8 * i + 8, :] = acc[v]
        p, z = i // 2, 2 + i % 2
        layer(p, z)
        leave(p, z, 1)
    for e in range(4):
        out = None
        for v in range(4):
            part = picked[v * 32 : v * 32 + 32, :]
            if v != e:
                part = pltpu.roll(part, (32 * (v - e)) % NY, 1)
            out = part if out is None else jnp.where(group == v, part, out)
        send[32 * e : 32 * e + 32, :] = out
    wait_all(outs)


def hazard_rows(got, power, out):
    block = jnp.concatenate([got[0:8, :], jnp.zeros((NY - 8, NY), f32)], axis=0)
    turned = jnp.transpose(block)
    for j in range(4):
        for qb in range(4):
            total = None
            for v in range(4):
                first = v * 32 + 8 * qb
                column = jnp.broadcast_to(turned[first : first + 8, j : j + 1], (8, power.shape[1]))
                term = column * power[4 * j + v : 4 * j + v + 1, :]
                total = term if total is None else total + term
            row = 32 * j + 8 * qb
            out[row : row + 8, :] = total


def partners(count):
    first = [(i, i ^ 1) for i in range(count)]
    second = [(i, ((i + 1) ^ 1) - 1) for i in range(1, count - 1)]
    return first, second


def exchange(to_a, to_b, axis):
    first, second = partners(lax.axis_size(axis))
    return lax.ppermute(to_a, axis, first), lax.ppermute(to_b, axis, second)


def per_device(right_side, conductance, owned_cells, spectra, scenario_tile):
    block = (NF, NZL, CX, NY)
    wide = (NF, NZL, WX, NY)
    whole = (2 * NF, NZL, CX, NY)
    dma = pltpu.SemaphoreType.DMA
    space = pltpu.VMEM((NF, EZ, WX, NY), f32)
    r_far = right_side.reshape(whole)
    side = (((2 * NF + 1) * NZL * SIDE, NY), VM)
    scen = spectra.shape[0]
    rims = [
        pltpu.VMEM((2 * NF, NZL, 16, NY), f32),
        pltpu.VMEM((NZL, 16, NY), f32),
        pltpu.VMEM((4, scen), f32),
        pltpu.VMEM((1, scen), jnp.int32),
        dma((6,)),
    ]
    to_a, to_b, power = call(
        pack_x, [HBM] * 4, [side] * 2 + [((16, scen), VM)], rims, limit=FIRST_LIMIT
    )(r_far, conductance, spectra.T, scenario_tile.reshape(1, scen))
    r, k = r_far, conductance
    near = exchange(to_a, to_b, "gx")
    deep = [((rows_of(REACH, with_k), NY), VM) for with_k in (True, False)]
    *packed, cells = call(
        pack_z,
        [VM] * 5,
        [deep[0]] * 2 + [deep[1]] * 2 + [((1, NY), VM)],
        [
            pltpu.VMEM((2 * NF, NZL, WX, NY), f32),
            pltpu.VMEM((NZL, WX, NY), f32),
            pltpu.VMEM((2, 8, WX, NY), f32),
        ],
        moved=1 << 22,
    )(r, k, *near, owned_cells[0])
    halo_0 = exchange(*packed[0:2], "gz")
    halo_1 = exchange(*packed[2:4], "gz")
    back = ((rows_of(0, False), NY), VM)
    far = pltpu.VMEM((8, WX, NY), f32)
    firsts = [(block, VM), (block, VM), (wide, VM), back, back, (block, HBM), (block, HBM)]
    cost = {"flops": 1 << 24, "moved": 1 << 23}
    *b_0, to_a, to_b, b1_0, b2_0, m = call(
        first_half_0,
        [VM] * 6,
        firsts + [((2, EZ, WX, NY), VM)],
        [pltpu.VMEM((EZ, WX, NY), f32)] + [space] * 5 + [far, dma((2,))],
        **cost,
    )(r, k, *near, *halo_0)
    halo_0 = exchange(to_a, to_b, "gz")
    *b_1, to_a, to_b, b1_1, b2_1 = call(
        first_half_1, [VM] * 6, firsts, [space] * 5 + [far, dma((2,))], **cost
    )(r, m, *near, *halo_1)
    halo_1 = exchange(to_a, to_b, "gz")
    table = ((64, NY), VM)
    part_0, part_1 = call(low_gram, [VM] * 7, [table] * 2, **cost)(r, *b_0, *b_1)
    seconds = [(block, HBM)] * 3
    spaces = [space] * 7 + [dma((3,))]
    *high_0, total = call(
        second_half_0, [VM] * 8, seconds + [table], spaces, **cost
    )(r, *b_0, m, *halo_0, part_0)
    *high_1, send = call(
        second_half_1,
        [VM] * 10,
        seconds + [((128, 2 * NY), VM)],
        [pltpu.VMEM((64, NY), f32)] + spaces,
        **cost,
    )(r, *b_1, m, *halo_1, part_1, total, cells)
    held = (send, conductance, r_far, b1_0, b2_0, *high_0, b1_1, b2_1, *high_1)
    send, *fars = lax.optimization_barrier(held)
    got = lax.all_to_all(send, ("gz", "gx"), 0, 0, tiled=True)
    x, send = call(
        finish,
        [VM] * 13,
        [(whole, HBM), ((128, NY), VM)],
        [
            pltpu.VMEM(whole, f32),
            pltpu.VMEM((4 * CX, NY), f32),
            pltpu.VMEM((4 * CX, NY), f32),
            dma((6,)),
        ],
    )(got, *fars)
    got = lax.all_to_all(send, ("gz", "gx"), 0, 0, tiled=True)
    (hazard,) = call(hazard_rows, [VM] * 2, [((128, scen), VM)])(got, power)
    return x.reshape(right_side.shape), hazard


def solution(mesh):
    return jax.shard_map(
        per_device,
        mesh=mesh,
        in_specs=(
            P(None, None, None, "gz", "gx", None),
            P("gz", "gx", None),
            P(("gz", "gx"), None, None),
            P(),
            P(),
        ),
        out_specs=(P(None, None, None, "gz", "gx", None), P(("gz", "gx"), None)),
        check_vma=False,
    )
```

```python
import jax
import jax.numpy as jnp
from jax import lax
from jax.experimental import pallas as pl
from jax.experimental.pallas import tpu as pltpu
from jax.sharding import PartitionSpec as P

SHIFTS = (1.8, 0.6, 1.8, 0.6, 1.8, 0.6)
SCALE = 1.0
ITERS = 3
REACH = 3
SIDE = 2 * REACH
NF = 6
CX, NZL, NY = 32, 4, 128
WX = 48
EZ = NZL + 2 * REACH
f32 = jnp.float32
VM = pl.BlockSpec(memory_space=pltpu.VMEM)
LIMIT = 14 * 1024 * 1024
FIRST_LIMIT = 14 * 1024 * 1024


HBM = pl.BlockSpec(memory_space=pltpu.HBM)


def call(body, ins, outs, scratch=(), flops=0, moved=0, limit=LIMIT):
    return pl.pallas_call(
        body,
        out_shape=[jax.ShapeDtypeStruct(shape, f32) for shape, _ in outs],
        in_specs=ins,
        out_specs=[spec for _, spec in outs],
        scratch_shapes=list(scratch),
        compiler_params=pltpu.CompilerParams(vmem_limit_bytes=limit),
        cost_estimate=pl.CostEstimate(flops=flops, bytes_accessed=moved, transcendentals=0),
    )


def odd(axis):
    return lax.rem(lax.axis_index(axis), 2) == 1


def either(flag, body, first, second):
    @pl.when(jnp.logical_not(flag))
    def _():
        body(first, second)

    @pl.when(flag)
    def _():
        body(second, first)


def start_all(pairs, sem, first=0):
    copies = [pltpu.make_async_copy(src, dst, sem.at[first + i]) for i, (src, dst) in enumerate(pairs)]
    for copy in copies:
        copy.start()
    return copies


def wait_all(copies):
    for copy in copies:
        copy.wait()


def pack_x(r, k, spectra, scenario, to_a, to_b, power, rim, rim_k, spec, scen, sem):
    pairs = []
    for i in range(2):
        src = pl.ds(i * (CX - 8), 8)
        pairs.append((r.at[:, :, src, :], rim.at[:, :, pl.ds(8 * i, 8), :]))
        pairs.append((k.at[:, src, :], rim_k.at[:, pl.ds(8 * i, 8), :]))
    pairs += [(spectra, spec), (scenario, scen)]
    wait_all(start_all(pairs, sem))

    def fill(up, down):
        for f in range(2 * NF + 1):
            for z in range(NZL):
                row = (f * NZL + z) * SIDE
                src = rim_k.at[z] if f == 2 * NF else rim.at[f, z]
                up[row : row + SIDE, :] = src[16 - SIDE : 16, :]
                down[row : row + SIDE, :] = src[0:SIDE, :]

    either(odd("gx"), fill, to_a, to_b)
    xr, xi, yr, yi = [spec[i : i + 1, :] for i in range(4)]
    base = [
        xr * xr + xi * xi,
        yr * yr + yi * yi,
        2.0 * (xr * yr + xi * yi),
        2.0 * (xi * yr - xr * yi),
    ]
    for j in range(4):
        weight = jnp.where(scen[...] == j, 1.0, 0.25)
        for v in range(4):
            power[4 * j + v : 4 * j + v + 1, :] = weight * base[v]


def sides(from_a, from_b, near):
    a, b = from_a[near : near + SIDE, :], from_b[near : near + SIDE, :]
    flag = odd("gx")
    return jnp.where(flag, a, b), jnp.where(flag, b, a)


def spans(margin):
    low, high = margin + REACH, CX - 1 + margin
    below = ((1 - low, high + 3), (2 - low, high + 3), (3 - low, high + 2))
    above = ((-low, high + 2), (-low, high + 1), (-low, high))
    return below, above


def layout(span, with_k):
    near, row = {}, 0
    for i in range(REACH - 1):
        for f in range(NF):
            near[i, f] = row
            row += span[i][1] - span[i][0] + 1
    far = []
    for _ in range(4):
        far.append(row)
        row += span[-1][1] - span[-1][0] + 1
    k = []
    for i in range(REACH - 1 if with_k else 0):
        k.append(row)
        row += span[i][1] - span[i][0] + 1
    return near, far, k, row


def rows_of(margin, with_k):
    return max(layout(span, with_k)[3] for span in spans(margin))


def cut(span):
    return slice(8 + span[0], 9 + span[1]), span[1] - span[0] + 1


def far_fields(b, first, weight, far):
    _, last = lanes()

    def y(z, c):
        mr, mi = weight(z)
        re, im = b[2 * c, first + z], b[2 * c + 1, first + z]
        return mr * re - mi * im, mr * im + mi * re

    ex, ey, ez = [y(NZL - REACH, c) for c in range(3)]
    for q in range(2):
        far[q] = ex[q] + (next_x(ez[q]) - ez[q])
        far[2 + q] = ey[q] + (next_y(ez[q], last) - ez[q])
    for c in range(2):
        far[4 + 2 * c], far[5 + 2 * c] = y(REACH - 1, c)


def fill_messages(b, first, far, k, margin, up, down):
    for side, (out, span) in enumerate(zip((up, down), spans(margin))):
        near, far_rows, k_rows, _ = layout(span, k is not None)
        for i in range(REACH - 1):
            z = first + (NZL - 1 - i if side == 0 else i)
            cols, n = cut(span[i])
            for f in range(NF):
                out[near[i, f] : near[i, f] + n, :] = b[f, z, cols, :]
            if k is not None:
                out[k_rows[i] : k_rows[i] + n, :] = k[z, cols, :]
        cols, n = cut(span[-1])
        for j, row in enumerate(far_rows):
            out[row : row + n, :] = far[4 * side + j, cols, :]


def take_messages(b, y, k, margin, above, below):
    for side, (src, span) in enumerate(zip((below, above), spans(margin))):
        near, far_rows, k_rows, _ = layout(span, k is not None)
        for i in range(REACH - 1):
            z = REACH - 1 - i if side == 0 else REACH + NZL + i
            cols, n = cut(span[i])
            for f in range(NF):
                b[f, z, cols, :] = src[near[i, f] : near[i, f] + n, :]
            if k is not None:
                k[z, cols, :] = src[k_rows[i] : k_rows[i] + n, :]
        cols, n = cut(span[-1])
        z = 0 if side == 0 else EZ - 1
        for j, row in enumerate(far_rows):
            y[j, z, cols, :] = src[row : row + n, :]


def clear_sides(ref):
    zero = jnp.zeros((EZ, 8, NY), f32)
    ref[:, 0:8, :] = zero
    ref[:, WX - 8 : WX, :] = zero


def clear_far(y):
    for f in range(NF):
        for z in (0, EZ - 1):
            if f < 4:
                y[f, z, 0:8, :] = jnp.zeros((8, NY), f32)
                y[f, z, WX - 8 : WX, :] = jnp.zeros((8, NY), f32)
            else:
                y[f, z] = jnp.zeros((WX, NY), f32)


def own_layers(dst, first, src, xa, xb, near):
    for z in range(NZL):
        left, right = sides(xa, xb, (near * NZL + z) * SIDE)
        dst[first + z, 8 - SIDE : 8, :] = left
        dst[first + z, 8 : 8 + CX, :] = src[z]
        dst[first + z, 8 + CX : 8 + CX + SIDE, :] = right


def weight_of(kz):
    inv = jnp.where(kz > 0.0, 1.0, 0.0) / (16.0 + kz * kz)
    return 4.0 * inv, -kz * inv


def pack_z(r, k, xa, xb, owned, a_0, b_0, a_1, b_1, cells, b, kx, far):
    for f in range(2 * NF + 1):
        dst = kx if f == 2 * NF else b.at[f]
        zero = jnp.zeros((NZL, 8, NY), f32)
        dst[:, 0:8, :] = zero
        dst[:, WX - 8 : WX, :] = zero
        own_layers(dst, 0, k if f == 2 * NF else r.at[f], xa, xb, f)
    weights = {z: weight_of(kx[z]) for z in (NZL - REACH, REACH - 1)}
    for p in range(2):
        far_fields(b.at[pl.ds(p * NF, NF)], 0, lambda z: weights[z], far.at[p])

    def fill(first, second):
        for p in range(2):
            own = b.at[pl.ds(p * NF, NF)]
            fill_messages(own, 0, far.at[p], kx if p == 0 else None, REACH, first[p], second[p])

    either(odd("gz"), fill, (a_0, a_1), (b_0, b_1))
    cells[...] = jnp.concatenate([owned[j : j + 1, :] for j in range(4)], axis=1).astype(f32)


def lanes():
    lane = lax.broadcasted_iota(jnp.int32, (WX, NY), 1)
    return lane == 0, lane == NY - 1


def next_y(a, last):
    return jnp.where(last, 0.0, pltpu.roll(a, NY - 1, 1))


def next_x(a):
    return pltpu.roll(a, WX - 1, 0)


def prev_x(a):
    return pltpu.roll(a, 1, 0)


def smooth(b, y, m, base, z):
    mr, mi = m[0, z], m[1, z]
    for c in range(3):
        re, im = b[base + 2 * c, z], b[base + 2 * c + 1, z]
        y[base + 2 * c, z] = mr * re - mi * im
        y[base + 2 * c + 1, z] = mr * im + mi * re


def apply_k(b, y, bn, yn, hs, m, lo, hi, shift, want_y):
    first, last = lanes()
    own = (1.0 - shift) / SCALE
    inv = 1.0 / SCALE
    for z in range(lo - 1, hi):
        for e in range(2):
            ex, ey, ez = y[e, z], y[e + 2, z], y[e + 4, z]
            hs[e, z] = next_y(ez, last) - ez - (y[e + 2, z + 1] - ey)
            hs[e + 2, z] = y[e, z + 1] - ex - (next_x(ez) - ez)
            hs[e + 4, z] = next_x(ey) - ey - (next_y(ex, last) - ex)
    for z in range(lo, hi):
        for e in range(2):
            hx, hy, hz = hs[e, z], hs[e + 2, z], hs[e + 4, z]
            ex, ey, ez = y[e, z], y[e + 2, z], y[e + 4, z]
            cx = hz - jnp.where(first, -ex, pltpu.roll(hz, 1, 1)) - (hy - hs[e + 2, z - 1])
            cy = hx - hs[e, z - 1] - (hz - prev_x(hz))
            cz = hy - prev_x(hy) - (hx - jnp.where(first, ez, pltpu.roll(hx, 1, 1)))
            for c, (cur, old) in enumerate(((cx, ex), (cy, ey), (cz, ez))):
                new = cur - 4.0 * old
                if inv != 1.0:
                    new = new * inv
                bn[e + 2 * c, z] = new + own * b[e + 2 * c, z]
        if want_y:
            smooth(bn, yn, m, 0, z)


def all_smooth(b, y, m):
    def layer(z, _):
        smooth(b, y, m, 0, z)
        return 0

    lax.fori_loop(1, EZ - 1, layer, 0)


def keep(src, out):
    def field(f, _):
        out[f] = src[f, REACH : REACH + NZL, 8 : 8 + CX, :]
        return 0

    lax.fori_loop(0, NF, field, 0)


def first_steps(p, r, k, kx, xa, xb, za, zb, b1, b2, b3w, to_a, to_b, b1_far, b2_far, m, ba, bb, ya, yb, hs, far, sem):
    for f in range(NF):
        clear_sides(ba.at[f])
        own_layers(ba.at[f], REACH, r.at[p * NF + f], xa, xb, p * NF + f)
    clear_far(ya)
    if p == 0:
        clear_sides(kx)
        own_layers(kx, REACH, k, xa, xb, 2 * NF)

    def take(above, below):
        take_messages(ba, ya, kx if p == 0 else None, REACH, above, below)

    either(odd("gz"), take, za, zb)
    if p == 0:

        def layer(z, _):
            m[0, z], m[1, z] = weight_of(kx[z])
            return 0

        lax.fori_loop(1, EZ - 1, layer, 0)
    all_smooth(ba, ya, m)
    apply_k(ba, ya, bb, yb, hs, m, 1, EZ - 1, SHIFTS[0], True)
    keep(bb, b1)
    copies = start_all([(b1, b1_far)], sem)
    apply_k(bb, yb, ba, ya, hs, m, 2, EZ - 2, SHIFTS[1], True)
    keep(ba, b2)
    copies += start_all([(b2, b2_far)], sem, 1)
    apply_k(ba, ya, bb, yb, hs, m, 3, EZ - 3, SHIFTS[2], False)
    for f in range(NF):
        b3w[f] = bb[f, REACH : REACH + NZL]
    far_fields(bb, REACH, lambda z: (m[0, REACH + z], m[1, REACH + z]), far)
    either(odd("gz"), lambda up, down: fill_messages(bb, REACH, far, None, 0, up, down), to_a, to_b)
    wait_all(copies)


def first_half_0(r, k, xa, xb, za, zb, b1, b2, b3w, to_a, to_b, b1_far, b2_far, m, kx, *space):
    first_steps(0, r, k, kx, xa, xb, za, zb, b1, b2, b3w, to_a, to_b, b1_far, b2_far, m, *space)


def first_half_1(r, m, xa, xb, za, zb, b1, b2, b3w, to_a, to_b, b1_far, b2_far, *space):
    first_steps(1, r, None, None, xa, xb, za, zb, b1, b2, b3w, to_a, to_b, b1_far, b2_far, m, *space)


PAIRS = [(i, j) for i in range(7) for j in range(i, 7)]
LOW = [pair for pair in PAIRS if pair[1] <= REACH]
HIGH = [pair for pair in PAIRS if pair[1] > REACH]
SLOT = {}
for _pair in LOW + HIGH:
    SLOT[_pair] = sum(1 if a == b else 2 for a, b in SLOT)


def gram(read, pairs, out):
    used = sorted({i for pair in pairs for i in pair})
    count = sum(1 if i == j else 2 for i, j in pairs)

    def block(step, acc):
        c, z = step // NZL, step % NZL
        acc = list(acc)
        for xb in range(CX // 8):
            vec = {i: (read(i, 2 * c, z, xb), read(i, 2 * c + 1, z, xb)) for i in used}
            at = 0
            for i, j in pairs:
                (ar, ai), (br, bi) = vec[i], vec[j]
                acc[at] = acc[at] + (ar * br + ai * bi)
                at += 1
                if i != j:
                    acc[at] = acc[at] + (ar * bi - ai * br)
                    at += 1
        return tuple(acc)

    acc = lax.fori_loop(0, 3 * NZL, block, (jnp.zeros((8, NY), f32),) * count)
    at = 0
    for i, j in pairs:
        for part in range(1 if i == j else 2):
            row = SLOT[i, j] + part
            out[row : row + 1, :] = jnp.sum(acc[at], axis=0, keepdims=True)
            at += 1


def low_gram(b0, b1_0, b2_0, b3w_0, b1_1, b2_1, b3w_1, part_0, part_1):
    for p, (b1, b2, b3w, part) in enumerate(((b1_0, b2_0, b3w_0, part_0), (b1_1, b2_1, b3w_1, part_1))):
        part[...] = jnp.zeros((64, NY), f32)
        gram(reader(p, b0, b1, b2, b3w), LOW, part)


def reader(p, b0, b1, b2, b3w, *slabs):
    def read(i, f, z, xb):
        if i == 0:
            return b0[p * NF + f, z, pl.ds(8 * xb, 8), :]
        if i < 3:
            return (b1, b2)[i - 1][f, z, pl.ds(8 * xb, 8), :]
        if i == 3:
            return b3w[f, z, pl.ds(8 + 8 * xb, 8), :]
        return slabs[i - 4][f, REACH + z, pl.ds(8 + 8 * xb, 8), :]

    return read


def second_steps(p, b0, b1, b2, b3w, m, za, zb, part, b3_far, b4_far, b5_far, total, ba, bb, bc, bd, ya, yb, hs, sem):
    own = pl.ds(REACH, NZL)
    mid = pl.ds(8, CX)
    copies = start_all([(b3w.at[:, :, mid, :], b3_far)], sem)
    for f in range(NF):
        clear_sides(ba.at[f])
        ba[f, REACH : REACH + NZL] = b3w[f]
    clear_far(ya)
    either(odd("gz"), lambda above, below: take_messages(ba, ya, None, 0, above, below), za, zb)
    all_smooth(ba, ya, m)
    apply_k(ba, ya, bb, yb, hs, m, 1, EZ - 1, SHIFTS[3], True)
    copies += start_all([(bb.at[:, own, mid, :], b4_far)], sem, 1)
    apply_k(bb, yb, bc, ya, hs, m, 2, EZ - 2, SHIFTS[4], True)
    copies += start_all([(bc.at[:, own, mid, :], b5_far)], sem, 2)
    apply_k(bc, ya, bd, yb, hs, m, 3, EZ - 3, SHIFTS[5], False)
    total[...] = part[...]
    gram(reader(p, b0, b1, b2, b3w, bb, bc, bd), HIGH, total)
    wait_all(copies)


def second_half_0(b0, b1, b2, b3w, m, za, zb, part, b3_far, b4_far, b5_far, total, *space):
    second_steps(0, b0, b1, b2, b3w, m, za, zb, part, b3_far, b4_far, b5_far, total, *space)


def second_half_1(b0, b1, b2, b3w, m, za, zb, part, other, cells, b3_far, b4_far, b5_far, send, total, *space):
    second_steps(1, b0, b1, b2, b3w, m, za, zb, part, b3_far, b4_far, b5_far, total, *space)
    both = jnp.concatenate([other[...], total[...]], axis=0)
    sums = jnp.sum(jnp.transpose(both), axis=0, keepdims=True)
    send[...] = jnp.broadcast_to(jnp.concatenate([sums, cells[...]], axis=1), (128, 2 * NY))


def cadd(a, b):
    return (a[0] + b[0], a[1] + b[1])


def csub(a, b):
    return (a[0] - b[0], a[1] - b[1])


def cmul(a, b):
    return (a[0] * b[0] - a[1] * b[1], a[0] * b[1] + a[1] * b[0])


def cconj_mul(a, b):
    return (a[0] * b[0] + a[1] * b[1], a[0] * b[1] - a[1] * b[0])


def cdiv(numer, denom, floor):
    size = jnp.maximum(denom[0] * denom[0] + denom[1] * denom[1], floor)
    return (
        (numer[0] * denom[0] + numer[1] * denom[1]) / size,
        (numer[1] * denom[0] - numer[0] * denom[1]) / size,
    )


def tree(terms):
    terms = list(terms)
    while len(terms) > 1:
        terms = [cadd(*terms[i : i + 2]) if i + 1 < len(terms) else terms[i] for i in range(0, len(terms), 2)]
    return terms[0]


def combine(a, scale, b):
    out = []
    for i in range(max(len(a), len(b))):
        if i >= len(b):
            out.append(a[i])
        elif i >= len(a):
            out.append(cmul(scale, b[i]))
        else:
            out.append(cadd(a[i], cmul(scale, b[i])))
    return out


def times_k(a):
    zero = (jnp.zeros_like(a[0][0]),) * 2
    out = [(SHIFTS[i] * v[0], SHIFTS[i] * v[1]) for i, v in enumerate(a)] + [zero]
    return [
        cadd(out[i], (SCALE * a[i - 1][0], SCALE * a[i - 1][1])) if i > 0 else out[i]
        for i in range(len(out))
    ]


def coefficients(entry):
    def g(i, j):
        if i > j:
            re, im = g(j, i)
            return (re, -im)
        if i == j:
            return (entry(SLOT[i, j]), 0.0)
        return (entry(SLOT[i, j]), entry(SLOT[i, j] + 1))

    def times_g(b, rows):
        return [tree([cmul(g(i, j), b[j]) for j in range(len(b))]) for i in range(rows)]

    def dot(a, gb):
        return tree([cconj_mul(a[i], gb[i]) for i in range(len(a))])

    def shadow(b):
        return tree([cmul(g(0, j), b[j]) for j in range(len(b))])

    one = jnp.ones_like(entry(0))
    residual = [(one, jnp.zeros_like(one))]
    direction = residual
    solution = []
    for step in range(ITERS):
        rho = shadow(residual)
        if step == 0:
            floor = 1e-06 * rho[0] * rho[0]
        else:
            beta = cmul(cdiv(rho, rho_prev, floor), cdiv(alpha, omega, 0.0001))
            minus = (-omega[0], -omega[1])
            direction = combine(residual, beta, combine(direction, minus, image))
        image = times_k(direction)
        alpha = cdiv(rho, shadow(image), floor)
        middle = combine(residual, (-alpha[0], -alpha[1]), image)
        bent = times_k(middle)
        seen = times_g(bent, len(bent))
        norm = dot(bent, seen)[0] + 1e-06
        against = dot(middle, seen)
        omega = (against[0] / norm, -against[1] / norm)
        solution = combine(combine(solution, alpha, direction), omega, middle)
        residual = combine(middle, (-omega[0], -omega[1]), bent)
        rho_prev = rho
    return solution


def surface_power(x, rows):
    def e(p, c, z):
        f = p * NF + 2 * c
        return (x[f, z, rows, :], x[f + 1, z, rows, :])

    ex, ey, hx, hy = [], [], [], []
    for p in range(2):
        ex0, ey0 = e(p, 0, 0), e(p, 1, 0)
        ex1, ey1 = e(p, 0, 1), e(p, 1, 1)
        ex.append(ex0)
        ey.append(ey0)
        one_x, one_y = (1.0, 0.0) if p == 0 else (0.0, 1.0)
        hx.append((one_x - 2.0 * (ey1[0] - ey0[0]), -2.0 * (ey1[1] - ey0[1])))
        hy.append((one_y + 2.0 * (ex1[0] - ex0[0]), 2.0 * (ex1[1] - ex0[1])))
    det = csub(cmul(hx[0], hy[1]), cmul(hx[1], hy[0]))
    zxx = csub(cmul(ex[0], hy[1]), cmul(ex[1], hy[0]))
    zxy = csub(cmul(ex[1], hx[0]), cmul(ex[0], hx[1]))
    zyx = csub(cmul(ey[0], hy[1]), cmul(ey[1], hy[0]))
    zyy = csub(cmul(ey[1], hx[0]), cmul(ey[0], hx[1]))
    size = det[0] * det[0] + det[1] * det[1]
    inv = 1.0 / jnp.maximum(size, 0.25)
    scale = size * inv * inv
    cross = cadd(cconj_mul(zxx, zxy), cconj_mul(zyx, zyy))
    first = zxx[0] * zxx[0] + zxx[1] * zxx[1] + (zyx[0] * zyx[0] + zyx[1] * zyx[1])
    second = zxy[0] * zxy[0] + zxy[1] * zxy[1] + (zyy[0] * zyy[0] + zyy[1] * zyy[1])
    return [scale * first, scale * second, scale * cross[0], scale * cross[1]]


def finish(got, k, *rest):
    fars, (x_far, send, x, surface, picked, sem) = rest[:11], rest[11:]
    sub = lax.broadcasted_iota(jnp.int32, (8, NY), 0)
    row = jnp.broadcast_to(jnp.sum(got[:, 0:NY], axis=0, keepdims=True), (8, NY))
    table = jnp.where(sub == 0, row, pltpu.roll(row, 64, 1))
    cache = {}

    def entry(slot):
        if slot not in cache:
            cache[slot] = jnp.broadcast_to(table[:, slot : slot + 1], (8, NY))
        return cache[slot]

    coefs = coefficients(entry)
    scal = [[tuple(jnp.broadcast_to(half[p : p + 1, :], (8, NY)) for half in c) for c in coefs] for p in range(2)]

    mine = pltpu.roll(got[:, NY : 2 * NY], lax.rem(NY - 32 * lax.axis_index("gx"), NY), 1).astype(jnp.int32)
    group = lax.broadcasted_iota(jnp.int32, (32, NY), 1) // 32
    cells = mine[0:32, :]
    for e in range(1, 4):
        cells = jnp.where(group == e, pltpu.roll(mine[32 * e : 32 * e + 32, :], 32 * e, 1), cells)
    col = cells % NY
    line = cells // NY
    cols = [col[8 * i : 8 * i + 8, :] for i in range(4)]
    lines = [line[8 * i : 8 * i + 8, :] for i in range(4)]

    def layer(p, z):
        for xb in range(CX // 8):
            rows = pl.ds(8 * xb, 8)
            kz = k[z, rows, :]
            inv = 1.0 / (16.0 + kz * kz)
            weight = (4.0 * inv, -kz * inv)
            for f in range(p * NF, p * NF + NF, 2):
                terms = [cmul(scal[p][i], (basis(i, f, z, rows), basis(i, f + 1, z, rows))) for i in range(6)]
                y = cmul(weight, tree(terms))
                x[f, z, rows, :] = y[0]
                x[f + 1, z, rows, :] = y[1]

    def basis(i, f, z, rows):
        if i == 0:
            return fars[0][f, z, rows, :]
        return fars[5 * (f // NF) + i][f % NF, z, rows, :]

    outs = []

    def leave(p, z, count):
        part = pl.ds(p * NF, NF), pl.ds(z, count)
        outs.extend(start_all([(x.at[part], x_far.at[part])], sem, len(outs)))

    for p in range(2):
        for z in range(2):
            layer(p, z)
        leave(p, 0, 2)
    for xb in range(CX // 8):
        for v, value in enumerate(surface_power(x, pl.ds(8 * xb, 8))):
            surface[v * CX + 8 * xb : v * CX + 8 * xb + 8, :] = value
    for i in range(4):
        acc = [jnp.zeros((8, NY), f32)] * 4
        for r in range(CX):
            for v in range(4):
                src = jnp.broadcast_to(surface[v * CX + r : v * CX + r + 1, :], (8, NY))
                hit = jnp.take_along_axis(src, cols[i], axis=1, mode="promise_in_bounds")
                acc[v] = jnp.where(lines[i] == r, hit, acc[v])
        for v in range(4):
            picked[v * 32 + 8 * i : v * 32 + 8 * i + 8, :] = acc[v]
        p, z = i // 2, 2 + i % 2
        layer(p, z)
        leave(p, z, 1)
    for e in range(4):
        out = None
        for v in range(4):
            part = picked[v * 32 : v * 32 + 32, :]
            if v != e:
                part = pltpu.roll(part, (32 * (v - e)) % NY, 1)
            out = part if out is None else jnp.where(group == v, part, out)
        send[32 * e : 32 * e + 32, :] = out
    wait_all(outs)


def hazard_rows(got, power, out):
    block = jnp.concatenate([got[0:8, :], jnp.zeros((NY - 8, NY), f32)], axis=0)
    turned = jnp.transpose(block)
    for j in range(4):
        for qb in range(4):
            total = None
            for v in range(4):
                first = v * 32 + 8 * qb
                column = jnp.broadcast_to(turned[first : first + 8, j : j + 1], (8, power.shape[1]))
                term = column * power[4 * j + v : 4 * j + v + 1, :]
                total = term if total is None else total + term
            row = 32 * j + 8 * qb
            out[row : row + 8, :] = total


def partners(count):
    first = [(i, i ^ 1) for i in range(count)]
    second = [(i, ((i + 1) ^ 1) - 1) for i in range(1, count - 1)]
    return first, second


def exchange(to_a, to_b, axis):
    first, second = partners(lax.axis_size(axis))
    return lax.ppermute(to_a, axis, first), lax.ppermute(to_b, axis, second)


def per_device(right_side, conductance, owned_cells, spectra, scenario_tile):
    block = (NF, NZL, CX, NY)
    wide = (NF, NZL, WX, NY)
    whole = (2 * NF, NZL, CX, NY)
    dma = pltpu.SemaphoreType.DMA
    space = pltpu.VMEM((NF, EZ, WX, NY), f32)
    r_far = right_side.reshape(whole)
    side = (((2 * NF + 1) * NZL * SIDE, NY), VM)
    scen = spectra.shape[0]
    rims = [
        pltpu.VMEM((2 * NF, NZL, 16, NY), f32),
        pltpu.VMEM((NZL, 16, NY), f32),
        pltpu.VMEM((4, scen), f32),
        pltpu.VMEM((1, scen), jnp.int32),
        dma((6,)),
    ]
    to_a, to_b, power = call(
        pack_x, [HBM] * 4, [side] * 2 + [((16, scen), VM)], rims, limit=FIRST_LIMIT
    )(*[pltpu.with_memory_space_constraint(v, pltpu.HBM) for v in (r_far, conductance, spectra.T, scenario_tile.reshape(1, scen))])
    r, k = r_far, conductance
    near = exchange(to_a, to_b, "gx")
    deep = [((rows_of(REACH, with_k), NY), VM) for with_k in (True, False)]
    *packed, cells = call(
        pack_z,
        [VM] * 5,
        [deep[0]] * 2 + [deep[1]] * 2 + [((1, NY), VM)],
        [
            pltpu.VMEM((2 * NF, NZL, WX, NY), f32),
            pltpu.VMEM((NZL, WX, NY), f32),
            pltpu.VMEM((2, 8, WX, NY), f32),
        ],
        moved=1 << 22,
    )(r, k, *near, owned_cells[0])
    halo_0 = exchange(*packed[0:2], "gz")
    halo_1 = exchange(*packed[2:4], "gz")
    back = ((rows_of(0, False), NY), VM)
    far = pltpu.VMEM((8, WX, NY), f32)
    firsts = [(block, VM), (block, VM), (wide, VM), back, back, (block, HBM), (block, HBM)]
    cost = {"flops": 1 << 24, "moved": 1 << 23}
    *b_0, to_a, to_b, b1_0, b2_0, m = call(
        first_half_0,
        [VM] * 6,
        firsts + [((2, EZ, WX, NY), VM)],
        [pltpu.VMEM((EZ, WX, NY), f32)] + [space] * 5 + [far, dma((2,))],
        **cost,
    )(r, k, *near, *halo_0)
    halo_0 = exchange(to_a, to_b, "gz")
    *b_1, to_a, to_b, b1_1, b2_1 = call(
        first_half_1, [VM] * 6, firsts, [space] * 5 + [far, dma((2,))], **cost
    )(r, m, *near, *halo_1)
    halo_1 = exchange(to_a, to_b, "gz")
    table = ((64, NY), VM)
    part_0, part_1 = call(low_gram, [VM] * 7, [table] * 2, **cost)(r, *b_0, *b_1)
    seconds = [(block, HBM)] * 3
    spaces = [space] * 7 + [dma((3,))]
    *high_0, total = call(
        second_half_0, [VM] * 8, seconds + [table], spaces, **cost
    )(r, *b_0, m, *halo_0, part_0)
    *high_1, send = call(
        second_half_1,
        [VM] * 10,
        seconds + [((128, 2 * NY), VM)],
        [pltpu.VMEM((64, NY), f32)] + spaces,
        **cost,
    )(r, *b_1, m, *halo_1, part_1, total, cells)
    held = (send, conductance, r_far, b1_0, b2_0, *high_0, b1_1, b2_1, *high_1)
    send, *fars = lax.optimization_barrier(held)
    got = lax.all_to_all(send, ("gz", "gx"), 0, 0, tiled=True)
    x, send = call(
        finish,
        [VM] * 13,
        [(whole, HBM), ((128, NY), VM)],
        [
            pltpu.VMEM(whole, f32),
            pltpu.VMEM((4 * CX, NY), f32),
            pltpu.VMEM((4 * CX, NY), f32),
            dma((6,)),
        ],
    )(got, *fars)
    got = lax.all_to_all(send, ("gz", "gx"), 0, 0, tiled=True)
    (hazard,) = call(hazard_rows, [VM] * 2, [((128, scen), VM)])(got, power)
    return x.reshape(right_side.shape), hazard


def solution(mesh):
    return jax.shard_map(
        per_device,
        mesh=mesh,
        in_specs=(
            P(None, None, None, "gz", "gx", None),
            P("gz", "gx", None),
            P(("gz", "gx"), None, None),
            P(),
            P(),
        ),
        out_specs=(P(None, None, None, "gz", "gx", None), P(("gz", "gx"), None)),
        check_vma=False,
    )
```

```python
import jax
import jax.numpy as jnp
from jax import lax
from jax.experimental import pallas as pl
from jax.experimental.pallas import tpu as pltpu
from jax.sharding import PartitionSpec as P

SHIFTS = (1.8, 0.6, 1.8, 0.6, 1.8, 0.6)
SCALE = 1.0
ITERS = 3
REACH = 3
SIDE = 2 * REACH
NF = 6
CX, NZL, NY = 32, 4, 128
WX = 48
EZ = NZL + 2 * REACH
f32 = jnp.float32
VM = pl.BlockSpec(memory_space=pltpu.VMEM)
LIMIT = 14 * 1024 * 1024
FIRST_LIMIT = 14 * 1024 * 1024


HBM = pl.BlockSpec(memory_space=pltpu.HBM)


def call(body, ins, outs, scratch=(), flops=0, moved=0, limit=LIMIT):
    return pl.pallas_call(
        body,
        out_shape=[jax.ShapeDtypeStruct(shape, f32) for shape, _ in outs],
        in_specs=ins,
        out_specs=[spec for _, spec in outs],
        scratch_shapes=list(scratch),
        compiler_params=pltpu.CompilerParams(vmem_limit_bytes=limit),
        cost_estimate=pl.CostEstimate(flops=flops, bytes_accessed=moved, transcendentals=0),
    )


def odd(axis):
    return lax.rem(lax.axis_index(axis), 2) == 1


def either(flag, body, first, second):
    @pl.when(jnp.logical_not(flag))
    def _():
        body(first, second)

    @pl.when(flag)
    def _():
        body(second, first)


def start_all(pairs, sem, first=0):
    copies = [pltpu.make_async_copy(src, dst, sem.at[first + i]) for i, (src, dst) in enumerate(pairs)]
    for copy in copies:
        copy.start()
    return copies


def wait_all(copies):
    for copy in copies:
        copy.wait()


def pack_x(r, k, spectra, scenario, to_a, to_b, power, rim, rim_k, spec, scen, sem):
    pairs = []
    for i in range(2):
        src = pl.ds(i * (CX - 8), 8)
        pairs.append((r.at[:, :, src, :], rim.at[:, :, pl.ds(8 * i, 8), :]))
        pairs.append((k.at[:, src, :], rim_k.at[:, pl.ds(8 * i, 8), :]))
    pairs += [(spectra, spec), (scenario, scen)]
    wait_all(start_all(pairs, sem))

    def fill(up, down):
        for f in range(2 * NF + 1):
            for z in range(NZL):
                row = (f * NZL + z) * SIDE
                src = rim_k.at[z] if f == 2 * NF else rim.at[f, z]
                up[row : row + SIDE, :] = src[16 - SIDE : 16, :]
                down[row : row + SIDE, :] = src[0:SIDE, :]

    either(odd("gx"), fill, to_a, to_b)
    xr, xi, yr, yi = [spec[i : i + 1, :] for i in range(4)]
    base = [
        xr * xr + xi * xi,
        yr * yr + yi * yi,
        2.0 * (xr * yr + xi * yi),
        2.0 * (xi * yr - xr * yi),
    ]
    for j in range(4):
        weight = jnp.where(scen[...] == j, 1.0, 0.25)
        for v in range(4):
            power[4 * j + v : 4 * j + v + 1, :] = weight * base[v]


def sides(from_a, from_b, near):
    a, b = from_a[near : near + SIDE, :], from_b[near : near + SIDE, :]
    flag = odd("gx")
    return jnp.where(flag, a, b), jnp.where(flag, b, a)


def spans(margin):
    low, high = margin + REACH, CX - 1 + margin
    below = ((1 - low, high + 3), (2 - low, high + 3), (3 - low, high + 2))
    above = ((-low, high + 2), (-low, high + 1), (-low, high))
    return below, above


def layout(span, with_k):
    near, row = {}, 0
    for i in range(REACH - 1):
        for f in range(NF):
            near[i, f] = row
            row += span[i][1] - span[i][0] + 1
    far = []
    for _ in range(4):
        far.append(row)
        row += span[-1][1] - span[-1][0] + 1
    k = []
    for i in range(REACH - 1 if with_k else 0):
        k.append(row)
        row += span[i][1] - span[i][0] + 1
    return near, far, k, row


def rows_of(margin, with_k):
    return max(layout(span, with_k)[3] for span in spans(margin))


def cut(span):
    return slice(8 + span[0], 9 + span[1]), span[1] - span[0] + 1


def far_fields(b, first, weight, far):
    _, last = lanes()

    def y(z, c):
        mr, mi = weight(z)
        re, im = b[2 * c, first + z], b[2 * c + 1, first + z]
        return mr * re - mi * im, mr * im + mi * re

    ex, ey, ez = [y(NZL - REACH, c) for c in range(3)]
    for q in range(2):
        far[q] = ex[q] + (next_x(ez[q]) - ez[q])
        far[2 + q] = ey[q] + (next_y(ez[q], last) - ez[q])
    for c in range(2):
        far[4 + 2 * c], far[5 + 2 * c] = y(REACH - 1, c)


def fill_messages(b, first, far, k, margin, up, down):
    for side, (out, span) in enumerate(zip((up, down), spans(margin))):
        near, far_rows, k_rows, _ = layout(span, k is not None)
        for i in range(REACH - 1):
            z = first + (NZL - 1 - i if side == 0 else i)
            cols, n = cut(span[i])
            for f in range(NF):
                out[near[i, f] : near[i, f] + n, :] = b[f, z, cols, :]
            if k is not None:
                out[k_rows[i] : k_rows[i] + n, :] = k[z, cols, :]
        cols, n = cut(span[-1])
        for j, row in enumerate(far_rows):
            out[row : row + n, :] = far[4 * side + j, cols, :]


def take_messages(b, y, k, margin, above, below):
    for side, (src, span) in enumerate(zip((below, above), spans(margin))):
        near, far_rows, k_rows, _ = layout(span, k is not None)
        for i in range(REACH - 1):
            z = REACH - 1 - i if side == 0 else REACH + NZL + i
            cols, n = cut(span[i])
            for f in range(NF):
                b[f, z, cols, :] = src[near[i, f] : near[i, f] + n, :]
            if k is not None:
                k[z, cols, :] = src[k_rows[i] : k_rows[i] + n, :]
        cols, n = cut(span[-1])
        z = 0 if side == 0 else EZ - 1
        for j, row in enumerate(far_rows):
            y[j, z, cols, :] = src[row : row + n, :]


def clear_sides(ref):
    zero = jnp.zeros((EZ, 8, NY), f32)
    ref[:, 0:8, :] = zero
    ref[:, WX - 8 : WX, :] = zero


def clear_far(y):
    for f in range(NF):
        for z in (0, EZ - 1):
            if f < 4:
                y[f, z, 0:8, :] = jnp.zeros((8, NY), f32)
                y[f, z, WX - 8 : WX, :] = jnp.zeros((8, NY), f32)
            else:
                y[f, z] = jnp.zeros((WX, NY), f32)


def own_layers(dst, first, src, xa, xb, near):
    for z in range(NZL):
        left, right = sides(xa, xb, (near * NZL + z) * SIDE)
        dst[first + z, 8 - SIDE : 8, :] = left
        dst[first + z, 8 : 8 + CX, :] = src[z]
        dst[first + z, 8 + CX : 8 + CX + SIDE, :] = right


def weight_of(kz):
    inv = jnp.where(kz > 0.0, 1.0, 0.0) / (16.0 + kz * kz)
    return 4.0 * inv, -kz * inv


def pack_z(r, k, xa, xb, owned, a_0, b_0, a_1, b_1, cells, b, kx, far):
    for f in range(2 * NF + 1):
        dst = kx if f == 2 * NF else b.at[f]
        zero = jnp.zeros((NZL, 8, NY), f32)
        dst[:, 0:8, :] = zero
        dst[:, WX - 8 : WX, :] = zero
        own_layers(dst, 0, k if f == 2 * NF else r.at[f], xa, xb, f)
    weights = {z: weight_of(kx[z]) for z in (NZL - REACH, REACH - 1)}
    for p in range(2):
        far_fields(b.at[pl.ds(p * NF, NF)], 0, lambda z: weights[z], far.at[p])

    def fill(first, second):
        for p in range(2):
            own = b.at[pl.ds(p * NF, NF)]
            fill_messages(own, 0, far.at[p], kx if p == 0 else None, REACH, first[p], second[p])

    either(odd("gz"), fill, (a_0, a_1), (b_0, b_1))
    cells[...] = jnp.concatenate([owned[j : j + 1, :] for j in range(4)], axis=1).astype(f32)


def lanes():
    lane = lax.broadcasted_iota(jnp.int32, (WX, NY), 1)
    return lane == 0, lane == NY - 1


def next_y(a, last):
    return jnp.where(last, 0.0, pltpu.roll(a, NY - 1, 1))


def next_x(a):
    return pltpu.roll(a, WX - 1, 0)


def prev_x(a):
    return pltpu.roll(a, 1, 0)


def smooth(b, y, m, base, z):
    mr, mi = m[0, z], m[1, z]
    for c in range(3):
        re, im = b[base + 2 * c, z], b[base + 2 * c + 1, z]
        y[base + 2 * c, z] = mr * re - mi * im
        y[base + 2 * c + 1, z] = mr * im + mi * re


def apply_k(b, y, bn, yn, hs, m, lo, hi, shift, want_y):
    first, last = lanes()
    own = (1.0 - shift) / SCALE
    inv = 1.0 / SCALE
    for z in range(lo - 1, hi):
        for e in range(2):
            ex, ey, ez = y[e, z], y[e + 2, z], y[e + 4, z]
            hs[e, z] = next_y(ez, last) - ez - (y[e + 2, z + 1] - ey)
            hs[e + 2, z] = y[e, z + 1] - ex - (next_x(ez) - ez)
            hs[e + 4, z] = next_x(ey) - ey - (next_y(ex, last) - ex)
    for z in range(lo, hi):
        for e in range(2):
            hx, hy, hz = hs[e, z], hs[e + 2, z], hs[e + 4, z]
            ex, ey, ez = y[e, z], y[e + 2, z], y[e + 4, z]
            cx = hz - jnp.where(first, -ex, pltpu.roll(hz, 1, 1)) - (hy - hs[e + 2, z - 1])
            cy = hx - hs[e, z - 1] - (hz - prev_x(hz))
            cz = hy - prev_x(hy) - (hx - jnp.where(first, ez, pltpu.roll(hx, 1, 1)))
            for c, (cur, old) in enumerate(((cx, ex), (cy, ey), (cz, ez))):
                new = cur - 4.0 * old
                if inv != 1.0:
                    new = new * inv
                bn[e + 2 * c, z] = new + own * b[e + 2 * c, z]
        if want_y:
            smooth(bn, yn, m, 0, z)


def all_smooth(b, y, m):
    def layer(z, _):
        smooth(b, y, m, 0, z)
        return 0

    lax.fori_loop(1, EZ - 1, layer, 0)


def keep(src, out):
    def field(f, _):
        out[f] = src[f, REACH : REACH + NZL, 8 : 8 + CX, :]
        return 0

    lax.fori_loop(0, NF, field, 0)


def first_steps(p, r, k, kx, xa, xb, za, zb, b1, b2, b3w, to_a, to_b, m, ba, bb, ya, yb, hs, far):
    for f in range(NF):
        clear_sides(ba.at[f])
        own_layers(ba.at[f], REACH, r.at[p * NF + f], xa, xb, p * NF + f)
    clear_far(ya)
    if p == 0:
        clear_sides(kx)
        own_layers(kx, REACH, k, xa, xb, 2 * NF)

    def take(above, below):
        take_messages(ba, ya, kx if p == 0 else None, REACH, above, below)

    either(odd("gz"), take, za, zb)
    if p == 0:

        def layer(z, _):
            m[0, z], m[1, z] = weight_of(kx[z])
            return 0

        lax.fori_loop(1, EZ - 1, layer, 0)
    all_smooth(ba, ya, m)
    apply_k(ba, ya, bb, yb, hs, m, 1, EZ - 1, SHIFTS[0], True)
    keep(bb, b1)
    apply_k(bb, yb, ba, ya, hs, m, 2, EZ - 2, SHIFTS[1], True)
    keep(ba, b2)
    apply_k(ba, ya, bb, yb, hs, m, 3, EZ - 3, SHIFTS[2], False)
    for f in range(NF):
        b3w[f] = bb[f, REACH : REACH + NZL]
    far_fields(bb, REACH, lambda z: (m[0, REACH + z], m[1, REACH + z]), far)
    either(odd("gz"), lambda up, down: fill_messages(bb, REACH, far, None, 0, up, down), to_a, to_b)


def first_half_0(r, k, xa, xb, za, zb, b1, b2, b3w, to_a, to_b, m, kx, *space):
    first_steps(0, r, k, kx, xa, xb, za, zb, b1, b2, b3w, to_a, to_b, m, *space)


def first_half_1(r, m, xa, xb, za, zb, b1, b2, b3w, to_a, to_b, *space):
    first_steps(1, r, None, None, xa, xb, za, zb, b1, b2, b3w, to_a, to_b, m, *space)


PAIRS = [(i, j) for i in range(7) for j in range(i, 7)]
LOW = [pair for pair in PAIRS if pair[1] <= REACH]
HIGH = [pair for pair in PAIRS if pair[1] > REACH]
SLOT = {}
for _pair in LOW + HIGH:
    SLOT[_pair] = sum(1 if a == b else 2 for a, b in SLOT)


def gram(read, pairs, out, unroll=False):
    used = sorted({i for pair in pairs for i in pair})
    count = sum(1 if i == j else 2 for i, j in pairs)

    def block(step, acc):
        c, z = step // NZL, step % NZL
        acc = list(acc)
        for xb in range(CX // 8):
            vec = {i: (read(i, 2 * c, z, xb), read(i, 2 * c + 1, z, xb)) for i in used}
            at = 0
            for i, j in pairs:
                (ar, ai), (br, bi) = vec[i], vec[j]
                acc[at] = acc[at] + (ar * br + ai * bi)
                at += 1
                if i != j:
                    acc[at] = acc[at] + (ar * bi - ai * br)
                    at += 1
        return tuple(acc)

    acc = lax.fori_loop(0, 3 * NZL, block, (jnp.zeros((8, NY), f32),) * count, unroll=unroll)
    at = 0
    for i, j in pairs:
        for part in range(1 if i == j else 2):
            row = SLOT[i, j] + part
            out[row : row + 1, :] = jnp.sum(acc[at], axis=0, keepdims=True)
            at += 1


def low_gram(b0, b1_0, b2_0, b3w_0, b1_1, b2_1, b3w_1, part_0, part_1):
    for p, (b1, b2, b3w, part) in enumerate(((b1_0, b2_0, b3w_0, part_0), (b1_1, b2_1, b3w_1, part_1))):
        part[...] = jnp.zeros((64, NY), f32)
        gram(reader(p, b0, b1, b2, b3w), LOW, part)


def reader(p, b0, b1, b2, b3w, *slabs):
    def read(i, f, z, xb):
        if i == 0:
            return b0[p * NF + f, z, pl.ds(8 * xb, 8), :]
        if i < 3:
            return (b1, b2)[i - 1][f, z, pl.ds(8 * xb, 8), :]
        if i == 3:
            return b3w[f, z, pl.ds(8 + 8 * xb, 8), :]
        return slabs[i - 4][f, REACH + z, pl.ds(8 + 8 * xb, 8), :]

    return read


def second_steps(p, b0, b1, b2, b3w, m, za, zb, part, b3_far, b4_far, b5_far, total, ba, bb, bc, bd, ya, yb, hs, sem):
    own = pl.ds(REACH, NZL)
    mid = pl.ds(8, CX)
    copies = start_all([(b3w.at[:, :, mid, :], b3_far)], sem)
    for f in range(NF):
        clear_sides(ba.at[f])
        ba[f, REACH : REACH + NZL] = b3w[f]
    clear_far(ya)
    either(odd("gz"), lambda above, below: take_messages(ba, ya, None, 0, above, below), za, zb)
    all_smooth(ba, ya, m)
    apply_k(ba, ya, bb, yb, hs, m, 1, EZ - 1, SHIFTS[3], True)
    copies += start_all([(bb.at[:, own, mid, :], b4_far)], sem, 1)
    apply_k(bb, yb, bc, ya, hs, m, 2, EZ - 2, SHIFTS[4], True)
    copies += start_all([(bc.at[:, own, mid, :], b5_far)], sem, 2)
    total[...] = part[...]
    read = reader(p, b0, b1, b2, b3w, bb, bc, bd)
    apply_k(bc, ya, bd, yb, hs, m, 3, EZ - 3, SHIFTS[5], False)
    gram(read, [pair for pair in HIGH if pair[1] < 6], total, True)
    gram(read, [pair for pair in HIGH if pair[1] == 6], total, True)
    wait_all(copies)


def second_half_0(b0, b1, b2, b3w, m, za, zb, part, b3_far, b4_far, b5_far, total, *space):
    second_steps(0, b0, b1, b2, b3w, m, za, zb, part, b3_far, b4_far, b5_far, total, *space)


def second_half_1(b0, b1, b2, b3w, m, za, zb, part, other, cells, b3_far, b4_far, b5_far, send, total, *space):
    second_steps(1, b0, b1, b2, b3w, m, za, zb, part, b3_far, b4_far, b5_far, total, *space)
    both = jnp.concatenate([other[...], total[...]], axis=0)
    sums = jnp.sum(jnp.transpose(both), axis=0, keepdims=True)
    send[...] = jnp.broadcast_to(jnp.concatenate([sums, cells[...]], axis=1), (128, 2 * NY))


def cadd(a, b):
    return (a[0] + b[0], a[1] + b[1])


def csub(a, b):
    return (a[0] - b[0], a[1] - b[1])


def cmul(a, b):
    return (a[0] * b[0] - a[1] * b[1], a[0] * b[1] + a[1] * b[0])


def cconj_mul(a, b):
    return (a[0] * b[0] + a[1] * b[1], a[0] * b[1] - a[1] * b[0])


def cdiv(numer, denom, floor):
    size = jnp.maximum(denom[0] * denom[0] + denom[1] * denom[1], floor)
    return (
        (numer[0] * denom[0] + numer[1] * denom[1]) / size,
        (numer[1] * denom[0] - numer[0] * denom[1]) / size,
    )


def tree(terms):
    terms = list(terms)
    while len(terms) > 1:
        terms = [cadd(*terms[i : i + 2]) if i + 1 < len(terms) else terms[i] for i in range(0, len(terms), 2)]
    return terms[0]


def combine(a, scale, b):
    out = []
    for i in range(max(len(a), len(b))):
        if i >= len(b):
            out.append(a[i])
        elif i >= len(a):
            out.append(cmul(scale, b[i]))
        else:
            out.append(cadd(a[i], cmul(scale, b[i])))
    return out


def times_k(a):
    zero = (jnp.zeros_like(a[0][0]),) * 2
    out = [(SHIFTS[i] * v[0], SHIFTS[i] * v[1]) for i, v in enumerate(a)] + [zero]
    return [
        cadd(out[i], (SCALE * a[i - 1][0], SCALE * a[i - 1][1])) if i > 0 else out[i]
        for i in range(len(out))
    ]


def coefficients(entry):
    def g(i, j):
        if i > j:
            re, im = g(j, i)
            return (re, -im)
        if i == j:
            return (entry(SLOT[i, j]), 0.0)
        return (entry(SLOT[i, j]), entry(SLOT[i, j] + 1))

    def times_g(b, rows):
        return [tree([cmul(g(i, j), b[j]) for j in range(len(b))]) for i in range(rows)]

    def dot(a, gb):
        return tree([cconj_mul(a[i], gb[i]) for i in range(len(a))])

    def shadow(b):
        return tree([cmul(g(0, j), b[j]) for j in range(len(b))])

    one = jnp.ones_like(entry(0))
    residual = [(one, jnp.zeros_like(one))]
    direction = residual
    solution = []
    for step in range(ITERS):
        rho = shadow(residual)
        if step == 0:
            floor = 1e-06 * rho[0] * rho[0]
        else:
            beta = cmul(cdiv(rho, rho_prev, floor), cdiv(alpha, omega, 0.0001))
            minus = (-omega[0], -omega[1])
            direction = combine(residual, beta, combine(direction, minus, image))
        image = times_k(direction)
        alpha = cdiv(rho, shadow(image), floor)
        middle = combine(residual, (-alpha[0], -alpha[1]), image)
        bent = times_k(middle)
        seen = times_g(bent, len(bent))
        norm = dot(bent, seen)[0] + 1e-06
        against = dot(middle, seen)
        omega = (against[0] / norm, -against[1] / norm)
        solution = combine(combine(solution, alpha, direction), omega, middle)
        residual = combine(middle, (-omega[0], -omega[1]), bent)
        rho_prev = rho
    return solution


def surface_power(x, rows):
    def e(p, c, z):
        f = p * NF + 2 * c
        return (x[f, z, rows, :], x[f + 1, z, rows, :])

    ex, ey, hx, hy = [], [], [], []
    for p in range(2):
        ex0, ey0 = e(p, 0, 0), e(p, 1, 0)
        ex1, ey1 = e(p, 0, 1), e(p, 1, 1)
        ex.append(ex0)
        ey.append(ey0)
        one_x, one_y = (1.0, 0.0) if p == 0 else (0.0, 1.0)
        hx.append((one_x - 2.0 * (ey1[0] - ey0[0]), -2.0 * (ey1[1] - ey0[1])))
        hy.append((one_y + 2.0 * (ex1[0] - ex0[0]), 2.0 * (ex1[1] - ex0[1])))
    det = csub(cmul(hx[0], hy[1]), cmul(hx[1], hy[0]))
    zxx = csub(cmul(ex[0], hy[1]), cmul(ex[1], hy[0]))
    zxy = csub(cmul(ex[1], hx[0]), cmul(ex[0], hx[1]))
    zyx = csub(cmul(ey[0], hy[1]), cmul(ey[1], hy[0]))
    zyy = csub(cmul(ey[1], hx[0]), cmul(ey[0], hx[1]))
    size = det[0] * det[0] + det[1] * det[1]
    inv = 1.0 / jnp.maximum(size, 0.25)
    scale = size * inv * inv
    cross = cadd(cconj_mul(zxx, zxy), cconj_mul(zyx, zyy))
    first = zxx[0] * zxx[0] + zxx[1] * zxx[1] + (zyx[0] * zyx[0] + zyx[1] * zyx[1])
    second = zxy[0] * zxy[0] + zxy[1] * zxy[1] + (zyy[0] * zyy[0] + zyy[1] * zyy[1])
    return [scale * first, scale * second, scale * cross[0], scale * cross[1]]


def finish(got, k, *rest):
    fars, (x_far, send, x, surface, picked, sem) = rest[:11], rest[11:]
    sub = lax.broadcasted_iota(jnp.int32, (8, NY), 0)
    row = jnp.broadcast_to(jnp.sum(got[:, 0:NY], axis=0, keepdims=True), (8, NY))
    table = jnp.where(sub == 0, row, pltpu.roll(row, 64, 1))
    cache = {}

    def entry(slot):
        if slot not in cache:
            cache[slot] = jnp.broadcast_to(table[:, slot : slot + 1], (8, NY))
        return cache[slot]

    coefs = coefficients(entry)
    scal = [[tuple(jnp.broadcast_to(half[p : p + 1, :], (8, NY)) for half in c) for c in coefs] for p in range(2)]

    mine = pltpu.roll(got[:, NY : 2 * NY], lax.rem(NY - 32 * lax.axis_index("gx"), NY), 1).astype(jnp.int32)
    group = lax.broadcasted_iota(jnp.int32, (32, NY), 1) // 32
    cells = mine[0:32, :]
    for e in range(1, 4):
        cells = jnp.where(group == e, pltpu.roll(mine[32 * e : 32 * e + 32, :], 32 * e, 1), cells)
    col = cells % NY
    line = cells // NY
    cols = [col[8 * i : 8 * i + 8, :] for i in range(4)]
    lines = [line[8 * i : 8 * i + 8, :] for i in range(4)]

    def layer(p, z):
        for xb in range(CX // 8):
            rows = pl.ds(8 * xb, 8)
            kz = k[z, rows, :]
            inv = 1.0 / (16.0 + kz * kz)
            weight = (4.0 * inv, -kz * inv)
            for f in range(p * NF, p * NF + NF, 2):
                terms = [cmul(scal[p][i], (basis(i, f, z, rows), basis(i, f + 1, z, rows))) for i in range(6)]
                y = cmul(weight, tree(terms))
                x[f, z, rows, :] = y[0]
                x[f + 1, z, rows, :] = y[1]

    def basis(i, f, z, rows):
        if i == 0:
            return fars[0][f, z, rows, :]
        return fars[5 * (f // NF) + i][f % NF, z, rows, :]

    outs = []

    def leave(p, z, count):
        part = pl.ds(p * NF, NF), pl.ds(z, count)
        outs.extend(start_all([(x.at[part], x_far.at[part])], sem, len(outs)))

    for p in range(2):
        for z in range(2):
            layer(p, z)
        leave(p, 0, 2)
    for xb in range(CX // 8):
        for v, value in enumerate(surface_power(x, pl.ds(8 * xb, 8))):
            surface[v * CX + 8 * xb : v * CX + 8 * xb + 8, :] = value
    for i in range(4):
        acc = [jnp.zeros((8, NY), f32)] * 4
        for r in range(CX):
            for v in range(4):
                src = jnp.broadcast_to(surface[v * CX + r : v * CX + r + 1, :], (8, NY))
                hit = jnp.take_along_axis(src, cols[i], axis=1, mode="promise_in_bounds")
                acc[v] = jnp.where(lines[i] == r, hit, acc[v])
        for v in range(4):
            picked[v * 32 + 8 * i : v * 32 + 8 * i + 8, :] = acc[v]
        p, z = i // 2, 2 + i % 2
        layer(p, z)
        leave(p, z, 1)
    for e in range(4):
        out = None
        for v in range(4):
            part = picked[v * 32 : v * 32 + 32, :]
            if v != e:
                part = pltpu.roll(part, (32 * (v - e)) % NY, 1)
            out = part if out is None else jnp.where(group == v, part, out)
        send[32 * e : 32 * e + 32, :] = out
    wait_all(outs)


def hazard_rows(got, power, out):
    block = jnp.concatenate([got[0:8, :], jnp.zeros((NY - 8, NY), f32)], axis=0)
    turned = jnp.transpose(block)
    for j in range(4):
        for qb in range(4):
            total = None
            for v in range(4):
                first = v * 32 + 8 * qb
                column = jnp.broadcast_to(turned[first : first + 8, j : j + 1], (8, power.shape[1]))
                term = column * power[4 * j + v : 4 * j + v + 1, :]
                total = term if total is None else total + term
            row = 32 * j + 8 * qb
            out[row : row + 8, :] = total


def partners(count):
    first = [(i, i ^ 1) for i in range(count)]
    second = [(i, ((i + 1) ^ 1) - 1) for i in range(1, count - 1)]
    return first, second


def exchange(to_a, to_b, axis):
    first, second = partners(lax.axis_size(axis))
    return lax.ppermute(to_a, axis, first), lax.ppermute(to_b, axis, second)


def per_device(right_side, conductance, owned_cells, spectra, scenario_tile):
    block = (NF, NZL, CX, NY)
    wide = (NF, NZL, WX, NY)
    whole = (2 * NF, NZL, CX, NY)
    dma = pltpu.SemaphoreType.DMA
    space = pltpu.VMEM((NF, EZ, WX, NY), f32)
    r_far = right_side.reshape(whole)
    side = (((2 * NF + 1) * NZL * SIDE, NY), VM)
    scen = spectra.shape[0]
    rims = [
        pltpu.VMEM((2 * NF, NZL, 16, NY), f32),
        pltpu.VMEM((NZL, 16, NY), f32),
        pltpu.VMEM((4, scen), f32),
        pltpu.VMEM((1, scen), jnp.int32),
        dma((6,)),
    ]
    to_a, to_b, power = call(
        pack_x, [HBM] * 4, [side] * 2 + [((16, scen), VM)], rims, limit=FIRST_LIMIT
    )(*[pltpu.with_memory_space_constraint(v, pltpu.HBM) for v in (r_far, conductance, spectra.T, scenario_tile.reshape(1, scen))])
    r, k = r_far, conductance
    near = exchange(to_a, to_b, "gx")
    deep = [((rows_of(REACH, with_k), NY), VM) for with_k in (True, False)]
    *packed, cells = call(
        pack_z,
        [VM] * 5,
        [deep[0]] * 2 + [deep[1]] * 2 + [((1, NY), VM)],
        [
            pltpu.VMEM((2 * NF, NZL, WX, NY), f32),
            pltpu.VMEM((NZL, WX, NY), f32),
            pltpu.VMEM((2, 8, WX, NY), f32),
        ],
        moved=1 << 22,
    )(r, k, *near, owned_cells[0])
    halo_0 = exchange(*packed[0:2], "gz")
    halo_1 = exchange(*packed[2:4], "gz")
    back = ((rows_of(0, False), NY), VM)
    far = pltpu.VMEM((8, WX, NY), f32)
    firsts = [(block, VM), (block, VM), (wide, VM), back, back]
    cost = {"flops": 1 << 24, "moved": 1 << 23}
    *b_0, to_a, to_b, m = call(
        first_half_0,
        [VM] * 6,
        firsts + [((2, EZ, WX, NY), VM)],
        [pltpu.VMEM((EZ, WX, NY), f32)] + [space] * 5 + [far],
        **cost,
    )(r, k, *near, *halo_0)
    halo_0 = exchange(to_a, to_b, "gz")
    *b_1, to_a, to_b = call(
        first_half_1, [VM] * 6, firsts, [space] * 5 + [far], **cost
    )(r, m, *near, *halo_1)
    halo_1 = exchange(to_a, to_b, "gz")
    table = ((64, NY), VM)
    part_0, part_1 = call(low_gram, [VM] * 7, [table] * 2, **cost)(r, *b_0, *b_1)
    seconds = [(block, HBM)] * 3
    spaces = [space] * 7 + [dma((3,))]
    *high_0, total = call(
        second_half_0, [VM] * 8, seconds + [table], spaces, **cost
    )(r, *b_0, m, *halo_0, part_0)
    *high_1, send = call(
        second_half_1,
        [VM] * 10,
        seconds + [((128, 2 * NY), VM)],
        [pltpu.VMEM((64, NY), f32)] + spaces,
        **cost,
    )(r, *b_1, m, *halo_1, part_1, total, cells)
    held = (send, conductance, r_far, *b_0[:2], *high_0, *b_1[:2], *high_1)
    send, *fars = lax.optimization_barrier(held)
    got = lax.all_to_all(send, ("gz", "gx"), 0, 0, tiled=True)
    x, send = call(
        finish,
        [VM] * 13,
        [(whole, HBM), ((128, NY), VM)],
        [
            pltpu.VMEM(whole, f32),
            pltpu.VMEM((4 * CX, NY), f32),
            pltpu.VMEM((4 * CX, NY), f32),
            dma((6,)),
        ],
    )(got, *fars)
    got = lax.all_to_all(send, ("gz", "gx"), 0, 0, tiled=True)
    (hazard,) = call(hazard_rows, [VM] * 2, [((128, scen), VM)])(got, power)
    return x.reshape(right_side.shape), hazard


def solution(mesh):
    return jax.shard_map(
        per_device,
        mesh=mesh,
        in_specs=(
            P(None, None, None, "gz", "gx", None),
            P("gz", "gx", None),
            P(("gz", "gx"), None, None),
            P(),
            P(),
        ),
        out_specs=(P(None, None, None, "gz", "gx", None), P(("gz", "gx"), None)),
        check_vma=False,
    )
```

```python
import jax
import jax.numpy as jnp
from jax import lax
from jax.experimental import pallas as pl
from jax.experimental.pallas import tpu as pltpu
from jax.sharding import PartitionSpec as P

SHIFTS = (0.3, 1.9, 0.3, 1.9, 0.3, 1.9)
SCALE = 1.0
ITERS = 3
REACH = 3
SIDE = 2 * REACH
NF = 6
CX, NZL, NY = 32, 4, 128
WX = 48
EZ = NZL + 2 * REACH
f32 = jnp.float32
VM = pl.BlockSpec(memory_space=pltpu.VMEM)
LIMIT = 14 * 1024 * 1024
FIRST_LIMIT = 14 * 1024 * 1024


HBM = pl.BlockSpec(memory_space=pltpu.HBM)


def call(body, ins, outs, scratch=(), flops=0, moved=0, limit=LIMIT):
    return pl.pallas_call(
        body,
        out_shape=[jax.ShapeDtypeStruct(shape, f32) for shape, _ in outs],
        in_specs=ins,
        out_specs=[spec for _, spec in outs],
        scratch_shapes=list(scratch),
        compiler_params=pltpu.CompilerParams(vmem_limit_bytes=limit),
        cost_estimate=pl.CostEstimate(flops=flops, bytes_accessed=moved, transcendentals=0),
    )


def odd(axis):
    return lax.rem(lax.axis_index(axis), 2) == 1


def either(flag, body, first, second):
    @pl.when(jnp.logical_not(flag))
    def _():
        body(first, second)

    @pl.when(flag)
    def _():
        body(second, first)


def start_all(pairs, sem, first=0):
    copies = [pltpu.make_async_copy(src, dst, sem.at[first + i]) for i, (src, dst) in enumerate(pairs)]
    for copy in copies:
        copy.start()
    return copies


def wait_all(copies):
    for copy in copies:
        copy.wait()


def pack_x(r, k, spectra, scenario, to_a, to_b, power, rim, rim_k, spec, scen, sem):
    pairs = []
    for i in range(2):
        src = pl.ds(i * (CX - 8), 8)
        pairs.append((r.at[:, :, src, :], rim.at[:, :, pl.ds(8 * i, 8), :]))
        pairs.append((k.at[:, src, :], rim_k.at[:, pl.ds(8 * i, 8), :]))
    pairs += [(spectra, spec), (scenario, scen)]
    wait_all(start_all(pairs, sem))

    def fill(up, down):
        for f in range(2 * NF + 1):
            for z in range(NZL):
                row = (f * NZL + z) * SIDE
                src = rim_k.at[z] if f == 2 * NF else rim.at[f, z]
                up[row : row + SIDE, :] = src[16 - SIDE : 16, :]
                down[row : row + SIDE, :] = src[0:SIDE, :]

    either(odd("gx"), fill, to_a, to_b)
    xr, xi, yr, yi = [spec[i : i + 1, :] for i in range(4)]
    base = [
        xr * xr + xi * xi,
        yr * yr + yi * yi,
        2.0 * (xr * yr + xi * yi),
        2.0 * (xi * yr - xr * yi),
    ]
    for j in range(4):
        weight = jnp.where(scen[...] == j, 1.0, 0.25)
        for v in range(4):
            power[4 * j + v : 4 * j + v + 1, :] = weight * base[v]


def sides(from_a, from_b, near):
    a, b = from_a[near : near + SIDE, :], from_b[near : near + SIDE, :]
    flag = odd("gx")
    return jnp.where(flag, a, b), jnp.where(flag, b, a)


def spans(margin):
    low, high = margin + REACH, CX - 1 + margin
    below = ((1 - low, high + 3), (2 - low, high + 3), (3 - low, high + 2))
    above = ((-low, high + 2), (-low, high + 1), (-low, high))
    return below, above


def layout(span, with_k):
    near, row = {}, 0
    for i in range(REACH - 1):
        for f in range(NF):
            near[i, f] = row
            row += span[i][1] - span[i][0] + 1
    far = []
    for _ in range(4):
        far.append(row)
        row += span[-1][1] - span[-1][0] + 1
    k = []
    for i in range(REACH - 1 if with_k else 0):
        k.append(row)
        row += span[i][1] - span[i][0] + 1
    return near, far, k, row


def rows_of(margin, with_k):
    return max(layout(span, with_k)[3] for span in spans(margin))


def cut(span):
    return slice(8 + span[0], 9 + span[1]), span[1] - span[0] + 1


def far_fields(b, first, weight, far):
    _, last = lanes()

    def y(z, c):
        mr, mi = weight(z)
        re, im = b[2 * c, first + z], b[2 * c + 1, first + z]
        return mr * re - mi * im, mr * im + mi * re

    ex, ey, ez = [y(NZL - REACH, c) for c in range(3)]
    for q in range(2):
        far[q] = ex[q] + (next_x(ez[q]) - ez[q])
        far[2 + q] = ey[q] + (next_y(ez[q], last) - ez[q])
    for c in range(2):
        far[4 + 2 * c], far[5 + 2 * c] = y(REACH - 1, c)


def fill_messages(b, first, far, k, margin, up, down):
    for side, (out, span) in enumerate(zip((up, down), spans(margin))):
        near, far_rows, k_rows, _ = layout(span, k is not None)
        for i in range(REACH - 1):
            z = first + (NZL - 1 - i if side == 0 else i)
            cols, n = cut(span[i])
            for f in range(NF):
                out[near[i, f] : near[i, f] + n, :] = b[f, z, cols, :]
            if k is not None:
                out[k_rows[i] : k_rows[i] + n, :] = k[z, cols, :]
        cols, n = cut(span[-1])
        for j, row in enumerate(far_rows):
            out[row : row + n, :] = far[4 * side + j, cols, :]


def take_messages(b, y, k, margin, above, below):
    for side, (src, span) in enumerate(zip((below, above), spans(margin))):
        near, far_rows, k_rows, _ = layout(span, k is not None)
        for i in range(REACH - 1):
            z = REACH - 1 - i if side == 0 else REACH + NZL + i
            cols, n = cut(span[i])
            for f in range(NF):
                b[f, z, cols, :] = src[near[i, f] : near[i, f] + n, :]
            if k is not None:
                k[z, cols, :] = src[k_rows[i] : k_rows[i] + n, :]
        cols, n = cut(span[-1])
        z = 0 if side == 0 else EZ - 1
        for j, row in enumerate(far_rows):
            y[j, z, cols, :] = src[row : row + n, :]


def clear_sides(ref):
    zero = jnp.zeros((EZ, 8, NY), f32)
    ref[:, 0:8, :] = zero
    ref[:, WX - 8 : WX, :] = zero


def clear_far(y):
    for f in range(NF):
        for z in (0, EZ - 1):
            if f < 4:
                y[f, z, 0:8, :] = jnp.zeros((8, NY), f32)
                y[f, z, WX - 8 : WX, :] = jnp.zeros((8, NY), f32)
            else:
                y[f, z] = jnp.zeros((WX, NY), f32)


def own_layers(dst, first, src, xa, xb, near):
    for z in range(NZL):
        left, right = sides(xa, xb, (near * NZL + z) * SIDE)
        dst[first + z, 8 - SIDE : 8, :] = left
        dst[first + z, 8 : 8 + CX, :] = src[z]
        dst[first + z, 8 + CX : 8 + CX + SIDE, :] = right


def weight_of(kz):
    inv = jnp.where(kz > 0.0, 1.0, 0.0) / (16.0 + kz * kz)
    return 4.0 * inv, -kz * inv


def pack_z(r, k, xa, xb, owned, a_0, b_0, a_1, b_1, cells, b, kx, far):
    for f in range(2 * NF + 1):
        dst = kx if f == 2 * NF else b.at[f]
        zero = jnp.zeros((NZL, 8, NY), f32)
        dst[:, 0:8, :] = zero
        dst[:, WX - 8 : WX, :] = zero
        own_layers(dst, 0, k if f == 2 * NF else r.at[f], xa, xb, f)
    weights = {z: weight_of(kx[z]) for z in (NZL - REACH, REACH - 1)}
    for p in range(2):
        far_fields(b.at[pl.ds(p * NF, NF)], 0, lambda z: weights[z], far.at[p])

    def fill(first, second):
        for p in range(2):
            own = b.at[pl.ds(p * NF, NF)]
            fill_messages(own, 0, far.at[p], kx if p == 0 else None, REACH, first[p], second[p])

    either(odd("gz"), fill, (a_0, a_1), (b_0, b_1))
    cells[...] = jnp.concatenate([owned[j : j + 1, :] for j in range(4)], axis=1).astype(f32)


def lanes():
    lane = lax.broadcasted_iota(jnp.int32, (WX, NY), 1)
    return lane == 0, lane == NY - 1


def next_y(a, last):
    return jnp.where(last, 0.0, pltpu.roll(a, NY - 1, 1))


def next_x(a):
    return pltpu.roll(a, WX - 1, 0)


def prev_x(a):
    return pltpu.roll(a, 1, 0)


def smooth(b, y, m, base, z):
    mr, mi = m[0, z], m[1, z]
    for c in range(3):
        re, im = b[base + 2 * c, z], b[base + 2 * c + 1, z]
        y[base + 2 * c, z] = mr * re - mi * im
        y[base + 2 * c + 1, z] = mr * im + mi * re


def apply_k(b, y, bn, yn, hs, m, lo, hi, shift, want_y):
    first, last = lanes()
    own = (1.0 - shift) / SCALE
    inv = 1.0 / SCALE
    for z in range(lo - 1, hi):
        for e in range(2):
            ex, ey, ez = y[e, z], y[e + 2, z], y[e + 4, z]
            hs[e, z] = next_y(ez, last) - ez - (y[e + 2, z + 1] - ey)
            hs[e + 2, z] = y[e, z + 1] - ex - (next_x(ez) - ez)
            hs[e + 4, z] = next_x(ey) - ey - (next_y(ex, last) - ex)
    for z in range(lo, hi):
        for e in range(2):
            hx, hy, hz = hs[e, z], hs[e + 2, z], hs[e + 4, z]
            ex, ey, ez = y[e, z], y[e + 2, z], y[e + 4, z]
            cx = hz - jnp.where(first, -ex, pltpu.roll(hz, 1, 1)) - (hy - hs[e + 2, z - 1])
            cy = hx - hs[e, z - 1] - (hz - prev_x(hz))
            cz = hy - prev_x(hy) - (hx - jnp.where(first, ez, pltpu.roll(hx, 1, 1)))
            for c, (cur, old) in enumerate(((cx, ex), (cy, ey), (cz, ez))):
                new = cur - 4.0 * old
                if inv != 1.0:
                    new = new * inv
                bn[e + 2 * c, z] = new + own * b[e + 2 * c, z]
        if want_y:
            smooth(bn, yn, m, 0, z)


def all_smooth(b, y, m):
    def layer(z, _):
        smooth(b, y, m, 0, z)
        return 0

    lax.fori_loop(1, EZ - 1, layer, 0)


def keep(src, out):
    def field(f, _):
        out[f] = src[f, REACH : REACH + NZL, 8 : 8 + CX, :]
        return 0

    lax.fori_loop(0, NF, field, 0)


def first_steps(p, r, k, kx, xa, xb, za, zb, b1, b2, b3w, to_a, to_b, m, ba, bb, ya, yb, hs, far):
    for f in range(NF):
        clear_sides(ba.at[f])
        own_layers(ba.at[f], REACH, r.at[p * NF + f], xa, xb, p * NF + f)
    clear_far(ya)
    if p == 0:
        clear_sides(kx)
        own_layers(kx, REACH, k, xa, xb, 2 * NF)

    def take(above, below):
        take_messages(ba, ya, kx if p == 0 else None, REACH, above, below)

    either(odd("gz"), take, za, zb)
    if p == 0:

        def layer(z, _):
            m[0, z], m[1, z] = weight_of(kx[z])
            return 0

        lax.fori_loop(1, EZ - 1, layer, 0)
    all_smooth(ba, ya, m)
    apply_k(ba, ya, bb, yb, hs, m, 1, EZ - 1, SHIFTS[0], True)
    keep(bb, b1)
    apply_k(bb, yb, ba, ya, hs, m, 2, EZ - 2, SHIFTS[1], True)
    keep(ba, b2)
    apply_k(ba, ya, bb, yb, hs, m, 3, EZ - 3, SHIFTS[2], False)
    for f in range(NF):
        b3w[f] = bb[f, REACH : REACH + NZL]
    far_fields(bb, REACH, lambda z: (m[0, REACH + z], m[1, REACH + z]), far)
    either(odd("gz"), lambda up, down: fill_messages(bb, REACH, far, None, 0, up, down), to_a, to_b)


def first_half_0(r, k, xa, xb, za, zb, b1, b2, b3w, to_a, to_b, m, kx, *space):
    first_steps(0, r, k, kx, xa, xb, za, zb, b1, b2, b3w, to_a, to_b, m, *space)


def first_half_1(r, m, xa, xb, za, zb, b1, b2, b3w, to_a, to_b, *space):
    first_steps(1, r, None, None, xa, xb, za, zb, b1, b2, b3w, to_a, to_b, m, *space)


PAIRS = [(i, j) for i in range(7) for j in range(i, 7)]
LOW = [pair for pair in PAIRS if pair[1] <= REACH]
HIGH = [pair for pair in PAIRS if pair[1] > REACH]
SLOT = {}
for _pair in LOW + HIGH:
    SLOT[_pair] = sum(1 if a == b else 2 for a, b in SLOT)


def gram(read, pairs, out, unroll=False):
    used = sorted({i for pair in pairs for i in pair})
    count = sum(1 if i == j else 2 for i, j in pairs)

    def block(step, acc):
        c, z = step // NZL, step % NZL
        acc = list(acc)
        for xb in range(CX // 8):
            vec = {i: (read(i, 2 * c, z, xb), read(i, 2 * c + 1, z, xb)) for i in used}
            at = 0
            for i, j in pairs:
                (ar, ai), (br, bi) = vec[i], vec[j]
                acc[at] = acc[at] + (ar * br + ai * bi)
                at += 1
                if i != j:
                    acc[at] = acc[at] + (ar * bi - ai * br)
                    at += 1
        return tuple(acc)

    acc = lax.fori_loop(0, 3 * NZL, block, (jnp.zeros((8, NY), f32),) * count, unroll=unroll)
    at = 0
    for i, j in pairs:
        for part in range(1 if i == j else 2):
            row = SLOT[i, j] + part
            out[row : row + 1, :] = jnp.sum(acc[at], axis=0, keepdims=True)
            at += 1


def low_gram(b0, b1_0, b2_0, b3w_0, b1_1, b2_1, b3w_1, part_0, part_1):
    for p, (b1, b2, b3w, part) in enumerate(((b1_0, b2_0, b3w_0, part_0), (b1_1, b2_1, b3w_1, part_1))):
        part[...] = jnp.zeros((64, NY), f32)
        gram(reader(p, b0, b1, b2, b3w), LOW, part)


def reader(p, b0, b1, b2, b3w, *slabs):
    def read(i, f, z, xb):
        if i == 0:
            return b0[p * NF + f, z, pl.ds(8 * xb, 8), :]
        if i < 3:
            return (b1, b2)[i - 1][f, z, pl.ds(8 * xb, 8), :]
        if i == 3:
            return b3w[f, z, pl.ds(8 + 8 * xb, 8), :]
        return slabs[i - 4][f, REACH + z, pl.ds(8 + 8 * xb, 8), :]

    return read


def second_steps(p, b0, b1, b2, b3w, m, za, zb, part, b3_far, b4_far, b5_far, total, ba, bb, bc, bd, ya, yb, hs, sem):
    own = pl.ds(REACH, NZL)
    mid = pl.ds(8, CX)
    copies = start_all([(b3w.at[:, :, mid, :], b3_far)], sem)
    for f in range(NF):
        clear_sides(ba.at[f])
        ba[f, REACH : REACH + NZL] = b3w[f]
    clear_far(ya)
    either(odd("gz"), lambda above, below: take_messages(ba, ya, None, 0, above, below), za, zb)
    all_smooth(ba, ya, m)
    apply_k(ba, ya, bb, yb, hs, m, 1, EZ - 1, SHIFTS[3], True)
    copies += start_all([(bb.at[:, own, mid, :], b4_far)], sem, 1)
    apply_k(bb, yb, bc, ya, hs, m, 2, EZ - 2, SHIFTS[4], True)
    copies += start_all([(bc.at[:, own, mid, :], b5_far)], sem, 2)
    total[...] = part[...]
    read = reader(p, b0, b1, b2, b3w, bb, bc, bd)
    apply_k(bc, ya, bd, yb, hs, m, 3, EZ - 3, SHIFTS[5], False)
    gram(read, [pair for pair in HIGH if pair[1] < 6], total, True)
    gram(read, [pair for pair in HIGH if pair[1] == 6], total, True)
    wait_all(copies)


def second_half_0(b0, b1, b2, b3w, m, za, zb, part, b3_far, b4_far, b5_far, total, *space):
    second_steps(0, b0, b1, b2, b3w, m, za, zb, part, b3_far, b4_far, b5_far, total, *space)


def second_half_1(b0, b1, b2, b3w, m, za, zb, part, other, cells, b3_far, b4_far, b5_far, send, total, *space):
    second_steps(1, b0, b1, b2, b3w, m, za, zb, part, b3_far, b4_far, b5_far, total, *space)
    both = jnp.concatenate([other[...], total[...]], axis=0)
    sums = jnp.sum(jnp.transpose(both), axis=0, keepdims=True)
    send[...] = jnp.broadcast_to(jnp.concatenate([sums, cells[...]], axis=1), (128, 2 * NY))


def cadd(a, b):
    return (a[0] + b[0], a[1] + b[1])


def csub(a, b):
    return (a[0] - b[0], a[1] - b[1])


def cmul(a, b):
    return (a[0] * b[0] - a[1] * b[1], a[0] * b[1] + a[1] * b[0])


def cconj_mul(a, b):
    return (a[0] * b[0] + a[1] * b[1], a[0] * b[1] - a[1] * b[0])


def cdiv(numer, denom, floor):
    size = jnp.maximum(denom[0] * denom[0] + denom[1] * denom[1], floor)
    return (
        (numer[0] * denom[0] + numer[1] * denom[1]) / size,
        (numer[1] * denom[0] - numer[0] * denom[1]) / size,
    )


def tree(terms):
    terms = list(terms)
    while len(terms) > 1:
        terms = [cadd(*terms[i : i + 2]) if i + 1 < len(terms) else terms[i] for i in range(0, len(terms), 2)]
    return terms[0]


def combine(a, scale, b):
    out = []
    for i in range(max(len(a), len(b))):
        if i >= len(b):
            out.append(a[i])
        elif i >= len(a):
            out.append(cmul(scale, b[i]))
        else:
            out.append(cadd(a[i], cmul(scale, b[i])))
    return out


def times_k(a):
    zero = (jnp.zeros_like(a[0][0]),) * 2
    out = [(SHIFTS[i] * v[0], SHIFTS[i] * v[1]) for i, v in enumerate(a)] + [zero]
    return [
        cadd(out[i], (SCALE * a[i - 1][0], SCALE * a[i - 1][1])) if i > 0 else out[i]
        for i in range(len(out))
    ]


def coefficients(entry):
    def g(i, j):
        if i > j:
            re, im = g(j, i)
            return (re, -im)
        if i == j:
            return (entry(SLOT[i, j]), 0.0)
        return (entry(SLOT[i, j]), entry(SLOT[i, j] + 1))

    def times_g(b, rows):
        return [tree([cmul(g(i, j), b[j]) for j in range(len(b))]) for i in range(rows)]

    def dot(a, gb):
        return tree([cconj_mul(a[i], gb[i]) for i in range(len(a))])

    def shadow(b):
        return tree([cmul(g(0, j), b[j]) for j in range(len(b))])

    one = jnp.ones_like(entry(0))
    residual = [(one, jnp.zeros_like(one))]
    direction = residual
    solution = []
    for step in range(ITERS):
        rho = shadow(residual)
        if step == 0:
            floor = 1e-06 * rho[0] * rho[0]
        else:
            beta = cmul(cdiv(rho, rho_prev, floor), cdiv(alpha, omega, 0.0001))
            minus = (-omega[0], -omega[1])
            direction = combine(residual, beta, combine(direction, minus, image))
        image = times_k(direction)
        alpha = cdiv(rho, shadow(image), floor)
        middle = combine(residual, (-alpha[0], -alpha[1]), image)
        bent = times_k(middle)
        seen = times_g(bent, len(bent))
        norm = dot(bent, seen)[0] + 1e-06
        against = dot(middle, seen)
        omega = (against[0] / norm, -against[1] / norm)
        solution = combine(combine(solution, alpha, direction), omega, middle)
        residual = combine(middle, (-omega[0], -omega[1]), bent)
        rho_prev = rho
    return solution


def surface_power(x, rows):
    def e(p, c, z):
        f = p * NF + 2 * c
        return (x[f, z, rows, :], x[f + 1, z, rows, :])

    ex, ey, hx, hy = [], [], [], []
    for p in range(2):
        ex0, ey0 = e(p, 0, 0), e(p, 1, 0)
        ex1, ey1 = e(p, 0, 1), e(p, 1, 1)
        ex.append(ex0)
        ey.append(ey0)
        one_x, one_y = (1.0, 0.0) if p == 0 else (0.0, 1.0)
        hx.append((one_x - 2.0 * (ey1[0] - ey0[0]), -2.0 * (ey1[1] - ey0[1])))
        hy.append((one_y + 2.0 * (ex1[0] - ex0[0]), 2.0 * (ex1[1] - ex0[1])))
    det = csub(cmul(hx[0], hy[1]), cmul(hx[1], hy[0]))
    zxx = csub(cmul(ex[0], hy[1]), cmul(ex[1], hy[0]))
    zxy = csub(cmul(ex[1], hx[0]), cmul(ex[0], hx[1]))
    zyx = csub(cmul(ey[0], hy[1]), cmul(ey[1], hy[0]))
    zyy = csub(cmul(ey[1], hx[0]), cmul(ey[0], hx[1]))
    size = det[0] * det[0] + det[1] * det[1]
    inv = 1.0 / jnp.maximum(size, 0.25)
    scale = size * inv * inv
    cross = cadd(cconj_mul(zxx, zxy), cconj_mul(zyx, zyy))
    first = zxx[0] * zxx[0] + zxx[1] * zxx[1] + (zyx[0] * zyx[0] + zyx[1] * zyx[1])
    second = zxy[0] * zxy[0] + zxy[1] * zxy[1] + (zyy[0] * zyy[0] + zyy[1] * zyy[1])
    return [scale * first, scale * second, scale * cross[0], scale * cross[1]]


def finish(got, k, *rest):
    fars, (x_far, send, x, surface, picked, sem) = rest[:11], rest[11:]
    sub = lax.broadcasted_iota(jnp.int32, (8, NY), 0)
    row = jnp.broadcast_to(jnp.sum(got[:, 0:NY], axis=0, keepdims=True), (8, NY))
    table = jnp.where(sub == 0, row, pltpu.roll(row, 64, 1))
    cache = {}

    def entry(slot):
        if slot not in cache:
            cache[slot] = jnp.broadcast_to(table[:, slot : slot + 1], (8, NY))
        return cache[slot]

    coefs = coefficients(entry)
    scal = [[tuple(jnp.broadcast_to(half[p : p + 1, :], (8, NY)) for half in c) for c in coefs] for p in range(2)]

    mine = pltpu.roll(got[:, NY : 2 * NY], lax.rem(NY - 32 * lax.axis_index("gx"), NY), 1).astype(jnp.int32)
    group = lax.broadcasted_iota(jnp.int32, (32, NY), 1) // 32
    cells = mine[0:32, :]
    for e in range(1, 4):
        cells = jnp.where(group == e, pltpu.roll(mine[32 * e : 32 * e + 32, :], 32 * e, 1), cells)
    col = cells % NY
    line = cells // NY
    cols = [col[8 * i : 8 * i + 8, :] for i in range(4)]
    lines = [line[8 * i : 8 * i + 8, :] for i in range(4)]

    def layer(p, z):
        for xb in range(CX // 8):
            rows = pl.ds(8 * xb, 8)
            kz = k[z, rows, :]
            inv = 1.0 / (16.0 + kz * kz)
            weight = (4.0 * inv, -kz * inv)
            for f in range(p * NF, p * NF + NF, 2):
                terms = [cmul(scal[p][i], (basis(i, f, z, rows), basis(i, f + 1, z, rows))) for i in range(6)]
                y = cmul(weight, tree(terms))
                x[f, z, rows, :] = y[0]
                x[f + 1, z, rows, :] = y[1]

    def basis(i, f, z, rows):
        if i == 0:
            return fars[0][f, z, rows, :]
        return fars[5 * (f // NF) + i][f % NF, z, rows, :]

    outs = []

    def leave(p, z, count):
        part = pl.ds(p * NF, NF), pl.ds(z, count)
        outs.extend(start_all([(x.at[part], x_far.at[part])], sem, len(outs)))

    for p in range(2):
        for z in range(2):
            layer(p, z)
        leave(p, 0, 2)
    for xb in range(CX // 8):
        for v, value in enumerate(surface_power(x, pl.ds(8 * xb, 8))):
            surface[v * CX + 8 * xb : v * CX + 8 * xb + 8, :] = value
    for i in range(4):
        acc = [jnp.zeros((8, NY), f32)] * 4
        for r in range(CX):
            for v in range(4):
                src = jnp.broadcast_to(surface[v * CX + r : v * CX + r + 1, :], (8, NY))
                hit = jnp.take_along_axis(src, cols[i], axis=1, mode="promise_in_bounds")
                acc[v] = jnp.where(lines[i] == r, hit, acc[v])
        for v in range(4):
            picked[v * 32 + 8 * i : v * 32 + 8 * i + 8, :] = acc[v]
        p, z = i // 2, 2 + i % 2
        layer(p, z)
        leave(p, z, 1)
    for e in range(4):
        out = None
        for v in range(4):
            part = picked[v * 32 : v * 32 + 32, :]
            if v != e:
                part = pltpu.roll(part, (32 * (v - e)) % NY, 1)
            out = part if out is None else jnp.where(group == v, part, out)
        send[32 * e : 32 * e + 32, :] = out
    wait_all(outs)


def hazard_rows(got, power, out):
    block = jnp.concatenate([got[0:8, :], jnp.zeros((NY - 8, NY), f32)], axis=0)
    turned = jnp.transpose(block)
    for j in range(4):
        for qb in range(4):
            total = None
            for v in range(4):
                first = v * 32 + 8 * qb
                column = jnp.broadcast_to(turned[first : first + 8, j : j + 1], (8, power.shape[1]))
                term = column * power[4 * j + v : 4 * j + v + 1, :]
                total = term if total is None else total + term
            row = 32 * j + 8 * qb
            out[row : row + 8, :] = total


def partners(count):
    first = [(i, i ^ 1) for i in range(count)]
    second = [(i, ((i + 1) ^ 1) - 1) for i in range(1, count - 1)]
    return first, second


def exchange(to_a, to_b, axis):
    first, second = partners(lax.axis_size(axis))
    return lax.ppermute(to_a, axis, first), lax.ppermute(to_b, axis, second)


def per_device(right_side, conductance, owned_cells, spectra, scenario_tile):
    block = (NF, NZL, CX, NY)
    wide = (NF, NZL, WX, NY)
    whole = (2 * NF, NZL, CX, NY)
    dma = pltpu.SemaphoreType.DMA
    space = pltpu.VMEM((NF, EZ, WX, NY), f32)
    r_far = right_side.reshape(whole)
    side = (((2 * NF + 1) * NZL * SIDE, NY), VM)
    scen = spectra.shape[0]
    rims = [
        pltpu.VMEM((2 * NF, NZL, 16, NY), f32),
        pltpu.VMEM((NZL, 16, NY), f32),
        pltpu.VMEM((4, scen), f32),
        pltpu.VMEM((1, scen), jnp.int32),
        dma((6,)),
    ]
    to_a, to_b, power = call(
        pack_x, [HBM] * 4, [side] * 2 + [((16, scen), VM)], rims, limit=FIRST_LIMIT
    )(*[pltpu.with_memory_space_constraint(v, pltpu.HBM) for v in (r_far, conductance, spectra.T, scenario_tile.reshape(1, scen))])
    r, k = r_far, conductance
    near = exchange(to_a, to_b, "gx")
    deep = [((rows_of(REACH, with_k), NY), VM) for with_k in (True, False)]
    *packed, cells = call(
        pack_z,
        [VM] * 5,
        [deep[0]] * 2 + [deep[1]] * 2 + [((1, NY), VM)],
        [
            pltpu.VMEM((2 * NF, NZL, WX, NY), f32),
            pltpu.VMEM((NZL, WX, NY), f32),
            pltpu.VMEM((2, 8, WX, NY), f32),
        ],
        moved=1 << 22,
    )(r, k, *near, owned_cells[0])
    halo_0 = exchange(*packed[0:2], "gz")
    halo_1 = exchange(*packed[2:4], "gz")
    back = ((rows_of(0, False), NY), VM)
    far = pltpu.VMEM((8, WX, NY), f32)
    firsts = [(block, VM), (block, VM), (wide, VM), back, back]
    cost = {"flops": 1 << 24, "moved": 1 << 23}
    *b_0, to_a, to_b, m = call(
        first_half_0,
        [VM] * 6,
        firsts + [((2, EZ, WX, NY), VM)],
        [pltpu.VMEM((EZ, WX, NY), f32)] + [space] * 5 + [far],
        **cost,
    )(r, k, *near, *halo_0)
    halo_0 = exchange(to_a, to_b, "gz")
    *b_1, to_a, to_b = call(
        first_half_1, [VM] * 6, firsts, [space] * 5 + [far], **cost
    )(r, m, *near, *halo_1)
    halo_1 = exchange(to_a, to_b, "gz")
    table = ((64, NY), VM)
    part_0, part_1 = call(low_gram, [VM] * 7, [table] * 2, **cost)(r, *b_0, *b_1)
    seconds = [(block, HBM)] * 3
    spaces = [space] * 7 + [dma((3,))]
    *high_0, total = call(
        second_half_0, [VM] * 8, seconds + [table], spaces, **cost
    )(r, *b_0, m, *halo_0, part_0)
    *high_1, send = call(
        second_half_1,
        [VM] * 10,
        seconds + [((128, 2 * NY), VM)],
        [pltpu.VMEM((64, NY), f32)] + spaces,
        **cost,
    )(r, *b_1, m, *halo_1, part_1, total, cells)
    held = (send, conductance, r_far, *b_0[:2], *high_0, *b_1[:2], *high_1)
    send, *fars = lax.optimization_barrier(held)
    got = lax.all_to_all(send, ("gz", "gx"), 0, 0, tiled=True)
    x, send = call(
        finish,
        [VM] * 13,
        [(whole, HBM), ((128, NY), VM)],
        [
            pltpu.VMEM(whole, f32),
            pltpu.VMEM((4 * CX, NY), f32),
            pltpu.VMEM((4 * CX, NY), f32),
            dma((6,)),
        ],
    )(got, *fars)
    got = lax.all_to_all(send, ("gz", "gx"), 0, 0, tiled=True)
    (hazard,) = call(hazard_rows, [VM] * 2, [((128, scen), VM)])(got, power)
    return x.reshape(right_side.shape), hazard


def solution(mesh):
    return jax.shard_map(
        per_device,
        mesh=mesh,
        in_specs=(
            P(None, None, None, "gz", "gx", None),
            P("gz", "gx", None),
            P(("gz", "gx"), None, None),
            P(),
            P(),
        ),
        out_specs=(P(None, None, None, "gz", "gx", None), P(("gz", "gx"), None)),
        check_vma=False,
    )
```
